32 devices in a mesh: cfg: 2 (over x), work: 16 (over z, y, core).
Axes of the slice: x: 2, y: 2, z: 4, core: 2. Of those that a mesh axis runs over, the one named last changes fastest.
Arguments:
- sources: bfloat16 [32, 16384, 128], P('cfg', 'work'), parts along dimension 0, may hold values from -6 to 6
- perambs: bfloat16 [192, 16384], P('cfg', 'work'), parts along dimension 0, may hold values from -0.5 to 0.5
- source_ids: int32 [16], replicated, may hold values from 0 to 15
- peramb_ids: int32 [48, 3], replicated, may hold values from 0 to 95
- sink_counts: int32 [16], replicated, may hold values from 1 to 6, 48 in all
- weights: float32 [48], replicated, may hold values from -2 to 2, as said below
Outputs:
- sink_tensors: bfloat16 [32, 16384, 128], P(('cfg', 'work')), parts along dimension 0
The draws below stay inside these ranges and needn't reach their ends.
There are 2 independent parts, one for each index of `cfg`. The reference program is written for one: setup_inputs(seed, part) draws one part's arguments, and reference() takes and returns one part's arrays. A program takes and returns all parts, laid end to end along the dimension named above; an argument that names none is the same for every part. Nothing has to cross between parts.
Inputs may be any that keep to these rules, and one draw needn't show every extreme that they name: `sink_counts`: diagrams are listed sink by sink in order; the counts add up to 48 and some sink has exactly 6 diagrams. `weights`: nonzero multiples of 1/4.
All inputs are finite; a program needn't handle non-finite values.
Results may differ from the reference program's by a relative error of at most 0.0064.
Values may be sent and summed in bfloat16 or wider, within the bound.
No kernel may reach another device: no remote copies, remote signals or barrier semaphores. Data moves between devices by JAX's collectives and lax.ppermute only.
A program may use at most 128 MiB of HBM per device.

```python
import math
import jax
import jax.numpy as jnp
import numpy as np
from jax import lax

N = 128
MOST = 6
SRC = 16
PERAMB = 96
DIAG = 48
SINK = 16


def draw_weights(key, part):
    key_mag, key_sign = jax.random.split(key)
    magnitude = jax.random.randint(key_mag, (DIAG,), 1, 9).astype(jnp.float32)
    signs = 2.0 * jax.random.randint(key_sign, (DIAG,), 0, 2).astype(jnp.float32) - 1.0
    return magnitude * signs * 0.25


def set_ends(drawn, rng, smallest, top_value):
    shape = drawn.shape
    place = [jax.random.randint(jax.random.fold_in(rng, axis), (), 0, shape[axis]) for axis in range(len(shape))]
    drawn = drawn.at[tuple(place)].set(smallest)
    longest = shape.index(max(shape))
    place[longest] = (place[longest] + 1) % shape[longest]
    return drawn.at[tuple(place)].set(top_value)


def steps_of(stream_key, shape, pieces, low, high):
    def one(position, blocks):
        heights = jax.random.uniform(jax.random.fold_in(jax.random.fold_in(stream_key, 6), position), (blocks,), jnp.float32, low / len(pieces), high / len(pieces))
        return jnp.repeat(jnp.exp(heights), shape[position] // blocks).reshape((-1,) + (1,) * (len(shape) - position - 1))

    level = one(*pieces[0])
    for cut in pieces[1:]:
        level = level * one(*cut)
    return level


def cumulative_ranks(number_of, slope):
    weights = [(1 << 20) // math.isqrt(standing ** slope) + 1 for standing in range(1, number_of + 1)]
    spread = 1 + sum(weights) // (1 << 30)
    return np.cumsum(np.array([max(1, weight // spread) for weight in weights]))


def skewed_ids(own_key, shape, number_of, lean):
    table = cumulative_ranks(number_of, lean)
    lot = jax.random.randint(jax.random.fold_in(own_key, 1), shape, 0, int(table[number_of - 1]))
    standing = jnp.searchsorted(jnp.asarray(table, jnp.int32), lot, side="right")
    return jax.random.permutation(jax.random.fold_in(own_key, 2), number_of)[standing].astype(jnp.int32)


def split_up(count, total, limit, lean):
    weights = [(1 << 20) // math.isqrt(standing ** lean) + 1 for standing in range(2, count + 1)]
    surplus, holding = total - limit - (count - 1), [1] * (count - 1)
    while surplus > 0:
        free = [i for i in range(count - 1) if holding[i] < limit]
        mass, left = sum([weights[i] for i in free]), surplus
        for i in free:
            extra = min(limit - holding[i], max(1, left * weights[i] // mass), surplus)
            holding[i] = holding[i] + extra
            surplus = surplus - extra
    return np.array([limit] + holding)


def uneven(own_key, count, total, bound, lean):
    if count == 2:
        one = jax.random.randint(own_key, (), max(1, total - bound), min(bound, total - 1) + 1)
        return jnp.stack([one, total - one])
    lengths = jnp.asarray(split_up(count, total, bound, lean), jnp.int32)
    twos = (count - 1) // 2
    source_of, sink = lengths[1:1 + 2 * twos:2], lengths[2:2 + 2 * twos:2]
    margin = jnp.minimum(source_of - 1, bound - sink)
    moved = jax.random.randint(jax.random.fold_in(own_key, 1), (twos,), 0, 1 << 20) % (margin + 1)
    lengths = lengths.at[1:1 + 2 * twos:2].set(source_of - moved).at[2:2 + 2 * twos:2].set(sink + moved)
    return lengths[jax.random.permutation(jax.random.fold_in(own_key, 2), count)]


def normal_values(rng, dims, deviation, bound, cuts=(), kind=jnp.bfloat16):
    drawn = jax.random.normal(rng, dims, jnp.float32) * deviation
    if len(cuts) > 0:
        drawn = steps_of(rng, dims, cuts, -0.22, 0.18) * drawn
    return jnp.clip(drawn, min=-bound, max=bound).astype(kind)


def setup_inputs(seed: int = 0, part: int = 0) -> dict:
    keys = jax.random.split(jax.random.key(seed), 7)
    part_splits = jax.random.split(jax.random.fold_in(keys[6], part), 7)
    return {
        "sources": normal_values(part_splits[0], (SRC, N * N, N), 1.0, 6.0, ((1, 16),)),
        "perambs": normal_values(part_splits[1], (PERAMB, N * N), N ** -0.5, 0.5, ((1, 16),)),
        "source_ids": set_ends(skewed_ids(keys[2], (SINK,), SRC, 2), jax.random.fold_in(keys[2], 3), 0, SRC - 1).astype(jnp.int32),
        "peramb_ids": set_ends(jax.random.randint(keys[3], (DIAG, 3), 0, PERAMB), jax.random.fold_in(keys[3], 1), 0, PERAMB - 1).astype(jnp.int32),
        "sink_counts": uneven(keys[4], SINK, DIAG, MOST, 2).astype(jnp.int32),
        "weights": draw_weights(jax.random.fold_in(keys[6], 71), part),
    }


def contract(tensor_rows, leg_mats):
    extent = tensor_rows.shape[1]
    third = jnp.dot(tensor_rows, leg_mats[2].T, preferred_element_type=jnp.float32).astype(jnp.bfloat16)
    third = third.reshape(extent, extent, extent)
    second = jnp.einsum("bk,akc->abc", leg_mats[1].astype(jnp.float32), third.astype(jnp.float32)).astype(jnp.bfloat16)
    whole = jnp.dot(leg_mats[0], second.reshape(extent, extent * extent), preferred_element_type=jnp.float32)
    return whole.reshape(extent * extent, extent)


def reference(sources, perambs, source_ids, peramb_ids, sink_counts, weights):
    matrices = perambs.reshape(PERAMB, N, N)
    sink_ends = jnp.cumsum(sink_counts)
    sink_of = jnp.sum((sink_ends[None, :] <= jnp.arange(DIAG, dtype=jnp.int32)[:, None]).astype(jnp.int32), axis=1)

    def advance(totals, diagram):
        target = sink_of[diagram]
        tensor_rows = sources[source_ids[target]]
        leg_mats = matrices[peramb_ids[diagram]]
        weighted = (weights[diagram] * contract(tensor_rows, leg_mats)).astype(jnp.bfloat16)
        weighted = lax.optimization_barrier(weighted).astype(jnp.float32)
        current = lax.dynamic_index_in_dim(totals, target, 0, keepdims=False)
        totals = lax.dynamic_update_index_in_dim(totals, current + weighted, target, 0)
        return totals, None

    totals, unused = lax.scan(advance, jnp.zeros((SINK, N * N, N), jnp.float32), jnp.arange(DIAG, dtype=jnp.int32))
    return totals.astype(jnp.bfloat16)
```

```python
import functools

import jax
import jax.numpy as jnp
from jax import lax
from jax.experimental import pallas as pl
from jax.experimental.pallas import tpu as pltpu
from jax.sharding import PartitionSpec as P

MOST = 6
GROUPS = 4
B_BLOCK = 16


def group_kernel(first, last, pieces, extent, *refs):
    piece_refs = refs[:pieces]
    leg3_ref, leg2_ref, leg1_ref = refs[pieces : pieces + 3]
    refs = refs[pieces + 3 :]
    if not first:
        acc_ref, refs = refs[0], refs[1:]
    out_ref, turned_ref = refs[0], refs[1]
    a_per = piece_refs[0].shape[0] // extent
    depth = MOST * a_per * pieces
    step = pl.program_id(0)

    def inner_legs(piece, piece_ref):
        def pair(index, carry):
            rows = piece_ref[pl.ds(pl.multiple_of(index * 2 * extent, 2 * extent), 2 * extent), :]
            third = lax.dot_general(
                rows, leg3_ref[...], (((1,), (1,)), ((), ())), preferred_element_type=jnp.float32
            ).astype(jnp.bfloat16)
            for d in range(MOST):
                columns = third[:, d * extent : (d + 1) * extent]
                both = jnp.concatenate([columns[:extent], columns[extent:]], axis=1)
                second = jnp.dot(
                    leg2_ref[d * extent : (d + 1) * extent, :],
                    both,
                    preferred_element_type=jnp.float32,
                )
                for half in range(2):
                    row = (d * pieces + piece) * a_per + 2 * index + half
                    turned_ref[pl.ds(row, extent, stride=depth), :] = second[
                        :, half * extent : (half + 1) * extent
                    ]
            return carry

        lax.fori_loop(0, a_per // 2, pair, 0)

    for piece in range(pieces):
        pl.when(step == piece)(functools.partial(inner_legs, piece, piece_refs[piece]))

    @pl.when(step >= pieces)
    def outer_leg():
        block = step - pieces

        def pair(index, carry):
            b = block * B_BLOCK + 2 * index
            start = pl.multiple_of(b * depth, 2 * depth)
            both = jnp.concatenate(
                [
                    turned_ref[pl.ds(start, depth), :].astype(jnp.bfloat16),
                    turned_ref[pl.ds(pl.multiple_of(start + depth, depth), depth), :].astype(
                        jnp.bfloat16
                    ),
                ],
                axis=1,
            )
            whole = jnp.dot(leg1_ref[...], both, preferred_element_type=jnp.float32)
            for half in range(2):
                part = whole[:, half * extent : (half + 1) * extent]
                local = 2 * index + half
                if not first:
                    part = part + acc_ref[local]
                if last:
                    refs[2][pl.ds(local, extent, stride=B_BLOCK), :] = part
                else:
                    out_ref[local] = part
            return carry

        lax.fori_loop(0, B_BLOCK // 2, pair, 0)
        if last:
            out_ref[...] = (
                refs[2][...].reshape(extent, B_BLOCK, extent).astype(jnp.bfloat16)
            )


def add_group(pieces, leg3, leg2, leg1, acc, last):
    extent = leg3.shape[1]
    count = len(pieces)
    a_per = pieces[0].shape[0] // extent
    depth = MOST * a_per * count
    first = acc is None
    blocks = extent // B_BLOCK

    def whole_spec(x):
        return pl.BlockSpec(x.shape, lambda i: (0,) * x.ndim)

    def block_of(i):
        return jnp.maximum(i - count, 0)

    operands = [*pieces, leg3, leg2, leg1]
    in_specs = [whole_spec(x) for x in operands]
    if not first:
        operands.append(acc)
        in_specs.append(pl.BlockSpec((B_BLOCK, extent, extent), lambda i: (block_of(i), 0, 0)))
    scratch = [pltpu.VMEM((extent * depth, extent), jnp.float32)]
    if last:
        out_shape = jax.ShapeDtypeStruct((extent, extent, extent), jnp.bfloat16)
        out_spec = pl.BlockSpec((extent, B_BLOCK, extent), lambda i: (0, block_of(i), 0))
        scratch.append(pltpu.VMEM((extent * B_BLOCK, extent), jnp.float32))
    else:
        out_shape = jax.ShapeDtypeStruct((extent, extent, extent), jnp.float32)
        out_spec = pl.BlockSpec((B_BLOCK, extent, extent), lambda i: (block_of(i), 0, 0))
    rows = count * a_per * extent
    return pl.pallas_call(
        functools.partial(group_kernel, first, last, count, extent),
        grid=(count + blocks,),
        in_specs=in_specs,
        out_specs=out_spec,
        out_shape=out_shape,
        scratch_shapes=scratch,
        compiler_params=pltpu.CompilerParams(
            dimension_semantics=("arbitrary",), vmem_limit_bytes=40 * 1024 * 1024
        ),
        cost_estimate=pl.CostEstimate(
            flops=6 * MOST * rows * extent * extent,
            bytes_accessed=12 * extent**3,
            transcendentals=0,
        ),
    )(*operands)


def per_device(sources, perambs, source_ids, peramb_ids, sink_counts, weights):
    workers = lax.axis_size("work")
    extent = sources.shape[2]
    a_per = sources.shape[1] // extent
    diagrams = peramb_ids.shape[0]
    own = lax.axis_index("work")

    pieces = []
    senders = []
    for shift in range(workers):
        partner = own ^ shift
        senders.append(partner)
        piece = lax.dynamic_index_in_dim(sources, source_ids[partner], 0, keepdims=False)
        if shift:
            piece = lax.ppermute(piece, "work", [(i, i ^ shift) for i in range(workers)])
        pieces.append(piece)
    senders = jnp.stack(senders)

    own_count = sink_counts[own]
    start = jnp.sum(jnp.where(jnp.arange(workers) < own, sink_counts, 0))
    slots = jnp.arange(MOST, dtype=jnp.int32)
    chosen = jnp.minimum(start + slots, diagrams - 1)
    factors = jnp.where(slots < own_count, weights[chosen], 0.0)
    matrices = lax.all_gather(
        perambs.reshape(perambs.shape[0], a_per, extent), "work", axis=1, tiled=True
    )
    legs = jnp.take(matrices, peramb_ids[chosen], axis=0, mode="clip")
    leg3 = legs[:, 2].reshape(MOST * extent, extent)
    leg2 = legs[:, 1].reshape(MOST * extent, extent)
    leg1 = (factors[:, None, None] * legs[:, 0].astype(jnp.float32)).astype(jnp.bfloat16)
    leg1 = leg1.reshape(MOST, extent, workers, a_per)
    leg1 = jnp.take(leg1, senders, axis=2, mode="clip").transpose(1, 0, 2, 3)

    size = workers // GROUPS
    acc = None
    for group in range(GROUPS):
        part = slice(group * size, (group + 1) * size)
        acc = add_group(
            pieces[part],
            leg3,
            leg2,
            leg1[:, :, part].reshape(extent, MOST * size * a_per),
            acc,
            group == GROUPS - 1,
        )
    return acc.reshape(1, extent * extent, extent)


def solution(mesh):
    return jax.shard_map(
        per_device,
        mesh=mesh,
        in_specs=(P("cfg", "work", None), P("cfg", "work"), P(), P(), P(), P()),
        out_specs=P(("cfg", "work"), None, None),
        check_vma=False,
    )
```

```python
import functools

import jax
import jax.numpy as jnp
from jax import lax
from jax.experimental import pallas as pl
from jax.experimental.pallas import tpu as pltpu
from jax.sharding import PartitionSpec as P

MOST = 6
LEGS = 3
UNIT_ROWS = 16
B_BLOCK = 16
GROUPS = ((0, 4), (1, 5), (2, 6), (3, 7))
VMEM = 56 * 1024 * 1024


def choose_kernel(
    workers, ids_ref, counts_ref, matrix_ids_ref, source_ref, peramb_ref, *refs
):
    piece_refs, matrix_ref = refs[:workers], refs[workers]
    sems, choice_ref, spread_ref = refs[workers + 1 :]
    own = lax.axis_index("work")
    copies = []
    for shift in range(workers):
        copy = pltpu.make_async_copy(
            source_ref.at[ids_ref[own ^ shift]], piece_refs[shift], sems.at[shift]
        )
        copy.start()
        copies.append(copy)

    rows = MOST * LEGS
    diagrams = matrix_ids_ref.shape[0]
    total = peramb_ref.shape[0]
    lanes = lax.broadcasted_iota(jnp.int32, (1, total), 1)

    def mark(sink, start):
        for slot in range(MOST):
            diagram = jnp.minimum(start + slot, diagrams - 1)
            for leg in range(LEGS):
                choice_ref[pl.ds(sink * rows + slot * LEGS + leg, 1), :] = jnp.where(
                    lanes == matrix_ids_ref[diagram, leg], 1.0, 0.0
                )
        return start + counts_ref[sink]

    lax.fori_loop(0, workers, mark, 0)
    chosen = jnp.dot(
        choice_ref[...].astype(jnp.bfloat16), peramb_ref[...], preferred_element_type=jnp.float32
    )
    extent = matrix_ref.shape[2]
    a_per = peramb_ref.shape[1] // extent
    for row in range(a_per):
        spread_ref[pl.ds(row, workers * rows, stride=a_per), :] = chosen[
            :, row * extent : (row + 1) * extent
        ]
    matrix_ref[...] = spread_ref[...].reshape(matrix_ref.shape).astype(jnp.bfloat16)
    for copy in copies:
        copy.wait()


def choose(sources, perambs, source_ids, peramb_ids, sink_counts, workers):
    extent = sources.shape[2]
    rows = MOST * LEGS
    a_per = perambs.shape[1] // extent
    smem = pl.BlockSpec(memory_space=pltpu.SMEM)
    anywhere = pl.BlockSpec(memory_space=pl.ANY)
    vmem = pl.BlockSpec(memory_space=pltpu.VMEM)
    outs = pl.pallas_call(
        functools.partial(choose_kernel, workers),
        in_specs=[smem, smem, smem, anywhere, vmem],
        out_specs=[anywhere] * workers + [vmem],
        out_shape=[jax.ShapeDtypeStruct(sources.shape[1:], sources.dtype)] * workers
        + [jax.ShapeDtypeStruct((workers, rows * a_per, extent), jnp.bfloat16)],
        scratch_shapes=[
            pltpu.SemaphoreType.DMA((workers,)),
            pltpu.VMEM((workers * rows, perambs.shape[0]), jnp.float32),
            pltpu.VMEM((workers * rows * a_per, extent), jnp.float32),
        ],
        compiler_params=pltpu.CompilerParams(vmem_limit_bytes=VMEM),
    )(source_ids, sink_counts, peramb_ids, sources, perambs)
    return outs[:workers], outs[workers]


def legs_kernel(
    workers, counts_ref, weights_ref, matrix_ref, leg3_ref, leg2_ref, leg1_ref, flat_ref, leg_ref
):
    extent = matrix_ref.shape[2]
    rows = MOST * LEGS
    a_per = matrix_ref.shape[1] // rows
    flat_ref[...] = matrix_ref[...].astype(jnp.float32).reshape(flat_ref.shape)
    own = lax.axis_index("work")
    start = lax.fori_loop(0, own, lambda i, total: total + counts_ref[i], 0)
    count = counts_ref[own]
    unit = UNIT_ROWS // a_per
    units = workers // unit
    for slot in range(MOST):
        for leg in range(LEGS):
            base = (slot * LEGS + leg) * a_per
            for row in range(a_per):
                leg_ref[pl.ds(row, workers, stride=a_per), :] = flat_ref[
                    pl.ds(base + row, workers, stride=rows * a_per), :
                ]
            if leg == 2:
                leg3_ref[:, slot * extent : (slot + 1) * extent] = leg_ref[...].T.astype(
                    jnp.bfloat16
                )
            elif leg == 1:
                leg2_ref[slot * extent : (slot + 1) * extent, :] = leg_ref[...].astype(
                    jnp.bfloat16
                )
            else:
                diagram = jnp.minimum(start + slot, weights_ref.shape[0] - 1)
                factor = jnp.where(slot < count, weights_ref[diagram], 0.0)
                leg_ref[...] = (factor * leg_ref[...]).T
                for block in range(units):
                    place = (own // unit) ^ block
                    leg1_ref[block, slot * UNIT_ROWS : (slot + 1) * UNIT_ROWS, :] = leg_ref[
                        pl.ds(pl.multiple_of(place * UNIT_ROWS, UNIT_ROWS), UNIT_ROWS), :
                    ].astype(jnp.bfloat16)


def make_legs(matrices, sink_counts, weights, workers):
    extent = matrices.shape[2]
    a_per = extent // workers
    smem = pl.BlockSpec(memory_space=pltpu.SMEM)
    vmem = pl.BlockSpec(memory_space=pltpu.VMEM)
    return pl.pallas_call(
        functools.partial(legs_kernel, workers),
        in_specs=[smem, smem, vmem],
        out_specs=[vmem] * 3,
        out_shape=[
            jax.ShapeDtypeStruct((extent, MOST * extent), jnp.bfloat16),
            jax.ShapeDtypeStruct((MOST * extent, extent), jnp.bfloat16),
            jax.ShapeDtypeStruct(
                (extent // UNIT_ROWS, MOST * UNIT_ROWS, extent), jnp.bfloat16
            ),
        ],
        scratch_shapes=[
            pltpu.VMEM((matrices.shape[0] * matrices.shape[1], extent), jnp.float32),
            pltpu.VMEM((extent, extent), jnp.float32),
        ],
        compiler_params=pltpu.CompilerParams(vmem_limit_bytes=VMEM),
    )(sink_counts, weights, matrices)


def group_kernel(first, last, units, per_unit, extent, *refs):
    pieces = len(units) * per_unit
    piece_refs = refs[:pieces]
    leg3_ref, leg2_ref, leg1_ref = refs[pieces : pieces + 3]
    refs = refs[pieces + 3 :]
    if not first:
        acc_ref, refs = refs[0], refs[1:]
    out_ref, turned_ref, outer_ref = refs[:3]
    a_per = piece_refs[0].shape[0] // extent
    unit_depth = MOST * UNIT_ROWS
    depth = unit_depth * len(units)
    pitch = depth + 8
    step = pl.program_id(0)

    def inner_legs(place, lane, piece_ref):
        sender = (lax.axis_index("work") & (per_unit - 1)) ^ lane
        third = jnp.dot(
            piece_ref[...], leg3_ref[...], preferred_element_type=jnp.float32
        ).astype(jnp.bfloat16)
        for d in range(MOST):
            columns = third[:, d * extent : (d + 1) * extent]
            wide = jnp.concatenate(
                [columns[a * extent : (a + 1) * extent] for a in range(a_per)], axis=1
            )
            second = jnp.dot(
                leg2_ref[d * extent : (d + 1) * extent, :],
                wide,
                preferred_element_type=jnp.float32,
            )
            for a in range(a_per):
                row = place * unit_depth + d * UNIT_ROWS + sender * a_per + a
                turned_ref[pl.ds(row, extent, stride=pitch), :] = second[
                    :, a * extent : (a + 1) * extent
                ]

    for piece in range(pieces):
        pl.when(step == piece)(
            functools.partial(
                inner_legs, piece // per_unit, piece % per_unit, piece_refs[piece]
            )
        )

    @pl.when(step == 0)
    def turn_outer():
        for place, unit in enumerate(units):
            outer_ref[place * unit_depth : (place + 1) * unit_depth, :] = leg1_ref[
                unit
            ].astype(jnp.float32)

    @pl.when(step >= pieces)
    def outer_leg():
        begin = (step - pieces) * B_BLOCK
        wide = jnp.concatenate(
            [
                turned_ref[pl.ds(pl.multiple_of((begin + b) * pitch, 8), depth), :].astype(
                    jnp.bfloat16
                )
                for b in range(B_BLOCK)
            ],
            axis=1,
        )
        outer = outer_ref[...].T.astype(jnp.bfloat16)
        whole = jnp.dot(outer, wide, preferred_element_type=jnp.float32)
        for b in range(B_BLOCK):
            part = whole[:, b * extent : (b + 1) * extent]
            if not first:
                part = part + acc_ref[b]
            if last:
                refs[3][pl.ds(b, extent, stride=B_BLOCK + 1), :] = part
            else:
                out_ref[b] = part
        if last:
            for a in range(extent):
                out_ref[a] = refs[3][pl.ds(a * (B_BLOCK + 1), B_BLOCK), :].astype(jnp.bfloat16)


def add_group(units, pieces, leg3, leg2, leg1, acc, last):
    extent = leg3.shape[0]
    count = len(pieces)
    per_unit = count // len(units)
    depth = MOST * UNIT_ROWS * len(units)
    first = acc is None
    blocks = extent // B_BLOCK

    def whole_spec(x):
        return pl.BlockSpec(x.shape, lambda i: (0,) * x.ndim)

    def block_of(i):
        return jnp.maximum(i - count, 0)

    operands = [*pieces, leg3, leg2, leg1]
    in_specs = [whole_spec(x) for x in operands]
    if not first:
        operands.append(acc)
        in_specs.append(pl.BlockSpec((B_BLOCK, extent, extent), lambda i: (block_of(i), 0, 0)))
    scratch = [
        pltpu.VMEM((extent * (depth + 8), extent), jnp.float32),
        pltpu.VMEM((depth, extent), jnp.float32),
    ]
    if last:
        out_shape = jax.ShapeDtypeStruct((extent, extent, extent), jnp.bfloat16)
        out_spec = pl.BlockSpec((extent, B_BLOCK, extent), lambda i: (0, block_of(i), 0))
        scratch.append(pltpu.VMEM((extent * (B_BLOCK + 1), extent), jnp.float32))
    else:
        out_shape = jax.ShapeDtypeStruct((extent, extent, extent), jnp.float32)
        out_spec = pl.BlockSpec((B_BLOCK, extent, extent), lambda i: (block_of(i), 0, 0))
    rows = count * pieces[0].shape[0]
    return pl.pallas_call(
        functools.partial(group_kernel, first, last, units, per_unit, extent),
        grid=(count + blocks,),
        in_specs=in_specs,
        out_specs=out_spec,
        out_shape=out_shape,
        scratch_shapes=scratch,
        compiler_params=pltpu.CompilerParams(
            dimension_semantics=("arbitrary",), vmem_limit_bytes=VMEM
        ),
        cost_estimate=pl.CostEstimate(
            flops=6 * MOST * rows * extent * extent,
            bytes_accessed=12 * extent**3,
            transcendentals=0,
        ),
    )(*operands)


def per_device(sources, perambs, source_ids, peramb_ids, sink_counts, weights):
    workers = lax.axis_size("work")
    extent = sources.shape[2]
    per_unit = UNIT_ROWS * workers // extent
    pieces, matrices = choose(sources, perambs, source_ids, peramb_ids, sink_counts, workers)
    matrices = lax.all_to_all(matrices, "work", split_axis=0, concat_axis=0, tiled=True)
    leg3, leg2, leg1 = make_legs(matrices, sink_counts, weights, workers)

    arrived = [pieces[0]]
    for shift in range(1, workers):
        arrived.append(
            lax.ppermute(pieces[shift], "work", [(i, i ^ shift) for i in range(workers)])
        )
    acc = None
    for group, units in enumerate(GROUPS):
        members = [arrived[u * per_unit + lane] for u in units for lane in range(per_unit)]
        acc = add_group(units, members, leg3, leg2, leg1, acc, group == len(GROUPS) - 1)
    return acc.reshape(1, extent * extent, extent)


def solution(mesh):
    return jax.shard_map(
        per_device,
        mesh=mesh,
        in_specs=(P("cfg", "work", None), P("cfg", "work"), P(), P(), P(), P()),
        out_specs=P(("cfg", "work"), None, None),
        check_vma=False,
    )
```

```python
import functools

import jax
import jax.numpy as jnp
from jax import lax
from jax.experimental import pallas as pl
from jax.experimental.pallas import tpu as pltpu
from jax.sharding import PartitionSpec as P

MOST = 6
LEGS = 3
UNIT_ROWS = 16
B_BLOCK = 64
ACC = jnp.bfloat16
SENT = (4, 0, 1, 5, 2, 3, 6, 7)
GROUPS = ((0, 1, 2, 4, 5), (3, 6), (7,))
IN_FLIGHT = 5
VMEM = 56 * 1024 * 1024


def pieces_kernel(shifts, ids_ref, source_ref, *refs):
    piece_refs, sems = refs[: len(shifts)], refs[len(shifts)]
    own = lax.axis_index("work")
    copies = []
    for i, shift in enumerate(shifts):
        copy = pltpu.make_async_copy(
            source_ref.at[ids_ref[own ^ shift]], piece_refs[i], sems.at[i]
        )
        copy.start()
        copies.append(copy)
    for copy in copies:
        copy.wait()


def choose_pieces(sources, source_ids, shifts):
    return pl.pallas_call(
        functools.partial(pieces_kernel, shifts),
        in_specs=[pl.BlockSpec(memory_space=pltpu.SMEM), pl.BlockSpec(memory_space=pl.ANY)],
        out_specs=[pl.BlockSpec(memory_space=pltpu.VMEM)] * len(shifts),
        out_shape=[jax.ShapeDtypeStruct(sources.shape[1:], sources.dtype)] * len(shifts),
        scratch_shapes=[pltpu.SemaphoreType.DMA((len(shifts),))],
        compiler_params=pltpu.CompilerParams(vmem_limit_bytes=VMEM),
    )(source_ids, sources)


def matrices_kernel(workers, counts_ref, matrix_ids_ref, peramb_ref, matrix_ref, choice_ref, spread_ref):
    rows = MOST * LEGS
    diagrams = matrix_ids_ref.shape[0]
    total = peramb_ref.shape[0]
    lanes = lax.broadcasted_iota(jnp.int32, (1, total), 1)

    def mark(sink, start):
        for slot in range(MOST):
            diagram = jnp.minimum(start + slot, diagrams - 1)
            for leg in range(LEGS):
                choice_ref[pl.ds(sink * rows + slot * LEGS + leg, 1), :] = jnp.where(
                    lanes == matrix_ids_ref[diagram, leg], 1.0, 0.0
                )
        return start + counts_ref[sink]

    lax.fori_loop(0, workers, mark, 0)
    chosen = jnp.dot(
        choice_ref[...].astype(jnp.bfloat16), peramb_ref[...], preferred_element_type=jnp.float32
    )
    extent = matrix_ref.shape[2]
    a_per = peramb_ref.shape[1] // extent
    for row in range(a_per):
        spread_ref[pl.ds(row, workers * rows, stride=a_per), :] = chosen[
            :, row * extent : (row + 1) * extent
        ]
    matrix_ref[...] = spread_ref[...].reshape(matrix_ref.shape).astype(jnp.bfloat16)


def choose_matrices(perambs, peramb_ids, sink_counts, workers, extent):
    rows = MOST * LEGS
    a_per = perambs.shape[1] // extent
    smem = pl.BlockSpec(memory_space=pltpu.SMEM)
    vmem = pl.BlockSpec(memory_space=pltpu.VMEM)
    return pl.pallas_call(
        functools.partial(matrices_kernel, workers),
        in_specs=[smem, smem, vmem],
        out_specs=vmem,
        out_shape=jax.ShapeDtypeStruct((workers, rows * a_per, extent), jnp.bfloat16),
        scratch_shapes=[
            pltpu.VMEM((workers * rows, perambs.shape[0]), jnp.float32),
            pltpu.VMEM((workers * rows * a_per, extent), jnp.float32),
        ],
        compiler_params=pltpu.CompilerParams(vmem_limit_bytes=VMEM),
    )(sink_counts, peramb_ids, perambs)


def legs_kernel(
    workers, counts_ref, weights_ref, matrix_ref, leg3_ref, leg2_ref, leg1_ref, flat_ref, leg_ref
):
    extent = matrix_ref.shape[2]
    rows = MOST * LEGS
    a_per = matrix_ref.shape[1] // rows
    flat_ref[...] = matrix_ref[...].astype(jnp.float32).reshape(flat_ref.shape)
    own = lax.axis_index("work")
    start = lax.fori_loop(0, own, lambda i, total: total + counts_ref[i], 0)
    count = counts_ref[own]
    unit = UNIT_ROWS // a_per
    units = workers // unit
    for slot in range(MOST):
        for leg in range(LEGS):
            base = (slot * LEGS + leg) * a_per
            for row in range(a_per):
                leg_ref[pl.ds(row, workers, stride=a_per), :] = flat_ref[
                    pl.ds(base + row, workers, stride=rows * a_per), :
                ]
            if leg == 2:
                leg3_ref[:, slot * extent : (slot + 1) * extent] = leg_ref[...].T.astype(
                    jnp.bfloat16
                )
            elif leg == 1:
                leg2_ref[slot * extent : (slot + 1) * extent, :] = leg_ref[...].astype(
                    jnp.bfloat16
                )
            else:
                diagram = jnp.minimum(start + slot, weights_ref.shape[0] - 1)
                factor = jnp.where(slot < count, weights_ref[diagram], 0.0)
                leg_ref[...] = (factor * leg_ref[...]).T
                for block in range(units):
                    place = (own // unit) ^ block
                    leg1_ref[block, slot * UNIT_ROWS : (slot + 1) * UNIT_ROWS, :] = leg_ref[
                        pl.ds(pl.multiple_of(place * UNIT_ROWS, UNIT_ROWS), UNIT_ROWS), :
                    ].astype(jnp.bfloat16)


def make_legs(matrices, sink_counts, weights, workers):
    extent = matrices.shape[2]
    a_per = extent // workers
    smem = pl.BlockSpec(memory_space=pltpu.SMEM)
    vmem = pl.BlockSpec(memory_space=pltpu.VMEM)
    return pl.pallas_call(
        functools.partial(legs_kernel, workers),
        in_specs=[smem, smem, vmem],
        out_specs=[vmem] * 3,
        out_shape=[
            jax.ShapeDtypeStruct((extent, MOST * extent), jnp.bfloat16),
            jax.ShapeDtypeStruct((MOST * extent, extent), jnp.bfloat16),
            jax.ShapeDtypeStruct(
                (extent // UNIT_ROWS, MOST * UNIT_ROWS, extent), jnp.bfloat16
            ),
        ],
        scratch_shapes=[
            pltpu.VMEM((matrices.shape[0] * matrices.shape[1], extent), jnp.float32),
            pltpu.VMEM((extent, extent), jnp.float32),
        ],
        compiler_params=pltpu.CompilerParams(vmem_limit_bytes=VMEM),
    )(sink_counts, weights, matrices)


def group_kernel(first, last, units, per_unit, extent, *refs):
    pieces = len(units) * per_unit
    piece_refs = refs[:pieces]
    leg3_ref, leg2_ref, leg1_ref = refs[pieces : pieces + 3]
    refs = refs[pieces + 3 :]
    if not first:
        acc_ref, refs = refs[0], refs[1:]
    out_ref, turned_ref, outer_ref, across_ref = refs[:4]
    a_per = piece_refs[0].shape[0] // extent
    unit_depth = MOST * UNIT_ROWS
    depth = unit_depth * len(units)
    pitch = depth + 8
    step = pl.program_id(0)

    def inner_legs(place, lane, piece_ref):
        sender = (lax.axis_index("work") & (per_unit - 1)) ^ lane
        third = jnp.dot(
            piece_ref[...], leg3_ref[...], preferred_element_type=jnp.float32
        ).astype(jnp.bfloat16)
        for d in range(MOST):
            columns = third[:, d * extent : (d + 1) * extent]
            wide = jnp.concatenate(
                [columns[a * extent : (a + 1) * extent] for a in range(a_per)], axis=1
            )
            second = jnp.dot(
                leg2_ref[d * extent : (d + 1) * extent, :],
                wide,
                preferred_element_type=jnp.float32,
            )
            for a in range(a_per):
                row = place * unit_depth + d * UNIT_ROWS + sender * a_per + a
                turned_ref[pl.ds(row, extent, stride=pitch), :] = second[
                    :, a * extent : (a + 1) * extent
                ]

    for piece in range(pieces):
        pl.when(step == piece)(
            functools.partial(
                inner_legs, piece // per_unit, piece % per_unit, piece_refs[piece]
            )
        )

    @pl.when(step == 0)
    def turn_outer():
        for place, unit in enumerate(units):
            outer_ref[place * unit_depth : (place + 1) * unit_depth, :] = leg1_ref[
                unit
            ].astype(jnp.float32)
        across_ref[...] = outer_ref[...].T.astype(jnp.bfloat16)

    @pl.when(step >= pieces)
    def outer_leg():
        begin = (step - pieces) * B_BLOCK
        wide = jnp.concatenate(
            [
                turned_ref[pl.ds(pl.multiple_of((begin + b) * pitch, 8), depth), :].astype(
                    jnp.bfloat16
                )
                for b in range(B_BLOCK)
            ],
            axis=1,
        )
        whole = jnp.dot(across_ref[...], wide, preferred_element_type=jnp.float32)
        for b in range(B_BLOCK):
            part = whole[:, b * extent : (b + 1) * extent]
            if not first:
                part = part + acc_ref[b].astype(jnp.float32)
            if last:
                refs[4][pl.ds(b, extent, stride=B_BLOCK + 8), :] = part
            else:
                out_ref[b] = part.astype(out_ref.dtype)
        if last:
            for a in range(extent):
                out_ref[a] = refs[4][pl.ds(a * (B_BLOCK + 8), B_BLOCK), :].astype(jnp.bfloat16)


def add_group(units, pieces, leg3, leg2, leg1, acc, last):
    extent = leg3.shape[0]
    count = len(pieces)
    per_unit = count // len(units)
    depth = MOST * UNIT_ROWS * len(units)
    first = acc is None
    blocks = extent // B_BLOCK

    def whole_spec(x):
        return pl.BlockSpec(x.shape, lambda i: (0,) * x.ndim)

    def block_of(i):
        return jnp.maximum(i - count, 0)

    operands = [*pieces, leg3, leg2, leg1]
    in_specs = [whole_spec(x) for x in operands]
    if not first:
        operands.append(acc)
        in_specs.append(pl.BlockSpec((B_BLOCK, extent, extent), lambda i: (block_of(i), 0, 0)))
    scratch = [
        pltpu.VMEM((extent * (depth + 8), extent), jnp.float32),
        pltpu.VMEM((depth, extent), jnp.float32),
        pltpu.VMEM((extent, depth), jnp.bfloat16),
    ]
    if last:
        out_shape = jax.ShapeDtypeStruct((extent, extent, extent), jnp.bfloat16)
        out_spec = pl.BlockSpec((extent, B_BLOCK, extent), lambda i: (0, block_of(i), 0))
        scratch.append(pltpu.VMEM((extent * (B_BLOCK + 8), extent), jnp.float32))
    else:
        out_shape = jax.ShapeDtypeStruct((extent, extent, extent), ACC)
        out_spec = pl.BlockSpec((B_BLOCK, extent, extent), lambda i: (block_of(i), 0, 0))
    rows = count * pieces[0].shape[0]
    return pl.pallas_call(
        functools.partial(group_kernel, first, last, units, per_unit, extent),
        grid=(count + blocks,),
        in_specs=in_specs,
        out_specs=out_spec,
        out_shape=out_shape,
        scratch_shapes=scratch,
        compiler_params=pltpu.CompilerParams(
            dimension_semantics=("arbitrary",), vmem_limit_bytes=VMEM
        ),
        cost_estimate=pl.CostEstimate(
            flops=6 * MOST * rows * extent * extent,
            bytes_accessed=12 * extent**3,
            transcendentals=0,
        ),
    )(*operands)


def per_device(sources, perambs, source_ids, peramb_ids, sink_counts, weights):
    workers = lax.axis_size("work")
    extent = sources.shape[2]
    per_unit = UNIT_ROWS * workers // extent
    order = [u * per_unit + lane for u in SENT for lane in range(per_unit)]
    order.remove(0)
    early, late = tuple(order[:IN_FLIGHT]), (0, *order[IN_FLIGHT:])
    pieces = dict(zip(early, choose_pieces(sources, source_ids, early)))
    pieces.update(zip(late, choose_pieces(sources, source_ids, late)))
    matrices = choose_matrices(perambs, peramb_ids, sink_counts, workers, extent)
    matrices = lax.all_to_all(matrices, "work", split_axis=0, concat_axis=0, tiled=True)
    leg3, leg2, leg1 = make_legs(matrices, sink_counts, weights, workers)

    arrived = {0: pieces[0]}
    for place, shift in enumerate(order):
        piece = pieces[shift]
        if place >= IN_FLIGHT:
            before = order[place - IN_FLIGHT]
            piece, arrived[before] = lax.optimization_barrier((piece, arrived[before]))
        arrived[shift] = lax.ppermute(piece, "work", [(i, i ^ shift) for i in range(workers)])
    acc = None
    for group, units in enumerate(GROUPS):
        members = [arrived[u * per_unit + lane] for u in units for lane in range(per_unit)]
        acc = add_group(units, members, leg3, leg2, leg1, acc, group == len(GROUPS) - 1)
    return acc.reshape(1, extent * extent, extent)


def solution(mesh):
    return jax.shard_map(
        per_device,
        mesh=mesh,
        in_specs=(P("cfg", "work", None), P("cfg", "work"), P(), P(), P(), P()),
        out_specs=P(("cfg", "work"), None, None),
        check_vma=False,
    )
```

```python
import functools

import jax
import jax.numpy as jnp
from jax import lax
from jax.experimental import pallas as pl
from jax.experimental.pallas import tpu as pltpu
from jax.sharding import PartitionSpec as P

MOST = 6
LEGS = 3
UNIT_ROWS = 16
B_BLOCK = 64
ACC = jnp.bfloat16
GROUPS = ((0, 1, 2, 3, 4), (5, 6), (7,))
FAR_AHEAD = 3
NEAR_AHEAD = 2
VMEM = 60 * 1024 * 1024


def pieces_kernel(shifts, ids_ref, source_ref, *refs):
    piece_refs, sems = refs[: len(shifts)], refs[len(shifts)]
    own = lax.axis_index("work")
    copies = []
    for i, shift in enumerate(shifts):
        copy = pltpu.make_async_copy(
            source_ref.at[ids_ref[own ^ shift]], piece_refs[i], sems.at[i]
        )
        copy.start()
        copies.append(copy)
    for copy in copies:
        copy.wait()


def choose_pieces(sources, source_ids, shifts):
    return pl.pallas_call(
        functools.partial(pieces_kernel, shifts),
        in_specs=[pl.BlockSpec(memory_space=pltpu.SMEM), pl.BlockSpec(memory_space=pl.ANY)],
        out_specs=[pl.BlockSpec(memory_space=pltpu.VMEM)] * len(shifts),
        out_shape=[jax.ShapeDtypeStruct(sources.shape[1:], sources.dtype)] * len(shifts),
        scratch_shapes=[pltpu.SemaphoreType.DMA((len(shifts),))],
        compiler_params=pltpu.CompilerParams(vmem_limit_bytes=VMEM),
    )(source_ids, sources)


def matrices_kernel(workers, counts_ref, matrix_ids_ref, peramb_ref, matrix_ref, choice_ref, spread_ref):
    rows = MOST * LEGS
    diagrams = matrix_ids_ref.shape[1]
    total = peramb_ref.shape[0]
    lanes = lax.broadcasted_iota(jnp.int32, (1, total), 1)

    def mark(sink, start):
        for slot in range(MOST):
            diagram = jnp.minimum(start + slot, diagrams - 1)
            for leg in range(LEGS):
                choice_ref[pl.ds(sink * rows + slot * LEGS + leg, 1), :] = jnp.where(
                    lanes == matrix_ids_ref[leg, diagram], 1.0, 0.0
                )
        return start + counts_ref[sink]

    lax.fori_loop(0, workers, mark, 0)
    chosen = jnp.dot(
        choice_ref[...].astype(jnp.bfloat16), peramb_ref[...], preferred_element_type=jnp.float32
    )
    extent = matrix_ref.shape[2]
    a_per = peramb_ref.shape[1] // extent
    for row in range(a_per):
        spread_ref[pl.ds(row, workers * rows, stride=a_per), :] = chosen[
            :, row * extent : (row + 1) * extent
        ]
    matrix_ref[...] = spread_ref[...].reshape(matrix_ref.shape).astype(jnp.bfloat16)


def choose_matrices(perambs, peramb_ids, sink_counts, workers, extent):
    rows = MOST * LEGS
    a_per = perambs.shape[1] // extent
    smem = pl.BlockSpec(memory_space=pltpu.SMEM)
    vmem = pl.BlockSpec(memory_space=pltpu.VMEM)
    return pl.pallas_call(
        functools.partial(matrices_kernel, workers),
        in_specs=[smem, smem, vmem],
        out_specs=vmem,
        out_shape=jax.ShapeDtypeStruct((workers, rows * a_per, extent), jnp.bfloat16),
        scratch_shapes=[
            pltpu.VMEM((workers * rows, perambs.shape[0]), jnp.float32),
            pltpu.VMEM((workers * rows * a_per, extent), jnp.float32),
        ],
        compiler_params=pltpu.CompilerParams(vmem_limit_bytes=VMEM),
    )(sink_counts, peramb_ids.T, perambs)


def legs_kernel(
    workers, counts_ref, weights_ref, matrix_ref, leg3_ref, leg2_ref, leg1_ref, flat_ref, leg_ref
):
    extent = matrix_ref.shape[2]
    rows = MOST * LEGS
    a_per = matrix_ref.shape[1] // rows
    flat_ref[...] = matrix_ref[...].astype(jnp.float32).reshape(flat_ref.shape)
    own = lax.axis_index("work")
    start = lax.fori_loop(0, own, lambda i, total: total + counts_ref[i], 0)
    count = counts_ref[own]
    unit = UNIT_ROWS // a_per
    units = workers // unit
    for slot in range(MOST):
        for leg in range(LEGS):
            base = (slot * LEGS + leg) * a_per
            for row in range(a_per):
                leg_ref[pl.ds(row, workers, stride=a_per), :] = flat_ref[
                    pl.ds(base + row, workers, stride=rows * a_per), :
                ]
            if leg == 2:
                leg3_ref[:, slot * extent : (slot + 1) * extent] = leg_ref[...].T.astype(
                    jnp.bfloat16
                )
            elif leg == 1:
                leg2_ref[slot * extent : (slot + 1) * extent, :] = leg_ref[...].astype(
                    jnp.bfloat16
                )
            else:
                diagram = jnp.minimum(start + slot, weights_ref.shape[0] - 1)
                factor = jnp.where(slot < count, weights_ref[diagram], 0.0)
                leg_ref[...] = (factor * leg_ref[...]).T
                for block in range(units):
                    place = (own // unit) ^ block
                    leg1_ref[block, slot * UNIT_ROWS : (slot + 1) * UNIT_ROWS, :] = leg_ref[
                        pl.ds(pl.multiple_of(place * UNIT_ROWS, UNIT_ROWS), UNIT_ROWS), :
                    ].astype(jnp.bfloat16)


def make_legs(matrices, sink_counts, weights, workers):
    extent = matrices.shape[2]
    a_per = extent // workers
    smem = pl.BlockSpec(memory_space=pltpu.SMEM)
    vmem = pl.BlockSpec(memory_space=pltpu.VMEM)
    return pl.pallas_call(
        functools.partial(legs_kernel, workers),
        in_specs=[smem, smem, vmem],
        out_specs=[vmem] * 3,
        out_shape=[
            jax.ShapeDtypeStruct((extent, MOST * extent), jnp.bfloat16),
            jax.ShapeDtypeStruct((MOST * extent, extent), jnp.bfloat16),
            jax.ShapeDtypeStruct(
                (extent // UNIT_ROWS, MOST * UNIT_ROWS, extent), jnp.bfloat16
            ),
        ],
        scratch_shapes=[
            pltpu.VMEM((matrices.shape[0] * matrices.shape[1], extent), jnp.float32),
            pltpu.VMEM((extent, extent), jnp.float32),
        ],
        compiler_params=pltpu.CompilerParams(vmem_limit_bytes=VMEM),
    )(sink_counts, weights, matrices)


def group_kernel(first, last, units, per_unit, extent, *refs):
    pieces = len(units) * per_unit
    piece_refs = refs[:pieces]
    leg3_ref, leg2_ref, leg1_ref = refs[pieces : pieces + 3]
    refs = refs[pieces + 3 :]
    if not first:
        acc_ref, refs = refs[0], refs[1:]
    out_ref, turned_ref, outer_ref, across_ref = refs[:4]
    a_per = piece_refs[0].shape[0] // extent
    unit_depth = MOST * UNIT_ROWS
    depth = unit_depth * len(units)
    pitch = depth + 8
    step = pl.program_id(0)

    def inner_legs(place, lane, piece_ref):
        sender = (lax.axis_index("work") & (per_unit - 1)) ^ lane
        third = jnp.dot(
            piece_ref[...], leg3_ref[...], preferred_element_type=jnp.float32
        ).astype(jnp.bfloat16)
        for d in range(MOST):
            columns = third[:, d * extent : (d + 1) * extent]
            wide = jnp.concatenate(
                [columns[a * extent : (a + 1) * extent] for a in range(a_per)], axis=1
            )
            second = jnp.dot(
                leg2_ref[d * extent : (d + 1) * extent, :],
                wide,
                preferred_element_type=jnp.float32,
            )
            for a in range(a_per):
                row = place * unit_depth + d * UNIT_ROWS + sender * a_per + a
                turned_ref[pl.ds(row, extent, stride=pitch), :] = second[
                    :, a * extent : (a + 1) * extent
                ]

    for piece in range(pieces):
        pl.when(step == piece)(
            functools.partial(
                inner_legs, piece // per_unit, piece % per_unit, piece_refs[piece]
            )
        )

    @pl.when(step == 0)
    def turn_outer():
        for place, unit in enumerate(units):
            outer_ref[place * unit_depth : (place + 1) * unit_depth, :] = leg1_ref[
                unit
            ].astype(jnp.float32)
        across_ref[...] = outer_ref[...].T.astype(jnp.bfloat16)

    @pl.when(step >= pieces)
    def outer_leg():
        begin = (step - pieces) * B_BLOCK
        wide = jnp.concatenate(
            [
                turned_ref[pl.ds(pl.multiple_of((begin + b) * pitch, 8), depth), :].astype(
                    jnp.bfloat16
                )
                for b in range(B_BLOCK)
            ],
            axis=1,
        )
        whole = jnp.dot(across_ref[...], wide, preferred_element_type=jnp.float32)
        for b in range(B_BLOCK):
            part = whole[:, b * extent : (b + 1) * extent]
            if not first:
                part = part + acc_ref[b].astype(jnp.float32)
            if last:
                refs[4][pl.ds(b, extent, stride=B_BLOCK + 8), :] = part
            else:
                out_ref[b] = part.astype(out_ref.dtype)
        if last:
            for a in range(extent):
                out_ref[a] = refs[4][pl.ds(a * (B_BLOCK + 8), B_BLOCK), :].astype(jnp.bfloat16)


def add_group(units, pieces, leg3, leg2, leg1, acc, last):
    extent = leg3.shape[0]
    count = len(pieces)
    per_unit = count // len(units)
    depth = MOST * UNIT_ROWS * len(units)
    first = acc is None
    blocks = extent // B_BLOCK

    def whole_spec(x):
        return pl.BlockSpec(x.shape, lambda i: (0,) * x.ndim)

    def block_of(i):
        return jnp.maximum(i - count, 0)

    operands = [*pieces, leg3, leg2, leg1]
    in_specs = [whole_spec(x) for x in operands]
    if not first:
        operands.append(acc)
        in_specs.append(pl.BlockSpec((B_BLOCK, extent, extent), lambda i: (block_of(i), 0, 0)))
    scratch = [
        pltpu.VMEM((extent * (depth + 8), extent), jnp.float32),
        pltpu.VMEM((depth, extent), jnp.float32),
        pltpu.VMEM((extent, depth), jnp.bfloat16),
    ]
    if last:
        out_shape = jax.ShapeDtypeStruct((extent, extent, extent), jnp.bfloat16)
        out_spec = pl.BlockSpec((extent, B_BLOCK, extent), lambda i: (0, block_of(i), 0))
        scratch.append(pltpu.VMEM((extent * (B_BLOCK + 8), extent), jnp.float32))
    else:
        out_shape = jax.ShapeDtypeStruct((extent, extent, extent), ACC)
        out_spec = pl.BlockSpec((B_BLOCK, extent, extent), lambda i: (block_of(i), 0, 0))
    rows = count * pieces[0].shape[0]
    return pl.pallas_call(
        functools.partial(group_kernel, first, last, units, per_unit, extent),
        grid=(count + blocks,),
        in_specs=in_specs,
        out_specs=out_spec,
        out_shape=out_shape,
        scratch_shapes=scratch,
        compiler_params=pltpu.CompilerParams(
            dimension_semantics=("arbitrary",), vmem_limit_bytes=VMEM
        ),
        cost_estimate=pl.CostEstimate(
            flops=6 * MOST * rows * extent * extent,
            bytes_accessed=12 * extent**3,
            transcendentals=0,
        ),
    )(*operands)


def per_device(sources, perambs, source_ids, peramb_ids, sink_counts, weights):
    workers = lax.axis_size("work")
    extent = sources.shape[2]
    per_unit = UNIT_ROWS * workers // extent
    half = workers // 2
    far = list(range(half, workers))
    near = [1, *range(half // 2, half), *range(2, half // 2)]
    early = (*far[:FAR_AHEAD], *near[:NEAR_AHEAD])
    late = (0, *far[FAR_AHEAD:], *near[NEAR_AHEAD:])
    pieces = dict(zip(early, choose_pieces(sources, source_ids, early)))
    pieces.update(zip(late, choose_pieces(sources, source_ids, late)))
    arrived = {0: pieces[0]}

    def send(shift, *after):
        piece = pieces[shift]
        for before in after:
            piece, arrived[before] = lax.optimization_barrier((piece, arrived[before]))
        arrived[shift] = lax.ppermute(piece, "work", [(i, i ^ shift) for i in range(workers)])

    for shift in early:
        send(shift)
    matrices = choose_matrices(perambs, peramb_ids, sink_counts, workers, extent)
    matrices, arrived[1] = lax.optimization_barrier((matrices, arrived[1]))
    matrices = lax.all_to_all(matrices, "work", split_axis=0, concat_axis=0, tiled=True)
    leg3, leg2, leg1 = make_legs(matrices, sink_counts, weights, workers)
    for place in range(NEAR_AHEAD, len(near)):
        send(near[place], near[place - NEAR_AHEAD])

    acc = None
    sent = FAR_AHEAD
    for group, units in enumerate(GROUPS):
        last = group == len(GROUPS) - 1
        members = [u * per_unit + lane for u in units for lane in range(per_unit)]
        wanted = len(far) if last else far.index(max(members)) + 1 + FAR_AHEAD
        while sent < min(wanted, len(far)):
            send(far[sent], far[sent - FAR_AHEAD])
            sent += 1
        acc = add_group(units, [arrived[m] for m in members], leg3, leg2, leg1, acc, last)
        if sent < len(far):
            pieces[far[sent]], acc = lax.optimization_barrier((pieces[far[sent]], acc))
    return acc.reshape(1, extent * extent, extent)


def solution(mesh):
    return jax.shard_map(
        per_device,
        mesh=mesh,
        in_specs=(P("cfg", "work", None), P("cfg", "work"), P(), P(), P(), P()),
        out_specs=P(("cfg", "work"), None, None),
        check_vma=False,
    )
```

```python
import functools

import jax
import jax.numpy as jnp
from jax import lax
from jax.experimental import pallas as pl
from jax.experimental.pallas import tpu as pltpu
from jax.sharding import PartitionSpec as P

MOST = 6
LEGS = 3
UNIT_ROWS = 16
B_BLOCK = 64
ACC = jnp.bfloat16
GROUPS = ((0, 1, 2, 3, 4), (5, 6), (7,))
FAR_AHEAD = 3
NEAR_AHEAD = 2
VMEM = 46 * 1024 * 1024


def pieces_kernel(shifts, ids_ref, source_ref, *refs):
    piece_refs, (held_ref, in_sems, out_sems) = refs[: len(shifts)], refs[len(shifts) :]
    own = lax.axis_index("work")
    reads, writes = [], []
    for i, shift in enumerate(shifts):
        reads.append(
            pltpu.make_async_copy(
                source_ref.at[ids_ref[own ^ shift]], held_ref.at[i], in_sems.at[i]
            )
        )
        writes.append(pltpu.make_async_copy(held_ref.at[i], piece_refs[i], out_sems.at[i]))
        reads[i].start()
    for read, write in zip(reads, writes):
        read.wait()
        write.start()
    for write in writes:
        write.wait()


def choose_pieces(sources, source_ids, shifts):
    return pl.pallas_call(
        functools.partial(pieces_kernel, shifts),
        in_specs=[pl.BlockSpec(memory_space=pltpu.SMEM), pl.BlockSpec(memory_space=pl.ANY)],
        out_specs=[pl.BlockSpec(memory_space=pl.ANY)] * len(shifts),
        out_shape=[jax.ShapeDtypeStruct(sources.shape[1:], sources.dtype)] * len(shifts),
        scratch_shapes=[
            pltpu.VMEM((len(shifts), *sources.shape[1:]), sources.dtype),
            pltpu.SemaphoreType.DMA((len(shifts),)),
            pltpu.SemaphoreType.DMA((len(shifts),)),
        ],
        compiler_params=pltpu.CompilerParams(vmem_limit_bytes=VMEM),
    )(source_ids, sources)


def matrices_kernel(workers, counts_ref, matrix_ids_ref, peramb_ref, matrix_ref, choice_ref, spread_ref):
    rows = MOST * LEGS
    diagrams = matrix_ids_ref.shape[1]
    total = peramb_ref.shape[0]
    lanes = lax.broadcasted_iota(jnp.int32, (1, total), 1)

    def mark(sink, start):
        for slot in range(MOST):
            diagram = jnp.minimum(start + slot, diagrams - 1)
            for leg in range(LEGS):
                choice_ref[pl.ds(sink * rows + slot * LEGS + leg, 1), :] = jnp.where(
                    lanes == matrix_ids_ref[leg, diagram], 1.0, 0.0
                )
        return start + counts_ref[sink]

    lax.fori_loop(0, workers, mark, 0)
    chosen = jnp.dot(
        choice_ref[...].astype(jnp.bfloat16), peramb_ref[...], preferred_element_type=jnp.float32
    )
    extent = matrix_ref.shape[2]
    a_per = peramb_ref.shape[1] // extent
    for row in range(a_per):
        spread_ref[pl.ds(row, workers * rows, stride=a_per), :] = chosen[
            :, row * extent : (row + 1) * extent
        ]
    matrix_ref[...] = spread_ref[...].reshape(matrix_ref.shape).astype(jnp.bfloat16)


def choose_matrices(perambs, peramb_ids, sink_counts, workers, extent):
    rows = MOST * LEGS
    a_per = perambs.shape[1] // extent
    smem = pl.BlockSpec(memory_space=pltpu.SMEM)
    vmem = pl.BlockSpec(memory_space=pltpu.VMEM)
    return pl.pallas_call(
        functools.partial(matrices_kernel, workers),
        in_specs=[smem, smem, vmem],
        out_specs=vmem,
        out_shape=jax.ShapeDtypeStruct((workers, rows * a_per, extent), jnp.bfloat16),
        scratch_shapes=[
            pltpu.VMEM((workers * rows, perambs.shape[0]), jnp.float32),
            pltpu.VMEM((workers * rows * a_per, extent), jnp.float32),
        ],
        compiler_params=pltpu.CompilerParams(vmem_limit_bytes=VMEM),
    )(sink_counts, peramb_ids.T, perambs)


def legs_kernel(
    workers, counts_ref, weights_ref, matrix_ref, leg3_ref, leg2_ref, leg1_ref, flat_ref, leg_ref
):
    extent = matrix_ref.shape[2]
    rows = MOST * LEGS
    a_per = matrix_ref.shape[1] // rows
    flat_ref[...] = matrix_ref[...].astype(jnp.float32).reshape(flat_ref.shape)
    own = lax.axis_index("work")
    start = lax.fori_loop(0, own, lambda i, total: total + counts_ref[i], 0)
    count = counts_ref[own]
    unit = UNIT_ROWS // a_per
    units = workers // unit
    for slot in range(MOST):
        for leg in range(LEGS):
            base = (slot * LEGS + leg) * a_per
            for row in range(a_per):
                leg_ref[pl.ds(row, workers, stride=a_per), :] = flat_ref[
                    pl.ds(base + row, workers, stride=rows * a_per), :
                ]
            if leg == 2:
                leg3_ref[:, slot * extent : (slot + 1) * extent] = leg_ref[...].T.astype(
                    jnp.bfloat16
                )
            elif leg == 1:
                leg2_ref[slot * extent : (slot + 1) * extent, :] = leg_ref[...].astype(
                    jnp.bfloat16
                )
            else:
                diagram = jnp.minimum(start + slot, weights_ref.shape[0] - 1)
                factor = jnp.where(slot < count, weights_ref[diagram], 0.0)
                leg_ref[...] = (factor * leg_ref[...]).T
                for block in range(units):
                    place = (own // unit) ^ block
                    leg1_ref[block, slot * UNIT_ROWS : (slot + 1) * UNIT_ROWS, :] = leg_ref[
                        pl.ds(pl.multiple_of(place * UNIT_ROWS, UNIT_ROWS), UNIT_ROWS), :
                    ].astype(jnp.bfloat16)


def make_legs(matrices, sink_counts, weights, workers):
    extent = matrices.shape[2]
    a_per = extent // workers
    smem = pl.BlockSpec(memory_space=pltpu.SMEM)
    vmem = pl.BlockSpec(memory_space=pltpu.VMEM)
    return pl.pallas_call(
        functools.partial(legs_kernel, workers),
        in_specs=[smem, smem, vmem],
        out_specs=[vmem] * 3,
        out_shape=[
            jax.ShapeDtypeStruct((extent, MOST * extent), jnp.bfloat16),
            jax.ShapeDtypeStruct((MOST * extent, extent), jnp.bfloat16),
            jax.ShapeDtypeStruct(
                (extent // UNIT_ROWS, MOST * UNIT_ROWS, extent), jnp.bfloat16
            ),
        ],
        scratch_shapes=[
            pltpu.VMEM((matrices.shape[0] * matrices.shape[1], extent), jnp.float32),
            pltpu.VMEM((extent, extent), jnp.float32),
        ],
        compiler_params=pltpu.CompilerParams(vmem_limit_bytes=VMEM),
    )(sink_counts, weights, matrices)


def group_kernel(first, last, units, per_unit, extent, *refs):
    pieces = len(units) * per_unit
    piece_refs = refs[:pieces]
    leg3_ref, leg2_ref, leg1_ref = refs[pieces : pieces + 3]
    refs = refs[pieces + 3 :]
    if not first:
        acc_ref, refs = refs[0], refs[1:]
    out_ref, turned_ref, outer_ref, across_ref, held_ref, sems = refs[:6]
    a_per = piece_refs[0].shape[0] // extent
    unit_depth = MOST * UNIT_ROWS
    depth = unit_depth * len(units)
    pitch = depth + 8
    step = pl.program_id(0)

    def fetch(piece):
        return pltpu.make_async_copy(piece_refs[piece], held_ref.at[piece], sems.at[piece])

    @pl.when(step == 0)
    def fetch_all():
        for piece in range(pieces):
            fetch(piece).start()

    def inner_legs(piece):
        place, lane = piece // per_unit, piece % per_unit
        fetch(piece).wait()
        sender = (lax.axis_index("work") & (per_unit - 1)) ^ lane
        third = jnp.dot(
            held_ref[piece], leg3_ref[...], preferred_element_type=jnp.float32
        ).astype(jnp.bfloat16)
        for d in range(MOST):
            columns = third[:, d * extent : (d + 1) * extent]
            wide = jnp.concatenate(
                [columns[a * extent : (a + 1) * extent] for a in range(a_per)], axis=1
            )
            second = jnp.dot(
                leg2_ref[d * extent : (d + 1) * extent, :],
                wide,
                preferred_element_type=jnp.float32,
            )
            for a in range(a_per):
                row = place * unit_depth + d * UNIT_ROWS + sender * a_per + a
                turned_ref[pl.ds(row, extent, stride=pitch), :] = second[
                    :, a * extent : (a + 1) * extent
                ]

    @pl.when(step == 0)
    def turn_outer():
        for place, unit in enumerate(units):
            outer_ref[place * unit_depth : (place + 1) * unit_depth, :] = leg1_ref[
                unit
            ].astype(jnp.float32)
        across_ref[...] = outer_ref[...].T.astype(jnp.bfloat16)

    for piece in range(pieces):
        pl.when(step == piece)(functools.partial(inner_legs, piece))

    @pl.when(step >= pieces)
    def outer_leg():
        begin = (step - pieces) * B_BLOCK
        wide = jnp.concatenate(
            [
                turned_ref[pl.ds(pl.multiple_of((begin + b) * pitch, 8), depth), :].astype(
                    jnp.bfloat16
                )
                for b in range(B_BLOCK)
            ],
            axis=1,
        )
        whole = jnp.dot(across_ref[...], wide, preferred_element_type=jnp.float32)
        for b in range(B_BLOCK):
            part = whole[:, b * extent : (b + 1) * extent]
            if not first:
                part = part + acc_ref[b].astype(jnp.float32)
            if last:
                refs[6][pl.ds(b, extent, stride=B_BLOCK + 8), :] = part
            else:
                out_ref[b] = part.astype(out_ref.dtype)
        if last:
            for a in range(extent):
                out_ref[a] = refs[6][pl.ds(a * (B_BLOCK + 8), B_BLOCK), :].astype(jnp.bfloat16)


def add_group(units, pieces, leg3, leg2, leg1, acc, last):
    extent = leg3.shape[0]
    count = len(pieces)
    per_unit = count // len(units)
    depth = MOST * UNIT_ROWS * len(units)
    first = acc is None
    blocks = extent // B_BLOCK

    def whole_spec(x):
        return pl.BlockSpec(x.shape, lambda i: (0,) * x.ndim)

    def block_of(i):
        return jnp.maximum(i - count, 0)

    operands = [*pieces, leg3, leg2, leg1]
    in_specs = [pl.BlockSpec(memory_space=pl.ANY)] * count
    in_specs += [whole_spec(x) for x in operands[count:]]
    if not first:
        operands.append(acc)
        in_specs.append(pl.BlockSpec((B_BLOCK, extent, extent), lambda i: (block_of(i), 0, 0)))
    scratch = [
        pltpu.VMEM((extent * (depth + 8), extent), jnp.float32),
        pltpu.VMEM((depth, extent), jnp.float32),
        pltpu.VMEM((extent, depth), jnp.bfloat16),
        pltpu.VMEM((count, *pieces[0].shape), jnp.bfloat16),
        pltpu.SemaphoreType.DMA((count,)),
    ]
    if last:
        out_shape = jax.ShapeDtypeStruct((extent, extent, extent), jnp.bfloat16)
        out_spec = pl.BlockSpec((extent, B_BLOCK, extent), lambda i: (0, block_of(i), 0))
        scratch.append(pltpu.VMEM((extent * (B_BLOCK + 8), extent), jnp.float32))
    else:
        out_shape = jax.ShapeDtypeStruct((extent, extent, extent), ACC)
        out_spec = pl.BlockSpec((B_BLOCK, extent, extent), lambda i: (block_of(i), 0, 0))
    rows = count * pieces[0].shape[0]
    return pl.pallas_call(
        functools.partial(group_kernel, first, last, units, per_unit, extent),
        grid=(count + blocks,),
        in_specs=in_specs,
        out_specs=out_spec,
        out_shape=out_shape,
        scratch_shapes=scratch,
        compiler_params=pltpu.CompilerParams(
            dimension_semantics=("arbitrary",), vmem_limit_bytes=VMEM
        ),
        cost_estimate=pl.CostEstimate(
            flops=6 * MOST * rows * extent * extent,
            bytes_accessed=12 * extent**3,
            transcendentals=0,
        ),
    )(*operands)


def per_device(sources, perambs, source_ids, peramb_ids, sink_counts, weights):
    workers = lax.axis_size("work")
    extent = sources.shape[2]
    per_unit = UNIT_ROWS * workers // extent
    half = workers // 2
    far = list(range(half, workers))
    near = [1, *range(half // 2, half), *range(2, half // 2)]
    early = (*far[:FAR_AHEAD], *near[:NEAR_AHEAD])
    late = (0, *far[FAR_AHEAD:], *near[NEAR_AHEAD:])
    pieces = dict(zip(early, choose_pieces(sources, source_ids, early)))
    pieces.update(zip(late, choose_pieces(sources, source_ids, late)))
    arrived = {0: pieces[0]}

    def send(shift, *after):
        piece = pieces[shift]
        for before in after:
            piece, arrived[before] = lax.optimization_barrier((piece, arrived[before]))
        arrived[shift] = lax.ppermute(piece, "work", [(i, i ^ shift) for i in range(workers)])

    for shift in early:
        send(shift)
    matrices = choose_matrices(perambs, peramb_ids, sink_counts, workers, extent)
    matrices, arrived[1] = lax.optimization_barrier((matrices, arrived[1]))
    matrices = lax.all_to_all(matrices, "work", split_axis=0, concat_axis=0, tiled=True)
    leg3, leg2, leg1 = make_legs(matrices, sink_counts, weights, workers)
    for place in range(NEAR_AHEAD, len(near)):
        joined = far[max(place - FAR_AHEAD, 0) : place - FAR_AHEAD + 1] if place < 2 * FAR_AHEAD else []
        send(near[place], near[place - NEAR_AHEAD], *joined)

    acc = None
    sent = FAR_AHEAD
    for group, units in enumerate(GROUPS):
        last = group == len(GROUPS) - 1
        members = [u * per_unit + lane for u in units for lane in range(per_unit)]
        wanted = len(far) if last else far.index(max(members)) + 1 + FAR_AHEAD
        while sent < min(wanted, len(far)):
            send(far[sent], far[sent - FAR_AHEAD])
            sent += 1
        acc = add_group(units, [arrived[m] for m in members], leg3, leg2, leg1, acc, last)
        if sent < len(far):
            pieces[far[sent]], acc = lax.optimization_barrier((pieces[far[sent]], acc))
    return acc.reshape(1, extent * extent, extent)


def solution(mesh):
    return jax.shard_map(
        per_device,
        mesh=mesh,
        in_specs=(P("cfg", "work", None), P("cfg", "work"), P(), P(), P(), P()),
        out_specs=P(("cfg", "work"), None, None),
        check_vma=False,
    )
```

```python
import functools

import jax
import jax.numpy as jnp
from jax import lax
from jax.experimental import pallas as pl
from jax.experimental.pallas import tpu as pltpu
from jax.sharding import PartitionSpec as P

MOST = 6
LEGS = 3
UNIT_ROWS = 16
B_BLOCK = 64
ACC = jnp.bfloat16
GROUPS = ((0, 1, 2, 3, 4), (5, 6), (7,))
IN_FLIGHT = 5
FAR_TURNS = (0, 2)
VMEM = 46 * 1024 * 1024
SMALL_VMEM = 16 * 1024 * 1024


def pieces_kernel(shifts, ids_ref, source_ref, *refs):
    piece_refs, (held_ref, in_sems, out_sems) = refs[: len(shifts)], refs[len(shifts) :]
    own = lax.axis_index("work")
    reads, writes = [], []
    for i, shift in enumerate(shifts):
        reads.append(
            pltpu.make_async_copy(
                source_ref.at[ids_ref[own ^ shift]], held_ref.at[i], in_sems.at[i]
            )
        )
        writes.append(pltpu.make_async_copy(held_ref.at[i], piece_refs[i], out_sems.at[i]))
        reads[i].start()
    for read, write in zip(reads, writes):
        read.wait()
        write.start()
    for write in writes:
        write.wait()


def choose_pieces(sources, source_ids, shifts):
    return pl.pallas_call(
        functools.partial(pieces_kernel, shifts),
        in_specs=[pl.BlockSpec(memory_space=pltpu.SMEM), pl.BlockSpec(memory_space=pl.ANY)],
        out_specs=[pl.BlockSpec(memory_space=pl.ANY)] * len(shifts),
        out_shape=[jax.ShapeDtypeStruct(sources.shape[1:], sources.dtype)] * len(shifts),
        scratch_shapes=[
            pltpu.VMEM((len(shifts), *sources.shape[1:]), sources.dtype),
            pltpu.SemaphoreType.DMA((len(shifts),)),
            pltpu.SemaphoreType.DMA((len(shifts),)),
        ],
        compiler_params=pltpu.CompilerParams(vmem_limit_bytes=SMALL_VMEM),
    )(source_ids, sources)


def matrices_kernel(workers, counts_ref, matrix_ids_ref, peramb_ref, matrix_ref, choice_ref, spread_ref):
    rows = MOST * LEGS
    diagrams = matrix_ids_ref.shape[1]
    total = peramb_ref.shape[0]
    lanes = lax.broadcasted_iota(jnp.int32, (1, total), 1)

    def mark(sink, start):
        for slot in range(MOST):
            diagram = jnp.minimum(start + slot, diagrams - 1)
            for leg in range(LEGS):
                choice_ref[pl.ds(sink * rows + slot * LEGS + leg, 1), :] = jnp.where(
                    lanes == matrix_ids_ref[leg, diagram], 1.0, 0.0
                )
        return start + counts_ref[sink]

    lax.fori_loop(0, workers, mark, 0)
    chosen = jnp.dot(
        choice_ref[...].astype(jnp.bfloat16), peramb_ref[...], preferred_element_type=jnp.float32
    )
    extent = matrix_ref.shape[2]
    a_per = peramb_ref.shape[1] // extent
    for row in range(a_per):
        spread_ref[pl.ds(row, workers * rows, stride=a_per), :] = chosen[
            :, row * extent : (row + 1) * extent
        ]
    matrix_ref[...] = spread_ref[...].reshape(matrix_ref.shape).astype(jnp.bfloat16)


def choose_matrices(perambs, peramb_ids, sink_counts, workers, extent):
    rows = MOST * LEGS
    a_per = perambs.shape[1] // extent
    smem = pl.BlockSpec(memory_space=pltpu.SMEM)
    vmem = pl.BlockSpec(memory_space=pltpu.VMEM)
    return pl.pallas_call(
        functools.partial(matrices_kernel, workers),
        in_specs=[smem, smem, vmem],
        out_specs=vmem,
        out_shape=jax.ShapeDtypeStruct((workers, rows * a_per, extent), jnp.bfloat16),
        scratch_shapes=[
            pltpu.VMEM((workers * rows, perambs.shape[0]), jnp.float32),
            pltpu.VMEM((workers * rows * a_per, extent), jnp.float32),
        ],
        compiler_params=pltpu.CompilerParams(vmem_limit_bytes=SMALL_VMEM),
    )(sink_counts, peramb_ids.T, perambs)


def legs_kernel(
    workers, counts_ref, weights_ref, matrix_ref, leg3_ref, leg2_ref, leg1_ref, flat_ref, leg_ref
):
    extent = matrix_ref.shape[2]
    rows = MOST * LEGS
    a_per = matrix_ref.shape[1] // rows
    flat_ref[...] = matrix_ref[...].astype(jnp.float32).reshape(flat_ref.shape)
    own = lax.axis_index("work")
    start = lax.fori_loop(0, own, lambda i, total: total + counts_ref[i], 0)
    count = counts_ref[own]
    unit = UNIT_ROWS // a_per
    units = workers // unit
    for slot in range(MOST):
        for leg in range(LEGS):
            base = (slot * LEGS + leg) * a_per
            for row in range(a_per):
                leg_ref[pl.ds(row, workers, stride=a_per), :] = flat_ref[
                    pl.ds(base + row, workers, stride=rows * a_per), :
                ]
            if leg == 2:
                leg3_ref[:, slot * extent : (slot + 1) * extent] = leg_ref[...].T.astype(
                    jnp.bfloat16
                )
            elif leg == 1:
                leg2_ref[slot * extent : (slot + 1) * extent, :] = leg_ref[...].astype(
                    jnp.bfloat16
                )
            else:
                diagram = jnp.minimum(start + slot, weights_ref.shape[0] - 1)
                factor = jnp.where(slot < count, weights_ref[diagram], 0.0)
                leg_ref[...] = (factor * leg_ref[...]).T
                for block in range(units):
                    place = (own // unit) ^ block
                    leg1_ref[block, slot * UNIT_ROWS : (slot + 1) * UNIT_ROWS, :] = leg_ref[
                        pl.ds(pl.multiple_of(place * UNIT_ROWS, UNIT_ROWS), UNIT_ROWS), :
                    ].astype(jnp.bfloat16)


def make_legs(matrices, sink_counts, weights, workers):
    extent = matrices.shape[2]
    a_per = extent // workers
    smem = pl.BlockSpec(memory_space=pltpu.SMEM)
    vmem = pl.BlockSpec(memory_space=pltpu.VMEM)
    return pl.pallas_call(
        functools.partial(legs_kernel, workers),
        in_specs=[smem, smem, vmem],
        out_specs=[vmem] * 3,
        out_shape=[
            jax.ShapeDtypeStruct((extent, MOST * extent), jnp.bfloat16),
            jax.ShapeDtypeStruct((MOST * extent, extent), jnp.bfloat16),
            jax.ShapeDtypeStruct(
                (extent // UNIT_ROWS, MOST * UNIT_ROWS, extent), jnp.bfloat16
            ),
        ],
        scratch_shapes=[
            pltpu.VMEM((matrices.shape[0] * matrices.shape[1], extent), jnp.float32),
            pltpu.VMEM((extent, extent), jnp.float32),
        ],
        compiler_params=pltpu.CompilerParams(vmem_limit_bytes=SMALL_VMEM),
    )(sink_counts, weights, matrices)


def group_kernel(first, last, units, per_unit, extent, *refs):
    pieces = len(units) * per_unit
    piece_refs = refs[:pieces]
    leg3_ref, leg2_ref, leg1_ref = refs[pieces : pieces + 3]
    refs = refs[pieces + 3 :]
    if not first:
        acc_ref, refs = refs[0], refs[1:]
    out_ref, turned_ref, outer_ref, across_ref, held_ref, sems = refs[:6]
    a_per = piece_refs[0].shape[0] // extent
    unit_depth = MOST * UNIT_ROWS
    depth = unit_depth * len(units)
    pitch = depth + 8
    step = pl.program_id(0)

    def fetch(piece):
        return pltpu.make_async_copy(piece_refs[piece], held_ref.at[piece], sems.at[piece])

    @pl.when(step == 0)
    def fetch_all():
        for piece in range(pieces):
            fetch(piece).start()

    def inner_legs(piece):
        place, lane = piece // per_unit, piece % per_unit
        fetch(piece).wait()
        sender = (lax.axis_index("work") & (per_unit - 1)) ^ lane
        third = jnp.dot(
            held_ref[piece], leg3_ref[...], preferred_element_type=jnp.float32
        ).astype(jnp.bfloat16)
        for d in range(MOST):
            columns = third[:, d * extent : (d + 1) * extent]
            wide = jnp.concatenate(
                [columns[a * extent : (a + 1) * extent] for a in range(a_per)], axis=1
            )
            second = jnp.dot(
                leg2_ref[d * extent : (d + 1) * extent, :],
                wide,
                preferred_element_type=jnp.float32,
            )
            for a in range(a_per):
                row = place * unit_depth + d * UNIT_ROWS + sender * a_per + a
                turned_ref[pl.ds(row, extent, stride=pitch), :] = second[
                    :, a * extent : (a + 1) * extent
                ]

    @pl.when(step == 0)
    def turn_outer():
        for place, unit in enumerate(units):
            outer_ref[place * unit_depth : (place + 1) * unit_depth, :] = leg1_ref[
                unit
            ].astype(jnp.float32)
        across_ref[...] = outer_ref[...].T.astype(jnp.bfloat16)

    for piece in range(pieces):
        pl.when(step == piece)(functools.partial(inner_legs, piece))

    @pl.when(step >= pieces)
    def outer_leg():
        begin = (step - pieces) * B_BLOCK
        wide = jnp.concatenate(
            [
                turned_ref[pl.ds(pl.multiple_of((begin + b) * pitch, 8), depth), :].astype(
                    jnp.bfloat16
                )
                for b in range(B_BLOCK)
            ],
            axis=1,
        )
        whole = jnp.dot(across_ref[...], wide, preferred_element_type=jnp.float32)
        for b in range(B_BLOCK):
            part = whole[:, b * extent : (b + 1) * extent]
            if not first:
                part = part + acc_ref[b].astype(jnp.float32)
            if last:
                refs[6][pl.ds(b, extent, stride=B_BLOCK + 8), :] = part
            else:
                out_ref[b] = part.astype(out_ref.dtype)
        if last:
            for a in range(extent):
                out_ref[a] = refs[6][pl.ds(a * (B_BLOCK + 8), B_BLOCK), :].astype(jnp.bfloat16)


def add_group(units, pieces, leg3, leg2, leg1, acc, last):
    extent = leg3.shape[0]
    count = len(pieces)
    per_unit = count // len(units)
    depth = MOST * UNIT_ROWS * len(units)
    first = acc is None
    blocks = extent // B_BLOCK

    def whole_spec(x):
        return pl.BlockSpec(x.shape, lambda i: (0,) * x.ndim)

    def block_of(i):
        return jnp.maximum(i - count, 0)

    operands = [*pieces, leg3, leg2, leg1]
    in_specs = [pl.BlockSpec(memory_space=pl.ANY)] * count
    in_specs += [whole_spec(x) for x in operands[count:]]
    if not first:
        operands.append(acc)
        in_specs.append(pl.BlockSpec((B_BLOCK, extent, extent), lambda i: (block_of(i), 0, 0)))
    scratch = [
        pltpu.VMEM((extent * (depth + 8), extent), jnp.float32),
        pltpu.VMEM((depth, extent), jnp.float32),
        pltpu.VMEM((extent, depth), jnp.bfloat16),
        pltpu.VMEM((count, *pieces[0].shape), jnp.bfloat16),
        pltpu.SemaphoreType.DMA((count,)),
    ]
    if last:
        out_shape = jax.ShapeDtypeStruct((extent, extent, extent), jnp.bfloat16)
        out_spec = pl.BlockSpec((extent, B_BLOCK, extent), lambda i: (0, block_of(i), 0))
        scratch.append(pltpu.VMEM((extent * (B_BLOCK + 8), extent), jnp.float32))
    else:
        out_shape = jax.ShapeDtypeStruct((extent, extent, extent), ACC)
        out_spec = pl.BlockSpec((B_BLOCK, extent, extent), lambda i: (block_of(i), 0, 0))
    rows = count * pieces[0].shape[0]
    return pl.pallas_call(
        functools.partial(group_kernel, first, last, units, per_unit, extent),
        grid=(count + blocks,),
        in_specs=in_specs,
        out_specs=out_spec,
        out_shape=out_shape,
        scratch_shapes=scratch,
        compiler_params=pltpu.CompilerParams(
            dimension_semantics=("arbitrary",), vmem_limit_bytes=VMEM
        ),
        cost_estimate=pl.CostEstimate(
            flops=6 * MOST * rows * extent * extent,
            bytes_accessed=12 * extent**3,
            transcendentals=0,
        ),
    )(*operands)


def per_device(sources, perambs, source_ids, peramb_ids, sink_counts, weights):
    workers = lax.axis_size("work")
    extent = sources.shape[2]
    per_unit = UNIT_ROWS * workers // extent
    half = workers // 2
    far = list(range(half, workers))
    near = [s for pair in zip(range(half // 2), range(half // 2, half)) for s in pair][1:]
    near = [1, *(s for s in near if s != 1)]
    order = []
    while far or near:
        take_far = far and (not near or len(order) % IN_FLIGHT in FAR_TURNS)
        order.append(far.pop(0) if take_far else near.pop(0))
    early, late = tuple(order[:IN_FLIGHT]), (0, *order[IN_FLIGHT:])
    pieces = dict(zip(early, choose_pieces(sources, source_ids, early)))
    pieces.update(zip(late, choose_pieces(sources, source_ids, late)))
    arrived = {0: pieces[0]}

    def send(place):
        shift = order[place]
        piece = pieces[shift]
        if place >= IN_FLIGHT:
            before = order[place - IN_FLIGHT]
            piece, arrived[before] = lax.optimization_barrier((piece, arrived[before]))
        arrived[shift] = lax.ppermute(piece, "work", [(i, i ^ shift) for i in range(workers)])

    for place in range(IN_FLIGHT):
        send(place)
    matrices = choose_matrices(perambs, peramb_ids, sink_counts, workers, extent)
    matrices, arrived[order[0]] = lax.optimization_barrier((matrices, arrived[order[0]]))
    matrices = lax.all_to_all(matrices, "work", split_axis=0, concat_axis=0, tiled=True)
    leg3, leg2, leg1 = make_legs(matrices, sink_counts, weights, workers)
    for place in range(IN_FLIGHT, len(order)):
        send(place)

    acc = None
    for group, units in enumerate(GROUPS):
        members = [arrived[u * per_unit + lane] for u in units for lane in range(per_unit)]
        acc = add_group(units, members, leg3, leg2, leg1, acc, group == len(GROUPS) - 1)
    return acc.reshape(1, extent * extent, extent)


def solution(mesh):
    return jax.shard_map(
        per_device,
        mesh=mesh,
        in_specs=(P("cfg", "work", None), P("cfg", "work"), P(), P(), P(), P()),
        out_specs=P(("cfg", "work"), None, None),
        check_vma=False,
    )
```

```python
import functools

import jax
import jax.numpy as jnp
from jax import lax
from jax.experimental import pallas as pl
from jax.experimental.pallas import tpu as pltpu
from jax.sharding import PartitionSpec as P

MOST = 6
LEGS = 3
UNIT_ROWS = 16
B_BLOCK = 64
ACC = jnp.bfloat16
GROUPS = ((0, 1, 2, 3), (4, 5), (6,), (7,))
IN_FLIGHT = 5
FAR_TURNS = (2, 4)
VMEM = 36 * 1024 * 1024
SMALL_VMEM = 16 * 1024 * 1024


def pieces_kernel(shifts, ids_ref, source_ref, *refs):
    piece_refs, (held_ref, in_sems, out_sems) = refs[: len(shifts)], refs[len(shifts) :]
    own = lax.axis_index("work")
    reads, writes = [], []
    for i, shift in enumerate(shifts):
        reads.append(
            pltpu.make_async_copy(
                source_ref.at[ids_ref[own ^ shift]], held_ref.at[i], in_sems.at[i]
            )
        )
        writes.append(pltpu.make_async_copy(held_ref.at[i], piece_refs[i], out_sems.at[i]))
        reads[i].start()
    for read, write in zip(reads, writes):
        read.wait()
        write.start()
    for write in writes:
        write.wait()


def choose_pieces(sources, source_ids, shifts):
    return pl.pallas_call(
        functools.partial(pieces_kernel, shifts),
        in_specs=[pl.BlockSpec(memory_space=pltpu.SMEM), pl.BlockSpec(memory_space=pl.ANY)],
        out_specs=[pl.BlockSpec(memory_space=pl.ANY)] * len(shifts),
        out_shape=[jax.ShapeDtypeStruct(sources.shape[1:], sources.dtype)] * len(shifts),
        scratch_shapes=[
            pltpu.VMEM((len(shifts), *sources.shape[1:]), sources.dtype),
            pltpu.SemaphoreType.DMA((len(shifts),)),
            pltpu.SemaphoreType.DMA((len(shifts),)),
        ],
        compiler_params=pltpu.CompilerParams(vmem_limit_bytes=SMALL_VMEM),
    )(source_ids, sources)


def matrices_kernel(workers, counts_ref, matrix_ids_ref, peramb_ref, matrix_ref, choice_ref, spread_ref):
    rows = MOST * LEGS
    diagrams = matrix_ids_ref.shape[1]
    total = peramb_ref.shape[0]
    lanes = lax.broadcasted_iota(jnp.int32, (1, total), 1)

    def mark(sink, start):
        for slot in range(MOST):
            diagram = jnp.minimum(start + slot, diagrams - 1)
            for leg in range(LEGS):
                choice_ref[pl.ds(sink * rows + slot * LEGS + leg, 1), :] = jnp.where(
                    lanes == matrix_ids_ref[leg, diagram], 1.0, 0.0
                )
        return start + counts_ref[sink]

    lax.fori_loop(0, workers, mark, 0)
    chosen = jnp.dot(
        choice_ref[...].astype(jnp.bfloat16), peramb_ref[...], preferred_element_type=jnp.float32
    )
    extent = matrix_ref.shape[2]
    a_per = peramb_ref.shape[1] // extent
    for row in range(a_per):
        spread_ref[pl.ds(row, workers * rows, stride=a_per), :] = chosen[
            :, row * extent : (row + 1) * extent
        ]
    matrix_ref[...] = spread_ref[...].reshape(matrix_ref.shape).astype(jnp.bfloat16)


def choose_matrices(perambs, peramb_ids, sink_counts, workers, extent):
    rows = MOST * LEGS
    a_per = perambs.shape[1] // extent
    smem = pl.BlockSpec(memory_space=pltpu.SMEM)
    vmem = pl.BlockSpec(memory_space=pltpu.VMEM)
    return pl.pallas_call(
        functools.partial(matrices_kernel, workers),
        in_specs=[smem, smem, vmem],
        out_specs=vmem,
        out_shape=jax.ShapeDtypeStruct((workers, rows * a_per, extent), jnp.bfloat16),
        scratch_shapes=[
            pltpu.VMEM((workers * rows, perambs.shape[0]), jnp.float32),
            pltpu.VMEM((workers * rows * a_per, extent), jnp.float32),
        ],
        compiler_params=pltpu.CompilerParams(vmem_limit_bytes=SMALL_VMEM),
    )(sink_counts, peramb_ids.T, perambs)


def legs_kernel(
    workers, counts_ref, weights_ref, matrix_ref, leg3_ref, leg2_ref, leg1_ref, flat_ref, leg_ref
):
    extent = matrix_ref.shape[2]
    rows = MOST * LEGS
    a_per = matrix_ref.shape[1] // rows
    flat_ref[...] = matrix_ref[...].astype(jnp.float32).reshape(flat_ref.shape)
    own = lax.axis_index("work")
    start = lax.fori_loop(0, own, lambda i, total: total + counts_ref[i], 0)
    count = counts_ref[own]
    unit = UNIT_ROWS // a_per
    units = workers // unit
    for slot in range(MOST):
        for leg in range(LEGS):
            base = (slot * LEGS + leg) * a_per
            for row in range(a_per):
                leg_ref[pl.ds(row, workers, stride=a_per), :] = flat_ref[
                    pl.ds(base + row, workers, stride=rows * a_per), :
                ]
            if leg == 2:
                leg3_ref[:, slot * extent : (slot + 1) * extent] = leg_ref[...].T.astype(
                    jnp.bfloat16
                )
            elif leg == 1:
                leg2_ref[slot * extent : (slot + 1) * extent, :] = leg_ref[...].astype(
                    jnp.bfloat16
                )
            else:
                diagram = jnp.minimum(start + slot, weights_ref.shape[0] - 1)
                factor = jnp.where(slot < count, weights_ref[diagram], 0.0)
                leg_ref[...] = (factor * leg_ref[...]).T
                for block in range(units):
                    place = (own // unit) ^ block
                    leg1_ref[block, slot * UNIT_ROWS : (slot + 1) * UNIT_ROWS, :] = leg_ref[
                        pl.ds(pl.multiple_of(place * UNIT_ROWS, UNIT_ROWS), UNIT_ROWS), :
                    ].astype(jnp.bfloat16)


def make_legs(matrices, sink_counts, weights, workers):
    extent = matrices.shape[2]
    a_per = extent // workers
    smem = pl.BlockSpec(memory_space=pltpu.SMEM)
    vmem = pl.BlockSpec(memory_space=pltpu.VMEM)
    return pl.pallas_call(
        functools.partial(legs_kernel, workers),
        in_specs=[smem, smem, vmem],
        out_specs=[vmem] * 3,
        out_shape=[
            jax.ShapeDtypeStruct((extent, MOST * extent), jnp.bfloat16),
            jax.ShapeDtypeStruct((MOST * extent, extent), jnp.bfloat16),
            jax.ShapeDtypeStruct(
                (extent // UNIT_ROWS, MOST * UNIT_ROWS, extent), jnp.bfloat16
            ),
        ],
        scratch_shapes=[
            pltpu.VMEM((matrices.shape[0] * matrices.shape[1], extent), jnp.float32),
            pltpu.VMEM((extent, extent), jnp.float32),
        ],
        compiler_params=pltpu.CompilerParams(vmem_limit_bytes=SMALL_VMEM),
    )(sink_counts, weights, matrices)


def group_kernel(first, last, units, per_unit, extent, *refs):
    pieces = len(units) * per_unit
    piece_refs = refs[:pieces]
    leg3_ref, leg2_ref, leg1_ref = refs[pieces : pieces + 3]
    refs = refs[pieces + 3 :]
    if not first:
        acc_ref, refs = refs[0], refs[1:]
    out_ref, turned_ref, outer_ref, across_ref, held_ref, sems = refs[:6]
    a_per = piece_refs[0].shape[0] // extent
    unit_depth = MOST * UNIT_ROWS
    depth = unit_depth * len(units)
    pitch = depth + 8
    step = pl.program_id(0)

    def fetch(piece):
        return pltpu.make_async_copy(piece_refs[piece], held_ref.at[piece], sems.at[piece])

    @pl.when(step == 0)
    def fetch_all():
        for piece in range(pieces):
            fetch(piece).start()

    def inner_legs(piece):
        place, lane = piece // per_unit, piece % per_unit
        fetch(piece).wait()
        sender = (lax.axis_index("work") & (per_unit - 1)) ^ lane
        third = jnp.dot(
            held_ref[piece], leg3_ref[...], preferred_element_type=jnp.float32
        ).astype(jnp.bfloat16)
        for d in range(MOST):
            columns = third[:, d * extent : (d + 1) * extent]
            wide = jnp.concatenate(
                [columns[a * extent : (a + 1) * extent] for a in range(a_per)], axis=1
            )
            second = jnp.dot(
                leg2_ref[d * extent : (d + 1) * extent, :],
                wide,
                preferred_element_type=jnp.float32,
            )
            for a in range(a_per):
                row = place * unit_depth + d * UNIT_ROWS + sender * a_per + a
                turned_ref[pl.ds(row, extent, stride=pitch), :] = second[
                    :, a * extent : (a + 1) * extent
                ]

    @pl.when(step == 0)
    def turn_outer():
        for place, unit in enumerate(units):
            outer_ref[place * unit_depth : (place + 1) * unit_depth, :] = leg1_ref[
                unit
            ].astype(jnp.float32)
        across_ref[...] = outer_ref[...].T.astype(jnp.bfloat16)

    for piece in range(pieces):
        pl.when(step == piece)(functools.partial(inner_legs, piece))

    @pl.when(step >= pieces)
    def outer_leg():
        begin = (step - pieces) * B_BLOCK
        wide = jnp.concatenate(
            [
                turned_ref[pl.ds(pl.multiple_of((begin + b) * pitch, 8), depth), :].astype(
                    jnp.bfloat16
                )
                for b in range(B_BLOCK)
            ],
            axis=1,
        )
        whole = jnp.dot(across_ref[...], wide, preferred_element_type=jnp.float32)
        for b in range(B_BLOCK):
            part = whole[:, b * extent : (b + 1) * extent]
            if not first:
                part = part + acc_ref[b].astype(jnp.float32)
            if last:
                refs[6][pl.ds(b, extent, stride=B_BLOCK + 8), :] = part
            else:
                out_ref[b] = part.astype(out_ref.dtype)
        if last:
            for a in range(extent):
                out_ref[a] = refs[6][pl.ds(a * (B_BLOCK + 8), B_BLOCK), :].astype(jnp.bfloat16)


def add_group(units, pieces, leg3, leg2, leg1, acc, last):
    extent = leg3.shape[0]
    count = len(pieces)
    per_unit = count // len(units)
    depth = MOST * UNIT_ROWS * len(units)
    first = acc is None
    blocks = extent // B_BLOCK

    def whole_spec(x):
        return pl.BlockSpec(x.shape, lambda i: (0,) * x.ndim)

    def block_of(i):
        return jnp.maximum(i - count, 0)

    operands = [*pieces, leg3, leg2, leg1]
    in_specs = [pl.BlockSpec(memory_space=pl.ANY)] * count
    in_specs += [whole_spec(x) for x in operands[count:]]
    if not first:
        operands.append(acc)
        in_specs.append(pl.BlockSpec((B_BLOCK, extent, extent), lambda i: (block_of(i), 0, 0)))
    scratch = [
        pltpu.VMEM((extent * (depth + 8), extent), jnp.float32),
        pltpu.VMEM((depth, extent), jnp.float32),
        pltpu.VMEM((extent, depth), jnp.bfloat16),
        pltpu.VMEM((count, *pieces[0].shape), jnp.bfloat16),
        pltpu.SemaphoreType.DMA((count,)),
    ]
    if last:
        out_shape = jax.ShapeDtypeStruct((extent, extent, extent), jnp.bfloat16)
        out_spec = pl.BlockSpec((extent, B_BLOCK, extent), lambda i: (0, block_of(i), 0))
        scratch.append(pltpu.VMEM((extent * (B_BLOCK + 8), extent), jnp.float32))
    else:
        out_shape = jax.ShapeDtypeStruct((extent, extent, extent), ACC)
        out_spec = pl.BlockSpec((B_BLOCK, extent, extent), lambda i: (block_of(i), 0, 0))
    rows = count * pieces[0].shape[0]
    return pl.pallas_call(
        functools.partial(group_kernel, first, last, units, per_unit, extent),
        grid=(count + blocks,),
        in_specs=in_specs,
        out_specs=out_spec,
        out_shape=out_shape,
        scratch_shapes=scratch,
        compiler_params=pltpu.CompilerParams(
            dimension_semantics=("arbitrary",), vmem_limit_bytes=VMEM
        ),
        cost_estimate=pl.CostEstimate(
            flops=6 * MOST * rows * extent * extent,
            bytes_accessed=12 * extent**3,
            transcendentals=0,
        ),
    )(*operands)


def per_device(sources, perambs, source_ids, peramb_ids, sink_counts, weights):
    workers = lax.axis_size("work")
    extent = sources.shape[2]
    per_unit = UNIT_ROWS * workers // extent
    half = workers // 2
    far = list(range(half, workers))
    near = [s for pair in zip(range(half // 2), range(half // 2, half)) for s in pair][1:]
    near = [1, *(s for s in near if s != 1)]
    order = []
    while far or near:
        take_far = far and (not near or len(order) % IN_FLIGHT in FAR_TURNS)
        order.append(far.pop(0) if take_far else near.pop(0))
    early, late = tuple(order[:IN_FLIGHT]), (0, *order[IN_FLIGHT:])
    pieces = dict(zip(early, choose_pieces(sources, source_ids, early)))
    pieces.update(zip(late, choose_pieces(sources, source_ids, late)))
    arrived = {0: pieces[0]}

    def send(place):
        shift = order[place]
        piece = pieces[shift]
        if place >= IN_FLIGHT:
            before = order[place - IN_FLIGHT]
            piece, arrived[before] = lax.optimization_barrier((piece, arrived[before]))
        arrived[shift] = lax.ppermute(piece, "work", [(i, i ^ shift) for i in range(workers)])

    for place in range(IN_FLIGHT):
        send(place)
    matrices = choose_matrices(perambs, peramb_ids, sink_counts, workers, extent)
    matrices = lax.all_to_all(matrices, "work", split_axis=0, concat_axis=0, tiled=True)
    leg3, leg2, leg1 = make_legs(matrices, sink_counts, weights, workers)
    for place in range(IN_FLIGHT, len(order)):
        send(place)

    acc = None
    for group, units in enumerate(GROUPS):
        members = [arrived[u * per_unit + lane] for u in units for lane in range(per_unit)]
        acc = add_group(units, members, leg3, leg2, leg1, acc, group == len(GROUPS) - 1)
    return acc.reshape(1, extent * extent, extent)


def solution(mesh):
    return jax.shard_map(
        per_device,
        mesh=mesh,
        in_specs=(P("cfg", "work", None), P("cfg", "work"), P(), P(), P(), P()),
        out_specs=P(("cfg", "work"), None, None),
        check_vma=False,
    )
```

```python
import functools

import jax
import jax.numpy as jnp
from jax import lax
from jax.experimental import pallas as pl
from jax.experimental.pallas import tpu as pltpu
from jax.sharding import PartitionSpec as P

MOST = 6
LEGS = 3
UNIT_ROWS = 16
B_BLOCK = 64
ACC = jnp.bfloat16
GROUPS = ((0, 1, 2, 3), (4, 5), (6,), (7,))
IN_FLIGHT = 6
FAR_TURNS = (2, 4)
HELD_BACK = 3
SMALL_VMEM = 16 * 1024 * 1024


def pieces_kernel(shifts, ids_ref, source_ref, *refs):
    piece_refs, (held_ref, in_sems, out_sems) = refs[: len(shifts)], refs[len(shifts) :]
    own = lax.axis_index("work")
    reads, writes = [], []
    for i, shift in enumerate(shifts):
        reads.append(
            pltpu.make_async_copy(
                source_ref.at[ids_ref[own ^ shift]], held_ref.at[i], in_sems.at[i]
            )
        )
        writes.append(pltpu.make_async_copy(held_ref.at[i], piece_refs[i], out_sems.at[i]))
        reads[i].start()
    for read, write in zip(reads, writes):
        read.wait()
        write.start()
    for write in writes:
        write.wait()


def choose_pieces(sources, source_ids, shifts):
    return pl.pallas_call(
        functools.partial(pieces_kernel, shifts),
        in_specs=[pl.BlockSpec(memory_space=pltpu.SMEM), pl.BlockSpec(memory_space=pl.ANY)],
        out_specs=[pl.BlockSpec(memory_space=pl.ANY)] * len(shifts),
        out_shape=[jax.ShapeDtypeStruct(sources.shape[1:], sources.dtype)] * len(shifts),
        scratch_shapes=[
            pltpu.VMEM((len(shifts), *sources.shape[1:]), sources.dtype),
            pltpu.SemaphoreType.DMA((len(shifts),)),
            pltpu.SemaphoreType.DMA((len(shifts),)),
        ],
        compiler_params=pltpu.CompilerParams(vmem_limit_bytes=SMALL_VMEM),
    )(source_ids, sources)


def matrices_kernel(workers, counts_ref, matrix_ids_ref, peramb_ref, matrix_ref, choice_ref, spread_ref):
    rows = MOST * LEGS
    diagrams = matrix_ids_ref.shape[1]
    total = peramb_ref.shape[0]
    lanes = lax.broadcasted_iota(jnp.int32, (1, total), 1)

    def mark(sink, start):
        for slot in range(MOST):
            diagram = jnp.minimum(start + slot, diagrams - 1)
            for leg in range(LEGS):
                choice_ref[pl.ds(sink * rows + slot * LEGS + leg, 1), :] = jnp.where(
                    lanes == matrix_ids_ref[leg, diagram], 1.0, 0.0
                )
        return start + counts_ref[sink]

    lax.fori_loop(0, workers, mark, 0)
    chosen = jnp.dot(
        choice_ref[...].astype(jnp.bfloat16), peramb_ref[...], preferred_element_type=jnp.float32
    )
    extent = matrix_ref.shape[2]
    a_per = peramb_ref.shape[1] // extent
    for row in range(a_per):
        spread_ref[pl.ds(row, workers * rows, stride=a_per), :] = chosen[
            :, row * extent : (row + 1) * extent
        ]
    matrix_ref[...] = spread_ref[...].reshape(matrix_ref.shape).astype(jnp.bfloat16)


def choose_matrices(perambs, peramb_ids, sink_counts, workers, extent):
    rows = MOST * LEGS
    a_per = perambs.shape[1] // extent
    smem = pl.BlockSpec(memory_space=pltpu.SMEM)
    vmem = pl.BlockSpec(memory_space=pltpu.VMEM)
    return pl.pallas_call(
        functools.partial(matrices_kernel, workers),
        in_specs=[smem, smem, vmem],
        out_specs=vmem,
        out_shape=jax.ShapeDtypeStruct((workers, rows * a_per, extent), jnp.bfloat16),
        scratch_shapes=[
            pltpu.VMEM((workers * rows, perambs.shape[0]), jnp.float32),
            pltpu.VMEM((workers * rows * a_per, extent), jnp.float32),
        ],
        compiler_params=pltpu.CompilerParams(vmem_limit_bytes=SMALL_VMEM),
    )(sink_counts, peramb_ids.T, perambs)


def legs_kernel(
    workers, counts_ref, weights_ref, matrix_ref, leg3_ref, leg2_ref, leg1_ref, flat_ref, leg_ref
):
    extent = matrix_ref.shape[2]
    rows = MOST * LEGS
    a_per = matrix_ref.shape[1] // rows
    flat_ref[...] = matrix_ref[...].astype(jnp.float32).reshape(flat_ref.shape)
    own = lax.axis_index("work")
    start = lax.fori_loop(0, own, lambda i, total: total + counts_ref[i], 0)
    count = counts_ref[own]
    unit = UNIT_ROWS // a_per
    units = workers // unit
    for slot in range(MOST):
        for leg in range(LEGS):
            base = (slot * LEGS + leg) * a_per
            for row in range(a_per):
                leg_ref[pl.ds(row, workers, stride=a_per), :] = flat_ref[
                    pl.ds(base + row, workers, stride=rows * a_per), :
                ]
            if leg == 2:
                leg3_ref[:, slot * extent : (slot + 1) * extent] = leg_ref[...].T.astype(
                    jnp.bfloat16
                )
            elif leg == 1:
                leg2_ref[slot * extent : (slot + 1) * extent, :] = leg_ref[...].astype(
                    jnp.bfloat16
                )
            else:
                diagram = jnp.minimum(start + slot, weights_ref.shape[0] - 1)
                factor = jnp.where(slot < count, weights_ref[diagram], 0.0)
                leg_ref[...] = (factor * leg_ref[...]).T
                for block in range(units):
                    place = (own // unit) ^ block
                    leg1_ref[block, slot * UNIT_ROWS : (slot + 1) * UNIT_ROWS, :] = leg_ref[
                        pl.ds(pl.multiple_of(place * UNIT_ROWS, UNIT_ROWS), UNIT_ROWS), :
                    ].astype(jnp.bfloat16)


def make_legs(matrices, sink_counts, weights, workers):
    extent = matrices.shape[2]
    a_per = extent // workers
    smem = pl.BlockSpec(memory_space=pltpu.SMEM)
    vmem = pl.BlockSpec(memory_space=pltpu.VMEM)
    return pl.pallas_call(
        functools.partial(legs_kernel, workers),
        in_specs=[smem, smem, vmem],
        out_specs=[vmem] * 3,
        out_shape=[
            jax.ShapeDtypeStruct((extent, MOST * extent), jnp.bfloat16),
            jax.ShapeDtypeStruct((MOST * extent, extent), jnp.bfloat16),
            jax.ShapeDtypeStruct(
                (extent // UNIT_ROWS, MOST * UNIT_ROWS, extent), jnp.bfloat16
            ),
        ],
        scratch_shapes=[
            pltpu.VMEM((matrices.shape[0] * matrices.shape[1], extent), jnp.float32),
            pltpu.VMEM((extent, extent), jnp.float32),
        ],
        compiler_params=pltpu.CompilerParams(vmem_limit_bytes=SMALL_VMEM),
    )(sink_counts, weights, matrices)


def group_kernel(first, last, units, per_unit, extent, *refs):
    pieces = len(units) * per_unit
    piece_refs = refs[:pieces]
    leg3_ref, leg2_ref, leg1_ref = refs[pieces : pieces + 3]
    refs = refs[pieces + 3 :]
    if not first:
        acc_ref, refs = refs[0], refs[1:]
    out_ref, turned_ref, outer_ref, across_ref, held_ref, sems = refs[:6]
    a_per = piece_refs[0].shape[0] // extent
    unit_depth = MOST * UNIT_ROWS
    depth = unit_depth * len(units)
    pitch = depth + 8
    step = pl.program_id(0)

    def fetch(piece):
        return pltpu.make_async_copy(piece_refs[piece], held_ref.at[piece], sems.at[piece])

    @pl.when(step == 0)
    def fetch_all():
        for piece in range(pieces):
            fetch(piece).start()

    def inner_legs(piece):
        place, lane = piece // per_unit, piece % per_unit
        fetch(piece).wait()
        sender = (lax.axis_index("work") & (per_unit - 1)) ^ lane
        third = jnp.dot(
            held_ref[piece], leg3_ref[...], preferred_element_type=jnp.float32
        ).astype(jnp.bfloat16)
        for d in range(MOST):
            columns = third[:, d * extent : (d + 1) * extent]
            wide = jnp.concatenate(
                [columns[a * extent : (a + 1) * extent] for a in range(a_per)], axis=1
            )
            second = jnp.dot(
                leg2_ref[d * extent : (d + 1) * extent, :],
                wide,
                preferred_element_type=jnp.float32,
            )
            for a in range(a_per):
                row = place * unit_depth + d * UNIT_ROWS + sender * a_per + a
                turned_ref[pl.ds(row, extent, stride=pitch), :] = second[
                    :, a * extent : (a + 1) * extent
                ]

    @pl.when(step == 0)
    def turn_outer():
        for place, unit in enumerate(units):
            outer_ref[place * unit_depth : (place + 1) * unit_depth, :] = leg1_ref[
                unit
            ].astype(jnp.float32)
        across_ref[...] = outer_ref[...].T.astype(jnp.bfloat16)

    for piece in range(pieces):
        pl.when(step == piece)(functools.partial(inner_legs, piece))

    @pl.when(step >= pieces)
    def outer_leg():
        begin = (step - pieces) * B_BLOCK
        wide = jnp.concatenate(
            [
                turned_ref[pl.ds(pl.multiple_of((begin + b) * pitch, 8), depth), :].astype(
                    jnp.bfloat16
                )
                for b in range(B_BLOCK)
            ],
            axis=1,
        )
        whole = jnp.dot(across_ref[...], wide, preferred_element_type=jnp.float32)
        for b in range(B_BLOCK):
            part = whole[:, b * extent : (b + 1) * extent]
            if not first:
                part = part + acc_ref[b].astype(jnp.float32)
            if last:
                refs[6][pl.ds(b, extent, stride=B_BLOCK + 8), :] = part
            else:
                out_ref[b] = part.astype(out_ref.dtype)
        if last:
            for a in range(extent):
                out_ref[a] = refs[6][pl.ds(a * (B_BLOCK + 8), B_BLOCK), :].astype(jnp.bfloat16)


def add_group(units, pieces, leg3, leg2, leg1, acc, last):
    extent = leg3.shape[0]
    count = len(pieces)
    per_unit = count // len(units)
    depth = MOST * UNIT_ROWS * len(units)
    first = acc is None
    blocks = extent // B_BLOCK

    def whole_spec(x):
        return pl.BlockSpec(x.shape, lambda i: (0,) * x.ndim)

    def block_of(i):
        return jnp.maximum(i - count, 0)

    operands = [*pieces, leg3, leg2, leg1]
    in_specs = [pl.BlockSpec(memory_space=pl.ANY)] * count
    in_specs += [whole_spec(x) for x in operands[count:]]
    if not first:
        operands.append(acc)
        in_specs.append(pl.BlockSpec((B_BLOCK, extent, extent), lambda i: (block_of(i), 0, 0)))
    scratch = [
        pltpu.VMEM((extent * (depth + 8), extent), jnp.float32),
        pltpu.VMEM((depth, extent), jnp.float32),
        pltpu.VMEM((extent, depth), jnp.bfloat16),
        pltpu.VMEM((count, *pieces[0].shape), jnp.bfloat16),
        pltpu.SemaphoreType.DMA((count,)),
    ]
    if last:
        out_shape = jax.ShapeDtypeStruct((extent, extent, extent), jnp.bfloat16)
        out_spec = pl.BlockSpec((extent, B_BLOCK, extent), lambda i: (0, block_of(i), 0))
        scratch.append(pltpu.VMEM((extent * (B_BLOCK + 8), extent), jnp.float32))
    else:
        out_shape = jax.ShapeDtypeStruct((extent, extent, extent), ACC)
        out_spec = pl.BlockSpec((B_BLOCK, extent, extent), lambda i: (block_of(i), 0, 0))
    rows = count * pieces[0].shape[0]
    return pl.pallas_call(
        functools.partial(group_kernel, first, last, units, per_unit, extent),
        grid=(count + blocks,),
        in_specs=in_specs,
        out_specs=out_spec,
        out_shape=out_shape,
        scratch_shapes=scratch,
        compiler_params=pltpu.CompilerParams(
            dimension_semantics=("arbitrary",), vmem_limit_bytes=SMALL_VMEM + 4 * extent * extent * (depth + 8)
        ),
        cost_estimate=pl.CostEstimate(
            flops=6 * MOST * rows * extent * extent,
            bytes_accessed=12 * extent**3,
            transcendentals=0,
        ),
    )(*operands)


def per_device(sources, perambs, source_ids, peramb_ids, sink_counts, weights):
    workers = lax.axis_size("work")
    extent = sources.shape[2]
    per_unit = UNIT_ROWS * workers // extent
    half = workers // 2
    far = list(range(half, workers))
    upper, lower = list(range(half // 2, half)), list(range(2, half // 2))
    near = [1, *upper[:-1], *lower, upper[-1]]
    order = []
    while far or near:
        take_far = far and (not near or len(order) % IN_FLIGHT in FAR_TURNS)
        order.append(far.pop(0) if take_far else near.pop(0))
    early, late = tuple(order[:IN_FLIGHT]), (0, *order[IN_FLIGHT:])
    pieces = dict(zip(early, choose_pieces(sources, source_ids, early)))
    pieces.update(zip(late, choose_pieces(sources, source_ids, late)))
    arrived = {0: pieces[0]}

    def send(place):
        shift = order[place]
        piece = pieces[shift]
        if place >= IN_FLIGHT:
            before = order[place - IN_FLIGHT]
            piece, arrived[before] = lax.optimization_barrier((piece, arrived[before]))
        arrived[shift] = lax.ppermute(piece, "work", [(i, i ^ shift) for i in range(workers)])

    for place in range(IN_FLIGHT):
        send(place)
    matrices = choose_matrices(perambs, peramb_ids, sink_counts, workers, extent)
    matrices = lax.all_to_all(matrices, "work", split_axis=0, concat_axis=0, tiled=True)
    leg3, leg2, leg1 = make_legs(matrices, sink_counts, weights, workers)
    for place in range(IN_FLIGHT, len(order) - HELD_BACK):
        send(place)

    acc = None
    for group, units in enumerate(GROUPS):
        members = [arrived[u * per_unit + lane] for u in units for lane in range(per_unit)]
        acc = add_group(units, members, leg3, leg2, leg1, acc, group == len(GROUPS) - 1)
        if group == 0:
            for place in range(len(order) - HELD_BACK, len(order)):
                shift = order[place]
                pieces[shift], acc = lax.optimization_barrier((pieces[shift], acc))
                send(place)
    return acc.reshape(1, extent * extent, extent)


def solution(mesh):
    return jax.shard_map(
        per_device,
        mesh=mesh,
        in_specs=(P("cfg", "work", None), P("cfg", "work"), P(), P(), P(), P()),
        out_specs=P(("cfg", "work"), None, None),
        check_vma=False,
    )
```

```python
import functools

import jax
import jax.numpy as jnp
from jax import lax
from jax.experimental import pallas as pl
from jax.experimental.pallas import tpu as pltpu
from jax.sharding import PartitionSpec as P

MOST = 6
LEGS = 3
UNIT_ROWS = 16
B_BLOCK = 64
ACC = jnp.bfloat16
GROUPS = ((0, 2, 4), (3, 5), (1, 6), (7,))
IN_FLIGHT = 5
FAR_TURNS = (2, 4, 6, 8)
HELD_BACK = 5
SMALL_VMEM = 16 * 1024 * 1024
ROOM = 13 * 1024 * 1024


def pieces_kernel(shifts, ids_ref, source_ref, *refs):
    piece_refs, (held_ref, in_sems, out_sems) = refs[: len(shifts)], refs[len(shifts) :]
    own = lax.axis_index("work")
    reads, writes = [], []
    for i, shift in enumerate(shifts):
        reads.append(
            pltpu.make_async_copy(
                source_ref.at[ids_ref[own ^ shift]], held_ref.at[i], in_sems.at[i]
            )
        )
        writes.append(pltpu.make_async_copy(held_ref.at[i], piece_refs[i], out_sems.at[i]))
        reads[i].start()
    for read, write in zip(reads, writes):
        read.wait()
        write.start()
    for write in writes:
        write.wait()


def choose_pieces(sources, source_ids, shifts):
    return pl.pallas_call(
        functools.partial(pieces_kernel, shifts),
        in_specs=[pl.BlockSpec(memory_space=pltpu.SMEM), pl.BlockSpec(memory_space=pl.ANY)],
        out_specs=[pl.BlockSpec(memory_space=pl.ANY)] * len(shifts),
        out_shape=[jax.ShapeDtypeStruct(sources.shape[1:], sources.dtype)] * len(shifts),
        scratch_shapes=[
            pltpu.VMEM((len(shifts), *sources.shape[1:]), sources.dtype),
            pltpu.SemaphoreType.DMA((len(shifts),)),
            pltpu.SemaphoreType.DMA((len(shifts),)),
        ],
        compiler_params=pltpu.CompilerParams(vmem_limit_bytes=SMALL_VMEM),
    )(source_ids, sources)


def matrices_kernel(workers, counts_ref, matrix_ids_ref, peramb_ref, matrix_ref, choice_ref, spread_ref):
    rows = MOST * LEGS
    diagrams = matrix_ids_ref.shape[1]
    total = peramb_ref.shape[0]
    lanes = lax.broadcasted_iota(jnp.int32, (1, total), 1)

    def mark(sink, start):
        for slot in range(MOST):
            diagram = jnp.minimum(start + slot, diagrams - 1)
            for leg in range(LEGS):
                choice_ref[pl.ds(sink * rows + slot * LEGS + leg, 1), :] = jnp.where(
                    lanes == matrix_ids_ref[leg, diagram], 1.0, 0.0
                )
        return start + counts_ref[sink]

    lax.fori_loop(0, workers, mark, 0)
    chosen = jnp.dot(
        choice_ref[...].astype(jnp.bfloat16), peramb_ref[...], preferred_element_type=jnp.float32
    )
    extent = matrix_ref.shape[2]
    a_per = peramb_ref.shape[1] // extent
    for row in range(a_per):
        spread_ref[pl.ds(row, workers * rows, stride=a_per), :] = chosen[
            :, row * extent : (row + 1) * extent
        ]
    matrix_ref[...] = spread_ref[...].reshape(matrix_ref.shape).astype(jnp.bfloat16)


def choose_matrices(perambs, peramb_ids, sink_counts, workers, extent):
    rows = MOST * LEGS
    a_per = perambs.shape[1] // extent
    smem = pl.BlockSpec(memory_space=pltpu.SMEM)
    vmem = pl.BlockSpec(memory_space=pltpu.VMEM)
    return pl.pallas_call(
        functools.partial(matrices_kernel, workers),
        in_specs=[smem, smem, vmem],
        out_specs=vmem,
        out_shape=jax.ShapeDtypeStruct((workers, rows * a_per, extent), jnp.bfloat16),
        scratch_shapes=[
            pltpu.VMEM((workers * rows, perambs.shape[0]), jnp.float32),
            pltpu.VMEM((workers * rows * a_per, extent), jnp.float32),
        ],
        compiler_params=pltpu.CompilerParams(vmem_limit_bytes=SMALL_VMEM),
    )(sink_counts, peramb_ids.T, perambs)


def legs_kernel(
    workers, counts_ref, weights_ref, matrix_ref, leg3_ref, leg2_ref, leg1_ref, flat_ref, leg_ref
):
    extent = matrix_ref.shape[2]
    rows = MOST * LEGS
    a_per = matrix_ref.shape[1] // rows
    flat_ref[...] = matrix_ref[...].astype(jnp.float32).reshape(flat_ref.shape)
    own = lax.axis_index("work")
    start = lax.fori_loop(0, own, lambda i, total: total + counts_ref[i], 0)
    count = counts_ref[own]
    unit = UNIT_ROWS // a_per
    units = workers // unit
    for slot in range(MOST):
        for leg in range(LEGS):
            base = (slot * LEGS + leg) * a_per
            for row in range(a_per):
                leg_ref[pl.ds(row, workers, stride=a_per), :] = flat_ref[
                    pl.ds(base + row, workers, stride=rows * a_per), :
                ]
            if leg == 2:
                leg3_ref[:, slot * extent : (slot + 1) * extent] = leg_ref[...].T.astype(
                    jnp.bfloat16
                )
            elif leg == 1:
                leg2_ref[slot * extent : (slot + 1) * extent, :] = leg_ref[...].astype(
                    jnp.bfloat16
                )
            else:
                diagram = jnp.minimum(start + slot, weights_ref.shape[0] - 1)
                factor = jnp.where(slot < count, weights_ref[diagram], 0.0)
                leg_ref[...] = (factor * leg_ref[...]).T
                for block in range(units):
                    place = (own // unit) ^ block
                    leg1_ref[block, slot * UNIT_ROWS : (slot + 1) * UNIT_ROWS, :] = leg_ref[
                        pl.ds(pl.multiple_of(place * UNIT_ROWS, UNIT_ROWS), UNIT_ROWS), :
                    ].astype(jnp.bfloat16)


def make_legs(matrices, sink_counts, weights, workers):
    extent = matrices.shape[2]
    a_per = extent // workers
    smem = pl.BlockSpec(memory_space=pltpu.SMEM)
    vmem = pl.BlockSpec(memory_space=pltpu.VMEM)
    return pl.pallas_call(
        functools.partial(legs_kernel, workers),
        in_specs=[smem, smem, vmem],
        out_specs=[vmem] * 3,
        out_shape=[
            jax.ShapeDtypeStruct((extent, MOST * extent), jnp.bfloat16),
            jax.ShapeDtypeStruct((MOST * extent, extent), jnp.bfloat16),
            jax.ShapeDtypeStruct(
                (extent // UNIT_ROWS, MOST * UNIT_ROWS, extent), jnp.bfloat16
            ),
        ],
        scratch_shapes=[
            pltpu.VMEM((matrices.shape[0] * matrices.shape[1], extent), jnp.float32),
            pltpu.VMEM((extent, extent), jnp.float32),
        ],
        compiler_params=pltpu.CompilerParams(vmem_limit_bytes=SMALL_VMEM),
    )(sink_counts, weights, matrices)


def group_kernel(first, last, units, per_unit, extent, *refs):
    pieces = len(units) * per_unit
    piece_refs = refs[:pieces]
    leg3_ref, leg2_ref, leg1_ref = refs[pieces : pieces + 3]
    refs = refs[pieces + 3 :]
    if not first:
        acc_ref, refs = refs[0], refs[1:]
    out_ref, turned_ref, outer_ref, across_ref, held_ref, sems = refs[:6]
    a_per = piece_refs[0].shape[0] // extent
    unit_depth = MOST * UNIT_ROWS
    depth = unit_depth * len(units)
    pitch = depth + 8
    step = pl.program_id(0)

    def fetch(piece):
        return pltpu.make_async_copy(piece_refs[piece], held_ref.at[piece], sems.at[piece])

    @pl.when(step == 0)
    def fetch_all():
        for piece in range(pieces):
            fetch(piece).start()

    def inner_legs(piece):
        place, lane = piece // per_unit, piece % per_unit
        fetch(piece).wait()
        sender = (lax.axis_index("work") & (per_unit - 1)) ^ lane
        third = jnp.dot(
            held_ref[piece], leg3_ref[...], preferred_element_type=jnp.float32
        ).astype(jnp.bfloat16)
        for d in range(MOST):
            columns = third[:, d * extent : (d + 1) * extent]
            wide = jnp.concatenate(
                [columns[a * extent : (a + 1) * extent] for a in range(a_per)], axis=1
            )
            second = jnp.dot(
                leg2_ref[d * extent : (d + 1) * extent, :],
                wide,
                preferred_element_type=jnp.float32,
            )
            for a in range(a_per):
                row = place * unit_depth + d * UNIT_ROWS + sender * a_per + a
                turned_ref[pl.ds(row, extent, stride=pitch), :] = second[
                    :, a * extent : (a + 1) * extent
                ]

    @pl.when(step == 0)
    def turn_outer():
        for place, unit in enumerate(units):
            outer_ref[place * unit_depth : (place + 1) * unit_depth, :] = leg1_ref[
                unit
            ].astype(jnp.float32)
        across_ref[...] = outer_ref[...].T.astype(jnp.bfloat16)

    for piece in range(pieces):
        pl.when(step == piece)(functools.partial(inner_legs, piece))

    @pl.when(step >= pieces)
    def outer_leg():
        begin = (step - pieces) * B_BLOCK
        wide = jnp.concatenate(
            [
                turned_ref[pl.ds(pl.multiple_of((begin + b) * pitch, 8), depth), :].astype(
                    jnp.bfloat16
                )
                for b in range(B_BLOCK)
            ],
            axis=1,
        )
        whole = jnp.dot(across_ref[...], wide, preferred_element_type=jnp.float32)
        for b in range(B_BLOCK):
            part = whole[:, b * extent : (b + 1) * extent]
            if not first:
                part = part + acc_ref[b].astype(jnp.float32)
            if last:
                refs[6][pl.ds(b, extent, stride=B_BLOCK + 8), :] = part
            else:
                out_ref[b] = part.astype(out_ref.dtype)
        if last:
            for a in range(extent):
                out_ref[a] = refs[6][pl.ds(a * (B_BLOCK + 8), B_BLOCK), :].astype(jnp.bfloat16)


def add_group(units, pieces, leg3, leg2, leg1, acc, last):
    extent = leg3.shape[0]
    count = len(pieces)
    per_unit = count // len(units)
    depth = MOST * UNIT_ROWS * len(units)
    first = acc is None
    blocks = extent // B_BLOCK

    def whole_spec(x):
        return pl.BlockSpec(x.shape, lambda i: (0,) * x.ndim)

    def block_of(i):
        return jnp.maximum(i - count, 0)

    operands = [*pieces, leg3, leg2, leg1]
    in_specs = [pl.BlockSpec(memory_space=pl.ANY)] * count
    in_specs += [whole_spec(x) for x in operands[count:]]
    if not first:
        operands.append(acc)
        in_specs.append(pl.BlockSpec((B_BLOCK, extent, extent), lambda i: (block_of(i), 0, 0)))
    scratch = [
        pltpu.VMEM((extent * (depth + 8), extent), jnp.float32),
        pltpu.VMEM((depth, extent), jnp.float32),
        pltpu.VMEM((extent, depth), jnp.bfloat16),
        pltpu.VMEM((count, *pieces[0].shape), jnp.bfloat16),
        pltpu.SemaphoreType.DMA((count,)),
    ]
    if last:
        out_shape = jax.ShapeDtypeStruct((extent, extent, extent), jnp.bfloat16)
        out_spec = pl.BlockSpec((extent, B_BLOCK, extent), lambda i: (0, block_of(i), 0))
        scratch.append(pltpu.VMEM((extent * (B_BLOCK + 8), extent), jnp.float32))
    else:
        out_shape = jax.ShapeDtypeStruct((extent, extent, extent), ACC)
        out_spec = pl.BlockSpec((B_BLOCK, extent, extent), lambda i: (block_of(i), 0, 0))
    rows = count * pieces[0].shape[0]
    return pl.pallas_call(
        functools.partial(group_kernel, first, last, units, per_unit, extent),
        grid=(count + blocks,),
        in_specs=in_specs,
        out_specs=out_spec,
        out_shape=out_shape,
        scratch_shapes=scratch,
        compiler_params=pltpu.CompilerParams(
            dimension_semantics=("arbitrary",), vmem_limit_bytes=ROOM + 4 * extent * extent * (depth + 8)
        ),
        cost_estimate=pl.CostEstimate(
            flops=6 * MOST * rows * extent * extent,
            bytes_accessed=12 * extent**3,
            transcendentals=0,
        ),
    )(*operands)


def per_device(sources, perambs, source_ids, peramb_ids, sink_counts, weights):
    workers = lax.axis_size("work")
    extent = sources.shape[2]
    per_unit = UNIT_ROWS * workers // extent
    half = workers // 2
    far = list(range(half, workers))
    near = [1, *range(half // 2, half), *range(2, half // 2)]
    order = []
    while far or near:
        take_far = far and (not near or len(order) in FAR_TURNS)
        order.append(far.pop(0) if take_far else near.pop(0))
    early, late = tuple(order[:IN_FLIGHT]), (0, *order[IN_FLIGHT:])
    pieces = dict(zip(early, choose_pieces(sources, source_ids, early)))
    pieces.update(zip(late, choose_pieces(sources, source_ids, late)))
    arrived = {0: pieces[0]}

    def send(place):
        shift = order[place]
        piece = pieces[shift]
        if place >= IN_FLIGHT:
            before = order[place - IN_FLIGHT]
            piece, arrived[before] = lax.optimization_barrier((piece, arrived[before]))
        arrived[shift] = lax.ppermute(piece, "work", [(i, i ^ shift) for i in range(workers)])

    for place in range(IN_FLIGHT):
        send(place)
    matrices = choose_matrices(perambs, peramb_ids, sink_counts, workers, extent)
    matrices = lax.all_to_all(matrices, "work", split_axis=0, concat_axis=0, tiled=True)
    leg3, leg2, leg1 = make_legs(matrices, sink_counts, weights, workers)
    for place in range(IN_FLIGHT, len(order) - HELD_BACK):
        send(place)

    acc = None
    for group, units in enumerate(GROUPS):
        members = [arrived[u * per_unit + lane] for u in units for lane in range(per_unit)]
        acc = add_group(units, members, leg3, leg2, leg1, acc, group == len(GROUPS) - 1)
        if group == 0:
            for place in range(len(order) - HELD_BACK, len(order)):
                shift = order[place]
                pieces[shift], acc = lax.optimization_barrier((pieces[shift], acc))
                send(place)
    return acc.reshape(1, extent * extent, extent)


def solution(mesh):
    return jax.shard_map(
        per_device,
        mesh=mesh,
        in_specs=(P("cfg", "work", None), P("cfg", "work"), P(), P(), P(), P()),
        out_specs=P(("cfg", "work"), None, None),
        check_vma=False,
    )
```

```python
import functools

import jax
import jax.numpy as jnp
from jax import lax
from jax.experimental import pallas as pl
from jax.experimental.pallas import tpu as pltpu
from jax.sharding import PartitionSpec as P

MOST = 6
LEGS = 3
UNIT_ROWS = 16
B_BLOCK = 64
ACC = jnp.bfloat16
GROUPS = ((0, 2, 4), (3, 5), (1, 6), (7,))
IN_FLIGHT = 5
FAR_TURNS = (2, 4, 5, 6, 10, 11)
HELD_BACK = 0
SMALL_VMEM = 16 * 1024 * 1024
ROOM = 13 * 1024 * 1024


def pieces_kernel(shifts, ids_ref, source_ref, *refs):
    piece_refs, (held_ref, in_sems, out_sems) = refs[: len(shifts)], refs[len(shifts) :]
    own = lax.axis_index("work")
    reads, writes = [], []
    for i, shift in enumerate(shifts):
        reads.append(
            pltpu.make_async_copy(
                source_ref.at[ids_ref[own ^ shift]], held_ref.at[i], in_sems.at[i]
            )
        )
        writes.append(pltpu.make_async_copy(held_ref.at[i], piece_refs[i], out_sems.at[i]))
        reads[i].start()
    for read, write in zip(reads, writes):
        read.wait()
        write.start()
    for write in writes:
        write.wait()


def choose_pieces(sources, source_ids, shifts):
    return pl.pallas_call(
        functools.partial(pieces_kernel, shifts),
        in_specs=[pl.BlockSpec(memory_space=pltpu.SMEM), pl.BlockSpec(memory_space=pl.ANY)],
        out_specs=[pl.BlockSpec(memory_space=pl.ANY)] * len(shifts),
        out_shape=[jax.ShapeDtypeStruct(sources.shape[1:], sources.dtype)] * len(shifts),
        scratch_shapes=[
            pltpu.VMEM((len(shifts), *sources.shape[1:]), sources.dtype),
            pltpu.SemaphoreType.DMA((len(shifts),)),
            pltpu.SemaphoreType.DMA((len(shifts),)),
        ],
        compiler_params=pltpu.CompilerParams(vmem_limit_bytes=SMALL_VMEM),
    )(source_ids, sources)


def matrices_kernel(workers, counts_ref, matrix_ids_ref, peramb_ref, matrix_ref, choice_ref, spread_ref):
    rows = MOST * LEGS
    diagrams = matrix_ids_ref.shape[1]
    total = peramb_ref.shape[0]
    lanes = lax.broadcasted_iota(jnp.int32, (1, total), 1)

    def mark(sink, start):
        for slot in range(MOST):
            diagram = jnp.minimum(start + slot, diagrams - 1)
            for leg in range(LEGS):
                choice_ref[pl.ds(sink * rows + slot * LEGS + leg, 1), :] = jnp.where(
                    lanes == matrix_ids_ref[leg, diagram], 1.0, 0.0
                )
        return start + counts_ref[sink]

    lax.fori_loop(0, workers, mark, 0)
    chosen = jnp.dot(
        choice_ref[...].astype(jnp.bfloat16), peramb_ref[...], preferred_element_type=jnp.float32
    )
    extent = matrix_ref.shape[2]
    a_per = peramb_ref.shape[1] // extent
    for row in range(a_per):
        spread_ref[pl.ds(row, workers * rows, stride=a_per), :] = chosen[
            :, row * extent : (row + 1) * extent
        ]
    matrix_ref[...] = spread_ref[...].reshape(matrix_ref.shape).astype(jnp.bfloat16)


def choose_matrices(perambs, peramb_ids, sink_counts, workers, extent):
    rows = MOST * LEGS
    a_per = perambs.shape[1] // extent
    smem = pl.BlockSpec(memory_space=pltpu.SMEM)
    vmem = pl.BlockSpec(memory_space=pltpu.VMEM)
    return pl.pallas_call(
        functools.partial(matrices_kernel, workers),
        in_specs=[smem, smem, vmem],
        out_specs=vmem,
        out_shape=jax.ShapeDtypeStruct((workers, rows * a_per, extent), jnp.bfloat16),
        scratch_shapes=[
            pltpu.VMEM((workers * rows, perambs.shape[0]), jnp.float32),
            pltpu.VMEM((workers * rows * a_per, extent), jnp.float32),
        ],
        compiler_params=pltpu.CompilerParams(vmem_limit_bytes=SMALL_VMEM),
    )(sink_counts, peramb_ids.T, perambs)


def legs_kernel(
    workers, counts_ref, weights_ref, matrix_ref, leg3_ref, leg2_ref, leg1_ref, flat_ref, leg_ref
):
    extent = matrix_ref.shape[2]
    rows = MOST * LEGS
    a_per = matrix_ref.shape[1] // rows
    flat_ref[...] = matrix_ref[...].astype(jnp.float32).reshape(flat_ref.shape)
    own = lax.axis_index("work")
    start = lax.fori_loop(0, own, lambda i, total: total + counts_ref[i], 0)
    count = counts_ref[own]
    unit = UNIT_ROWS // a_per
    units = workers // unit
    for slot in range(MOST):
        for leg in range(LEGS):
            base = (slot * LEGS + leg) * a_per
            for row in range(a_per):
                leg_ref[pl.ds(row, workers, stride=a_per), :] = flat_ref[
                    pl.ds(base + row, workers, stride=rows * a_per), :
                ]
            if leg == 2:
                leg3_ref[:, slot * extent : (slot + 1) * extent] = leg_ref[...].T.astype(
                    jnp.bfloat16
                )
            elif leg == 1:
                leg2_ref[slot * extent : (slot + 1) * extent, :] = leg_ref[...].astype(
                    jnp.bfloat16
                )
            else:
                diagram = jnp.minimum(start + slot, weights_ref.shape[0] - 1)
                factor = jnp.where(slot < count, weights_ref[diagram], 0.0)
                leg_ref[...] = (factor * leg_ref[...]).T
                for block in range(units):
                    place = (own // unit) ^ block
                    leg1_ref[block, slot * UNIT_ROWS : (slot + 1) * UNIT_ROWS, :] = leg_ref[
                        pl.ds(pl.multiple_of(place * UNIT_ROWS, UNIT_ROWS), UNIT_ROWS), :
                    ].astype(jnp.bfloat16)


def make_legs(matrices, sink_counts, weights, workers):
    extent = matrices.shape[2]
    a_per = extent // workers
    smem = pl.BlockSpec(memory_space=pltpu.SMEM)
    vmem = pl.BlockSpec(memory_space=pltpu.VMEM)
    return pl.pallas_call(
        functools.partial(legs_kernel, workers),
        in_specs=[smem, smem, vmem],
        out_specs=[vmem] * 3,
        out_shape=[
            jax.ShapeDtypeStruct((extent, MOST * extent), jnp.bfloat16),
            jax.ShapeDtypeStruct((MOST * extent, extent), jnp.bfloat16),
            jax.ShapeDtypeStruct(
                (extent // UNIT_ROWS, MOST * UNIT_ROWS, extent), jnp.bfloat16
            ),
        ],
        scratch_shapes=[
            pltpu.VMEM((matrices.shape[0] * matrices.shape[1], extent), jnp.float32),
            pltpu.VMEM((extent, extent), jnp.float32),
        ],
        compiler_params=pltpu.CompilerParams(vmem_limit_bytes=SMALL_VMEM),
    )(sink_counts, weights, matrices)


def group_kernel(first, last, units, per_unit, extent, *refs):
    pieces = len(units) * per_unit
    piece_refs = refs[:pieces]
    leg3_ref, leg2_ref, leg1_ref = refs[pieces : pieces + 3]
    refs = refs[pieces + 3 :]
    if not first:
        acc_ref, refs = refs[0], refs[1:]
    out_ref, turned_ref, outer_ref, across_ref, held_ref, sems = refs[:6]
    a_per = piece_refs[0].shape[0] // extent
    unit_depth = MOST * UNIT_ROWS
    depth = unit_depth * len(units)
    pitch = depth + 8
    step = pl.program_id(0)

    def fetch(piece):
        return pltpu.make_async_copy(piece_refs[piece], held_ref.at[piece], sems.at[piece])

    @pl.when(step == 0)
    def fetch_all():
        for piece in range(pieces):
            fetch(piece).start()

    def inner_legs(piece):
        place, lane = piece // per_unit, piece % per_unit
        fetch(piece).wait()
        sender = (lax.axis_index("work") & (per_unit - 1)) ^ lane
        third = jnp.dot(
            held_ref[piece], leg3_ref[...], preferred_element_type=jnp.float32
        ).astype(jnp.bfloat16)
        for d in range(MOST):
            columns = third[:, d * extent : (d + 1) * extent]
            wide = jnp.concatenate(
                [columns[a * extent : (a + 1) * extent] for a in range(a_per)], axis=1
            )
            second = jnp.dot(
                leg2_ref[d * extent : (d + 1) * extent, :],
                wide,
                preferred_element_type=jnp.float32,
            )
            for a in range(a_per):
                row = place * unit_depth + d * UNIT_ROWS + sender * a_per + a
                turned_ref[pl.ds(row, extent, stride=pitch), :] = second[
                    :, a * extent : (a + 1) * extent
                ]

    @pl.when(step == 0)
    def turn_outer():
        for place, unit in enumerate(units):
            outer_ref[place * unit_depth : (place + 1) * unit_depth, :] = leg1_ref[
                unit
            ].astype(jnp.float32)
        across_ref[...] = outer_ref[...].T.astype(jnp.bfloat16)

    for piece in range(pieces):
        pl.when(step == piece)(functools.partial(inner_legs, piece))

    @pl.when(step >= pieces)
    def outer_leg():
        begin = (step - pieces) * B_BLOCK
        wide = jnp.concatenate(
            [
                turned_ref[pl.ds(pl.multiple_of((begin + b) * pitch, 8), depth), :].astype(
                    jnp.bfloat16
                )
                for b in range(B_BLOCK)
            ],
            axis=1,
        )
        whole = jnp.dot(across_ref[...], wide, preferred_element_type=jnp.float32)
        for b in range(B_BLOCK):
            part = whole[:, b * extent : (b + 1) * extent]
            if not first:
                part = part + acc_ref[b].astype(jnp.float32)
            if last:
                refs[6][pl.ds(b, extent, stride=B_BLOCK + 8), :] = part
            else:
                out_ref[b] = part.astype(out_ref.dtype)
        if last:
            for a in range(extent):
                out_ref[a] = refs[6][pl.ds(a * (B_BLOCK + 8), B_BLOCK), :].astype(jnp.bfloat16)


def add_group(units, pieces, leg3, leg2, leg1, acc, last):
    extent = leg3.shape[0]
    count = len(pieces)
    per_unit = count // len(units)
    depth = MOST * UNIT_ROWS * len(units)
    first = acc is None
    blocks = extent // B_BLOCK

    def whole_spec(x):
        return pl.BlockSpec(x.shape, lambda i: (0,) * x.ndim)

    def block_of(i):
        return jnp.maximum(i - count, 0)

    operands = [*pieces, leg3, leg2, leg1]
    in_specs = [pl.BlockSpec(memory_space=pl.ANY)] * count
    in_specs += [whole_spec(x) for x in operands[count:]]
    if not first:
        operands.append(acc)
        in_specs.append(pl.BlockSpec((B_BLOCK, extent, extent), lambda i: (block_of(i), 0, 0)))
    scratch = [
        pltpu.VMEM((extent * (depth + 8), extent), jnp.float32),
        pltpu.VMEM((depth, extent), jnp.float32),
        pltpu.VMEM((extent, depth), jnp.bfloat16),
        pltpu.VMEM((count, *pieces[0].shape), jnp.bfloat16),
        pltpu.SemaphoreType.DMA((count,)),
    ]
    if last:
        out_shape = jax.ShapeDtypeStruct((extent, extent, extent), jnp.bfloat16)
        out_spec = pl.BlockSpec((extent, B_BLOCK, extent), lambda i: (0, block_of(i), 0))
        scratch.append(pltpu.VMEM((extent * (B_BLOCK + 8), extent), jnp.float32))
    else:
        out_shape = jax.ShapeDtypeStruct((extent, extent, extent), ACC)
        out_spec = pl.BlockSpec((B_BLOCK, extent, extent), lambda i: (block_of(i), 0, 0))
    rows = count * pieces[0].shape[0]
    return pl.pallas_call(
        functools.partial(group_kernel, first, last, units, per_unit, extent),
        grid=(count + blocks,),
        in_specs=in_specs,
        out_specs=out_spec,
        out_shape=out_shape,
        scratch_shapes=scratch,
        compiler_params=pltpu.CompilerParams(
            dimension_semantics=("arbitrary",), vmem_limit_bytes=ROOM + 4 * extent * extent * (depth + 8)
        ),
        cost_estimate=pl.CostEstimate(
            flops=6 * MOST * rows * extent * extent,
            bytes_accessed=12 * extent**3,
            transcendentals=0,
        ),
    )(*operands)


def per_device(sources, perambs, source_ids, peramb_ids, sink_counts, weights):
    workers = lax.axis_size("work")
    extent = sources.shape[2]
    per_unit = UNIT_ROWS * workers // extent
    half = workers // 2
    far = list(range(half, workers))
    upper, lower = list(range(half // 2, half)), list(range(2, half // 2))
    near = [1, *upper[:-1], *lower[:1], upper[-1], *lower[1:]]
    order = []
    while far or near:
        take_far = far and (not near or len(order) in FAR_TURNS)
        order.append(far.pop(0) if take_far else near.pop(0))
    early, late = tuple(order[:IN_FLIGHT]), (0, *order[IN_FLIGHT:])
    pieces = dict(zip(early, choose_pieces(sources, source_ids, early)))
    pieces.update(zip(late, choose_pieces(sources, source_ids, late)))
    arrived = {0: pieces[0]}

    def send(place):
        shift = order[place]
        piece = pieces[shift]
        if place >= IN_FLIGHT:
            before = order[place - IN_FLIGHT]
            piece, arrived[before] = lax.optimization_barrier((piece, arrived[before]))
        arrived[shift] = lax.ppermute(piece, "work", [(i, i ^ shift) for i in range(workers)])

    for place in range(IN_FLIGHT):
        send(place)
    matrices = choose_matrices(perambs, peramb_ids, sink_counts, workers, extent)
    matrices = lax.all_to_all(matrices, "work", split_axis=0, concat_axis=0, tiled=True)
    leg3, leg2, leg1 = make_legs(matrices, sink_counts, weights, workers)
    for place in range(IN_FLIGHT, len(order) - HELD_BACK):
        send(place)

    acc = None
    for group, units in enumerate(GROUPS):
        members = [arrived[u * per_unit + lane] for u in units for lane in range(per_unit)]
        acc = add_group(units, members, leg3, leg2, leg1, acc, group == len(GROUPS) - 1)
        if group == 0:
            for place in range(len(order) - HELD_BACK, len(order)):
                shift = order[place]
                pieces[shift], acc = lax.optimization_barrier((pieces[shift], acc))
                send(place)
    return acc.reshape(1, extent * extent, extent)


def solution(mesh):
    return jax.shard_map(
        per_device,
        mesh=mesh,
        in_specs=(P("cfg", "work", None), P("cfg", "work"), P(), P(), P(), P()),
        out_specs=P(("cfg", "work"), None, None),
        check_vma=False,
    )
```

```python
import functools

import jax
import jax.numpy as jnp
from jax import lax
from jax.experimental import pallas as pl
from jax.experimental.pallas import tpu as pltpu
from jax.sharding import PartitionSpec as P

MOST = 6
LEGS = 3
UNIT_ROWS = 16
B_BLOCK = 64
ACC = jnp.bfloat16
GROUPS = ((0, 2, 4), (3, 5), (1, 6), (7,))
IN_FLIGHT = 5
FAR_TURNS = (2, 4, 5, 6, 10, 11)
HELD_BACK = 5
SMALL_VMEM = 16 * 1024 * 1024
ROOM = 13 * 1024 * 1024


def pieces_kernel(shifts, ids_ref, source_ref, *refs):
    piece_refs, (held_ref, in_sems, out_sems) = refs[: len(shifts)], refs[len(shifts) :]
    own = lax.axis_index("work")
    reads, writes = [], []
    for i, shift in enumerate(shifts):
        reads.append(
            pltpu.make_async_copy(
                source_ref.at[ids_ref[own ^ shift]], held_ref.at[i], in_sems.at[i]
            )
        )
        writes.append(pltpu.make_async_copy(held_ref.at[i], piece_refs[i], out_sems.at[i]))
        reads[i].start()
    for read, write in zip(reads, writes):
        read.wait()
        write.start()
    for write in writes:
        write.wait()


def choose_pieces(sources, source_ids, shifts):
    return pl.pallas_call(
        functools.partial(pieces_kernel, shifts),
        in_specs=[pl.BlockSpec(memory_space=pltpu.SMEM), pl.BlockSpec(memory_space=pl.ANY)],
        out_specs=[pl.BlockSpec(memory_space=pl.ANY)] * len(shifts),
        out_shape=[jax.ShapeDtypeStruct(sources.shape[1:], sources.dtype)] * len(shifts),
        scratch_shapes=[
            pltpu.VMEM((len(shifts), *sources.shape[1:]), sources.dtype),
            pltpu.SemaphoreType.DMA((len(shifts),)),
            pltpu.SemaphoreType.DMA((len(shifts),)),
        ],
        compiler_params=pltpu.CompilerParams(vmem_limit_bytes=SMALL_VMEM),
    )(source_ids, sources)


def matrices_kernel(workers, counts_ref, matrix_ids_ref, peramb_ref, matrix_ref, choice_ref, spread_ref):
    rows = MOST * LEGS
    diagrams = matrix_ids_ref.shape[1]
    total = peramb_ref.shape[0]
    lanes = lax.broadcasted_iota(jnp.int32, (1, total), 1)

    def mark(sink, start):
        for slot in range(MOST):
            diagram = jnp.minimum(start + slot, diagrams - 1)
            for leg in range(LEGS):
                choice_ref[pl.ds(sink * rows + slot * LEGS + leg, 1), :] = jnp.where(
                    lanes == matrix_ids_ref[leg, diagram], 1.0, 0.0
                )
        return start + counts_ref[sink]

    lax.fori_loop(0, workers, mark, 0)
    chosen = jnp.dot(
        choice_ref[...].astype(jnp.bfloat16), peramb_ref[...], preferred_element_type=jnp.float32
    )
    extent = matrix_ref.shape[2]
    a_per = peramb_ref.shape[1] // extent
    for row in range(a_per):
        spread_ref[pl.ds(row, workers * rows, stride=a_per), :] = chosen[
            :, row * extent : (row + 1) * extent
        ]
    matrix_ref[...] = spread_ref[...].reshape(matrix_ref.shape).astype(jnp.bfloat16)


def choose_matrices(perambs, peramb_ids, sink_counts, workers, extent):
    rows = MOST * LEGS
    a_per = perambs.shape[1] // extent
    smem = pl.BlockSpec(memory_space=pltpu.SMEM)
    vmem = pl.BlockSpec(memory_space=pltpu.VMEM)
    return pl.pallas_call(
        functools.partial(matrices_kernel, workers),
        in_specs=[smem, smem, vmem],
        out_specs=vmem,
        out_shape=jax.ShapeDtypeStruct((workers, rows * a_per, extent), jnp.bfloat16),
        scratch_shapes=[
            pltpu.VMEM((workers * rows, perambs.shape[0]), jnp.float32),
            pltpu.VMEM((workers * rows * a_per, extent), jnp.float32),
        ],
        compiler_params=pltpu.CompilerParams(vmem_limit_bytes=SMALL_VMEM),
    )(sink_counts, peramb_ids.T, perambs)


def legs_kernel(
    workers, counts_ref, weights_ref, matrix_ref, leg3_ref, leg2_ref, leg1_ref, flat_ref, leg_ref
):
    extent = matrix_ref.shape[2]
    rows = MOST * LEGS
    a_per = matrix_ref.shape[1] // rows
    flat_ref[...] = matrix_ref[...].astype(jnp.float32).reshape(flat_ref.shape)
    own = lax.axis_index("work")
    start = lax.fori_loop(0, own, lambda i, total: total + counts_ref[i], 0)
    count = counts_ref[own]
    unit = UNIT_ROWS // a_per
    units = workers // unit
    for slot in range(MOST):
        for leg in range(LEGS):
            base = (slot * LEGS + leg) * a_per
            for row in range(a_per):
                leg_ref[pl.ds(row, workers, stride=a_per), :] = flat_ref[
                    pl.ds(base + row, workers, stride=rows * a_per), :
                ]
            if leg == 2:
                leg3_ref[:, slot * extent : (slot + 1) * extent] = leg_ref[...].T.astype(
                    jnp.bfloat16
                )
            elif leg == 1:
                leg2_ref[slot * extent : (slot + 1) * extent, :] = leg_ref[...].astype(
                    jnp.bfloat16
                )
            else:
                diagram = jnp.minimum(start + slot, weights_ref.shape[0] - 1)
                factor = jnp.where(slot < count, weights_ref[diagram], 0.0)
                leg_ref[...] = (factor * leg_ref[...]).T
                for block in range(units):
                    place = (own // unit) ^ block
                    leg1_ref[block, slot * UNIT_ROWS : (slot + 1) * UNIT_ROWS, :] = leg_ref[
                        pl.ds(pl.multiple_of(place * UNIT_ROWS, UNIT_ROWS), UNIT_ROWS), :
                    ].astype(jnp.bfloat16)


def make_legs(matrices, sink_counts, weights, workers):
    extent = matrices.shape[2]
    a_per = extent // workers
    smem = pl.BlockSpec(memory_space=pltpu.SMEM)
    vmem = pl.BlockSpec(memory_space=pltpu.VMEM)
    return pl.pallas_call(
        functools.partial(legs_kernel, workers),
        in_specs=[smem, smem, vmem],
        out_specs=[vmem] * 3,
        out_shape=[
            jax.ShapeDtypeStruct((extent, MOST * extent), jnp.bfloat16),
            jax.ShapeDtypeStruct((MOST * extent, extent), jnp.bfloat16),
            jax.ShapeDtypeStruct(
                (extent // UNIT_ROWS, MOST * UNIT_ROWS, extent), jnp.bfloat16
            ),
        ],
        scratch_shapes=[
            pltpu.VMEM((matrices.shape[0] * matrices.shape[1], extent), jnp.float32),
            pltpu.VMEM((extent, extent), jnp.float32),
        ],
        compiler_params=pltpu.CompilerParams(vmem_limit_bytes=SMALL_VMEM),
    )(sink_counts, weights, matrices)


def group_kernel(first, last, units, per_unit, extent, *refs):
    pieces = len(units) * per_unit
    piece_refs = refs[:pieces]
    leg3_ref, leg2_ref, leg1_ref = refs[pieces : pieces + 3]
    refs = refs[pieces + 3 :]
    if not first:
        acc_ref, refs = refs[0], refs[1:]
    out_ref, turned_ref, outer_ref, across_ref, held_ref, sems = refs[:6]
    a_per = piece_refs[0].shape[0] // extent
    unit_depth = MOST * UNIT_ROWS
    depth = unit_depth * len(units)
    pitch = depth + 8
    step = pl.program_id(0)

    def fetch(piece):
        return pltpu.make_async_copy(piece_refs[piece], held_ref.at[piece], sems.at[piece])

    @pl.when(step == 0)
    def fetch_all():
        for piece in range(pieces):
            fetch(piece).start()

    def inner_legs(piece):
        place, lane = piece // per_unit, piece % per_unit
        fetch(piece).wait()
        sender = (lax.axis_index("work") & (per_unit - 1)) ^ lane
        third = jnp.dot(
            held_ref[piece], leg3_ref[...], preferred_element_type=jnp.float32
        ).astype(jnp.bfloat16)
        for d in range(MOST):
            columns = third[:, d * extent : (d + 1) * extent]
            wide = jnp.concatenate(
                [columns[a * extent : (a + 1) * extent] for a in range(a_per)], axis=1
            )
            second = jnp.dot(
                leg2_ref[d * extent : (d + 1) * extent, :],
                wide,
                preferred_element_type=jnp.float32,
            )
            for a in range(a_per):
                row = place * unit_depth + d * UNIT_ROWS + sender * a_per + a
                turned_ref[pl.ds(row, extent, stride=pitch), :] = second[
                    :, a * extent : (a + 1) * extent
                ]

    @pl.when(step == 0)
    def turn_outer():
        for place, unit in enumerate(units):
            outer_ref[place * unit_depth : (place + 1) * unit_depth, :] = leg1_ref[
                unit
            ].astype(jnp.float32)
        across_ref[...] = outer_ref[...].T.astype(jnp.bfloat16)

    for piece in range(pieces):
        pl.when(step == piece)(functools.partial(inner_legs, piece))

    @pl.when(step >= pieces)
    def outer_leg():
        begin = (step - pieces) * B_BLOCK
        wide = jnp.concatenate(
            [
                turned_ref[pl.ds(pl.multiple_of((begin + b) * pitch, 8), depth), :].astype(
                    jnp.bfloat16
                )
                for b in range(B_BLOCK)
            ],
            axis=1,
        )
        whole = jnp.dot(across_ref[...], wide, preferred_element_type=jnp.float32)
        for b in range(B_BLOCK):
            part = whole[:, b * extent : (b + 1) * extent]
            if not first:
                part = part + acc_ref[b].astype(jnp.float32)
            if last:
                refs[6][pl.ds(b, extent, stride=B_BLOCK + 8), :] = part
            else:
                out_ref[b] = part.astype(out_ref.dtype)
        if last:
            for a in range(extent):
                out_ref[a] = refs[6][pl.ds(a * (B_BLOCK + 8), B_BLOCK), :].astype(jnp.bfloat16)


def add_group(units, pieces, leg3, leg2, leg1, acc, last):
    extent = leg3.shape[0]
    count = len(pieces)
    per_unit = count // len(units)
    depth = MOST * UNIT_ROWS * len(units)
    first = acc is None
    blocks = extent // B_BLOCK

    def whole_spec(x):
        return pl.BlockSpec(x.shape, lambda i: (0,) * x.ndim)

    def block_of(i):
        return jnp.maximum(i - count, 0)

    operands = [*pieces, leg3, leg2, leg1]
    in_specs = [pl.BlockSpec(memory_space=pltpu.HBM)] * count
    in_specs += [whole_spec(x) for x in operands[count:]]
    if not first:
        operands.append(acc)
        in_specs.append(pl.BlockSpec((B_BLOCK, extent, extent), lambda i: (block_of(i), 0, 0)))
    scratch = [
        pltpu.VMEM((extent * (depth + 8), extent), jnp.float32),
        pltpu.VMEM((depth, extent), jnp.float32),
        pltpu.VMEM((extent, depth), jnp.bfloat16),
        pltpu.VMEM((count, *pieces[0].shape), jnp.bfloat16),
        pltpu.SemaphoreType.DMA((count,)),
    ]
    if last:
        out_shape = jax.ShapeDtypeStruct((extent, extent, extent), jnp.bfloat16)
        out_spec = pl.BlockSpec((extent, B_BLOCK, extent), lambda i: (0, block_of(i), 0))
        scratch.append(pltpu.VMEM((extent * (B_BLOCK + 8), extent), jnp.float32))
    else:
        out_shape = jax.ShapeDtypeStruct((extent, extent, extent), ACC)
        out_spec = pl.BlockSpec((B_BLOCK, extent, extent), lambda i: (block_of(i), 0, 0))
    rows = count * pieces[0].shape[0]
    return pl.pallas_call(
        functools.partial(group_kernel, first, last, units, per_unit, extent),
        grid=(count + blocks,),
        in_specs=in_specs,
        out_specs=out_spec,
        out_shape=out_shape,
        scratch_shapes=scratch,
        compiler_params=pltpu.CompilerParams(
            dimension_semantics=("arbitrary",), vmem_limit_bytes=ROOM + 4 * extent * extent * (depth + 8)
        ),
        cost_estimate=pl.CostEstimate(
            flops=6 * MOST * rows * extent * extent,
            bytes_accessed=12 * extent**3,
            transcendentals=0,
        ),
    )(*operands)


def per_device(sources, perambs, source_ids, peramb_ids, sink_counts, weights):
    workers = lax.axis_size("work")
    extent = sources.shape[2]
    per_unit = UNIT_ROWS * workers // extent
    half = workers // 2
    far = list(range(half, workers))
    upper, lower = list(range(half // 2, half)), list(range(2, half // 2))
    near = [1, *upper, *lower]
    order = []
    while far or near:
        take_far = far and (not near or len(order) in FAR_TURNS)
        order.append(far.pop(0) if take_far else near.pop(0))
    early, late = tuple(order[:IN_FLIGHT]), (0, *order[IN_FLIGHT:])
    pieces = dict(zip(early, choose_pieces(sources, source_ids, early)))
    pieces.update(zip(late, choose_pieces(sources, source_ids, late)))
    arrived = {0: pieces[0]}

    def send(place):
        shift = order[place]
        piece = pieces[shift]
        if place >= IN_FLIGHT:
            before = order[place - IN_FLIGHT]
            piece, arrived[before] = lax.optimization_barrier((piece, arrived[before]))
        arrived[shift] = lax.ppermute(piece, "work", [(i, i ^ shift) for i in range(workers)])

    for place in range(IN_FLIGHT):
        send(place)
    matrices = choose_matrices(perambs, peramb_ids, sink_counts, workers, extent)
    matrices = lax.all_to_all(matrices, "work", split_axis=0, concat_axis=0, tiled=True)
    leg3, leg2, leg1 = make_legs(matrices, sink_counts, weights, workers)
    for place in range(IN_FLIGHT, len(order) - HELD_BACK):
        send(place)

    acc = None
    for group, units in enumerate(GROUPS):
        members = [arrived[u * per_unit + lane] for u in units for lane in range(per_unit)]
        acc = add_group(units, members, leg3, leg2, leg1, acc, group == len(GROUPS) - 1)
        if group == 0:
            for place in range(len(order) - HELD_BACK, len(order)):
                shift = order[place]
                pieces[shift], acc = lax.optimization_barrier((pieces[shift], acc))
                send(place)
    return acc.reshape(1, extent * extent, extent)


def solution(mesh):
    return jax.shard_map(
        per_device,
        mesh=mesh,
        in_specs=(P("cfg", "work", None), P("cfg", "work"), P(), P(), P(), P()),
        out_specs=P(("cfg", "work"), None, None),
        check_vma=False,
    )
```

```python
import functools

import jax
import jax.numpy as jnp
from jax import lax
from jax.experimental import pallas as pl
from jax.experimental.pallas import tpu as pltpu
from jax.sharding import PartitionSpec as P

MOST = 6
LEGS = 3
UNIT_ROWS = 16
B_BLOCK = 64
ACC = jnp.bfloat16
GROUPS = ((0, 2, 4), (3, 5), (1, 6), (7,))
IN_FLIGHT = 5
FAR_TURNS = (2, 4, 5, 6, 10, 11)
HELD_BACK = 5
SMALL_VMEM = 16 * 1024 * 1024
ROOM = 13 * 1024 * 1024


def pieces_kernel(shifts, ids_ref, source_ref, *refs):
    piece_refs, (held_ref, in_sems, out_sems) = refs[: len(shifts)], refs[len(shifts) :]
    own = lax.axis_index("work")
    reads, writes = [], []
    for i, shift in enumerate(shifts):
        reads.append(
            pltpu.make_async_copy(
                source_ref.at[ids_ref[own ^ shift]], held_ref.at[i], in_sems.at[i]
            )
        )
        writes.append(pltpu.make_async_copy(held_ref.at[i], piece_refs[i], out_sems.at[i]))
        reads[i].start()
    for read, write in zip(reads, writes):
        read.wait()
        write.start()
    for write in writes:
        write.wait()


def choose_pieces(sources, source_ids, shifts):
    return pl.pallas_call(
        functools.partial(pieces_kernel, shifts),
        in_specs=[pl.BlockSpec(memory_space=pltpu.SMEM), pl.BlockSpec(memory_space=pl.ANY)],
        out_specs=[pl.BlockSpec(memory_space=pl.ANY)] * len(shifts),
        out_shape=[jax.ShapeDtypeStruct(sources.shape[1:], sources.dtype)] * len(shifts),
        scratch_shapes=[
            pltpu.VMEM((len(shifts), *sources.shape[1:]), sources.dtype),
            pltpu.SemaphoreType.DMA((len(shifts),)),
            pltpu.SemaphoreType.DMA((len(shifts),)),
        ],
        compiler_params=pltpu.CompilerParams(vmem_limit_bytes=SMALL_VMEM),
    )(source_ids, sources)


def matrices_kernel(workers, counts_ref, matrix_ids_ref, peramb_ref, matrix_ref, choice_ref, spread_ref):
    rows = MOST * LEGS
    diagrams = matrix_ids_ref.shape[1]
    total = peramb_ref.shape[0]
    lanes = lax.broadcasted_iota(jnp.int32, (1, total), 1)

    def mark(sink, start):
        for slot in range(MOST):
            diagram = jnp.minimum(start + slot, diagrams - 1)
            for leg in range(LEGS):
                choice_ref[pl.ds(sink * rows + slot * LEGS + leg, 1), :] = jnp.where(
                    lanes == matrix_ids_ref[leg, diagram], 1.0, 0.0
                )
        return start + counts_ref[sink]

    lax.fori_loop(0, workers, mark, 0)
    chosen = jnp.dot(
        choice_ref[...].astype(jnp.bfloat16), peramb_ref[...], preferred_element_type=jnp.float32
    )
    extent = matrix_ref.shape[2]
    a_per = peramb_ref.shape[1] // extent
    for row in range(a_per):
        spread_ref[pl.ds(row, workers * rows, stride=a_per), :] = chosen[
            :, row * extent : (row + 1) * extent
        ]
    matrix_ref[...] = spread_ref[...].reshape(matrix_ref.shape).astype(jnp.bfloat16)


def choose_matrices(perambs, peramb_ids, sink_counts, workers, extent):
    rows = MOST * LEGS
    a_per = perambs.shape[1] // extent
    smem = pl.BlockSpec(memory_space=pltpu.SMEM)
    vmem = pl.BlockSpec(memory_space=pltpu.VMEM)
    return pl.pallas_call(
        functools.partial(matrices_kernel, workers),
        in_specs=[smem, smem, vmem],
        out_specs=vmem,
        out_shape=jax.ShapeDtypeStruct((workers, rows * a_per, extent), jnp.bfloat16),
        scratch_shapes=[
            pltpu.VMEM((workers * rows, perambs.shape[0]), jnp.float32),
            pltpu.VMEM((workers * rows * a_per, extent), jnp.float32),
        ],
        compiler_params=pltpu.CompilerParams(vmem_limit_bytes=SMALL_VMEM),
    )(sink_counts, peramb_ids.T, perambs)


def legs_kernel(
    workers, counts_ref, weights_ref, matrix_ref, leg3_ref, leg2_ref, leg1_ref, flat_ref, leg_ref
):
    extent = matrix_ref.shape[2]
    rows = MOST * LEGS
    a_per = matrix_ref.shape[1] // rows
    flat_ref[...] = matrix_ref[...].astype(jnp.float32).reshape(flat_ref.shape)
    own = lax.axis_index("work")
    start = lax.fori_loop(0, own, lambda i, total: total + counts_ref[i], 0)
    count = counts_ref[own]
    unit = UNIT_ROWS // a_per
    units = workers // unit
    for slot in range(MOST):
        for leg in range(LEGS):
            base = (slot * LEGS + leg) * a_per
            for row in range(a_per):
                leg_ref[pl.ds(row, workers, stride=a_per), :] = flat_ref[
                    pl.ds(base + row, workers, stride=rows * a_per), :
                ]
            if leg == 2:
                leg3_ref[:, slot * extent : (slot + 1) * extent] = leg_ref[...].T.astype(
                    jnp.bfloat16
                )
            elif leg == 1:
                leg2_ref[slot * extent : (slot + 1) * extent, :] = leg_ref[...].astype(
                    jnp.bfloat16
                )
            else:
                diagram = jnp.minimum(start + slot, weights_ref.shape[0] - 1)
                factor = jnp.where(slot < count, weights_ref[diagram], 0.0)
                leg_ref[...] = (factor * leg_ref[...]).T
                for block in range(units):
                    place = (own // unit) ^ block
                    leg1_ref[block, slot * UNIT_ROWS : (slot + 1) * UNIT_ROWS, :] = leg_ref[
                        pl.ds(pl.multiple_of(place * UNIT_ROWS, UNIT_ROWS), UNIT_ROWS), :
                    ].astype(jnp.bfloat16)


def make_legs(matrices, sink_counts, weights, workers):
    extent = matrices.shape[2]
    a_per = extent // workers
    smem = pl.BlockSpec(memory_space=pltpu.SMEM)
    vmem = pl.BlockSpec(memory_space=pltpu.VMEM)
    return pl.pallas_call(
        functools.partial(legs_kernel, workers),
        in_specs=[smem, smem, vmem],
        out_specs=[vmem] * 3,
        out_shape=[
            jax.ShapeDtypeStruct((extent, MOST * extent), jnp.bfloat16),
            jax.ShapeDtypeStruct((MOST * extent, extent), jnp.bfloat16),
            jax.ShapeDtypeStruct(
                (extent // UNIT_ROWS, MOST * UNIT_ROWS, extent), jnp.bfloat16
            ),
        ],
        scratch_shapes=[
            pltpu.VMEM((matrices.shape[0] * matrices.shape[1], extent), jnp.float32),
            pltpu.VMEM((extent, extent), jnp.float32),
        ],
        compiler_params=pltpu.CompilerParams(vmem_limit_bytes=SMALL_VMEM),
    )(sink_counts, weights, matrices)


def group_kernel(first, last, units, per_unit, extent, *refs):
    pieces = len(units) * per_unit
    piece_refs = refs[:pieces]
    leg3_ref, leg2_ref, leg1_ref = refs[pieces : pieces + 3]
    refs = refs[pieces + 3 :]
    if not first:
        acc_ref, refs = refs[0], refs[1:]
    out_ref, turned_ref, outer_ref, across_ref, held_ref, sems = refs[:6]
    a_per = piece_refs[0].shape[0] // extent
    unit_depth = MOST * UNIT_ROWS
    depth = unit_depth * len(units)
    pitch = depth + 8
    step = pl.program_id(0)

    def fetch(piece):
        return pltpu.make_async_copy(piece_refs[piece], held_ref.at[piece], sems.at[piece])

    @pl.when(step == 0)
    def fetch_all():
        for piece in range(pieces):
            if not first:
                fetch(piece).start()

    def inner_legs(piece):
        place, lane = piece // per_unit, piece % per_unit
        if not first:
            fetch(piece).wait()
        rows_ref = piece_refs[piece] if first else held_ref.at[piece]
        sender = (lax.axis_index("work") & (per_unit - 1)) ^ lane
        third = jnp.dot(
            rows_ref[...], leg3_ref[...], preferred_element_type=jnp.float32
        ).astype(jnp.bfloat16)
        for d in range(MOST):
            columns = third[:, d * extent : (d + 1) * extent]
            wide = jnp.concatenate(
                [columns[a * extent : (a + 1) * extent] for a in range(a_per)], axis=1
            )
            second = jnp.dot(
                leg2_ref[d * extent : (d + 1) * extent, :],
                wide,
                preferred_element_type=jnp.float32,
            )
            for a in range(a_per):
                row = place * unit_depth + d * UNIT_ROWS + sender * a_per + a
                turned_ref[pl.ds(row, extent, stride=pitch), :] = second[
                    :, a * extent : (a + 1) * extent
                ]

    @pl.when(step == 0)
    def turn_outer():
        for place, unit in enumerate(units):
            outer_ref[place * unit_depth : (place + 1) * unit_depth, :] = leg1_ref[
                unit
            ].astype(jnp.float32)
        across_ref[...] = outer_ref[...].T.astype(jnp.bfloat16)

    for piece in range(pieces):
        pl.when(step == piece)(functools.partial(inner_legs, piece))

    @pl.when(step >= pieces)
    def outer_leg():
        begin = (step - pieces) * B_BLOCK
        wide = jnp.concatenate(
            [
                turned_ref[pl.ds(pl.multiple_of((begin + b) * pitch, 8), depth), :].astype(
                    jnp.bfloat16
                )
                for b in range(B_BLOCK)
            ],
            axis=1,
        )
        whole = jnp.dot(across_ref[...], wide, preferred_element_type=jnp.float32)
        for b in range(B_BLOCK):
            part = whole[:, b * extent : (b + 1) * extent]
            if not first:
                part = part + acc_ref[b].astype(jnp.float32)
            if last:
                refs[6][pl.ds(b, extent, stride=B_BLOCK + 8), :] = part
            else:
                out_ref[b] = part.astype(out_ref.dtype)
        if last:
            for a in range(extent):
                out_ref[a] = refs[6][pl.ds(a * (B_BLOCK + 8), B_BLOCK), :].astype(jnp.bfloat16)


def add_group(units, pieces, leg3, leg2, leg1, acc, last):
    extent = leg3.shape[0]
    count = len(pieces)
    per_unit = count // len(units)
    depth = MOST * UNIT_ROWS * len(units)
    first = acc is None
    blocks = extent // B_BLOCK

    def whole_spec(x):
        return pl.BlockSpec(x.shape, lambda i: (0,) * x.ndim)

    def block_of(i):
        return jnp.maximum(i - count, 0)

    operands = [*pieces, leg3, leg2, leg1]
    in_specs = [whole_spec(x) for x in operands]
    if not first:
        in_specs[:count] = [pl.BlockSpec(memory_space=pl.ANY)] * count
    if not first:
        operands.append(acc)
        in_specs.append(pl.BlockSpec((B_BLOCK, extent, extent), lambda i: (block_of(i), 0, 0)))
    scratch = [
        pltpu.VMEM((extent * (depth + 8), extent), jnp.float32),
        pltpu.VMEM((depth, extent), jnp.float32),
        pltpu.VMEM((extent, depth), jnp.bfloat16),
        pltpu.VMEM((count, *pieces[0].shape), jnp.bfloat16),
        pltpu.SemaphoreType.DMA((count,)),
    ]
    if last:
        out_shape = jax.ShapeDtypeStruct((extent, extent, extent), jnp.bfloat16)
        out_spec = pl.BlockSpec((extent, B_BLOCK, extent), lambda i: (0, block_of(i), 0))
        scratch.append(pltpu.VMEM((extent * (B_BLOCK + 8), extent), jnp.float32))
    else:
        out_shape = jax.ShapeDtypeStruct((extent, extent, extent), ACC)
        out_spec = pl.BlockSpec((B_BLOCK, extent, extent), lambda i: (block_of(i), 0, 0))
    rows = count * pieces[0].shape[0]
    return pl.pallas_call(
        functools.partial(group_kernel, first, last, units, per_unit, extent),
        grid=(count + blocks,),
        in_specs=in_specs,
        out_specs=out_spec,
        out_shape=out_shape,
        scratch_shapes=scratch,
        compiler_params=pltpu.CompilerParams(
            dimension_semantics=("arbitrary",), vmem_limit_bytes=ROOM + 4 * extent * extent * (depth + 8)
        ),
        cost_estimate=pl.CostEstimate(
            flops=6 * MOST * rows * extent * extent,
            bytes_accessed=12 * extent**3,
            transcendentals=0,
        ),
    )(*operands)


def per_device(sources, perambs, source_ids, peramb_ids, sink_counts, weights):
    workers = lax.axis_size("work")
    extent = sources.shape[2]
    per_unit = UNIT_ROWS * workers // extent
    half = workers // 2
    far = list(range(half, workers))
    upper, lower = list(range(half // 2, half)), list(range(2, half // 2))
    near = [1, *upper, *lower]
    order = []
    while far or near:
        take_far = far and (not near or len(order) in FAR_TURNS)
        order.append(far.pop(0) if take_far else near.pop(0))
    early, late = tuple(order[:IN_FLIGHT]), (0, *order[IN_FLIGHT:])
    pieces = dict(zip(early, choose_pieces(sources, source_ids, early)))
    pieces.update(zip(late, choose_pieces(sources, source_ids, late)))
    arrived = {0: pieces[0]}

    def send(place):
        shift = order[place]
        piece = pieces[shift]
        if place >= IN_FLIGHT:
            before = order[place - IN_FLIGHT]
            piece, arrived[before] = lax.optimization_barrier((piece, arrived[before]))
        arrived[shift] = lax.ppermute(piece, "work", [(i, i ^ shift) for i in range(workers)])

    for place in range(IN_FLIGHT):
        send(place)
    matrices = choose_matrices(perambs, peramb_ids, sink_counts, workers, extent)
    matrices = lax.all_to_all(matrices, "work", split_axis=0, concat_axis=0, tiled=True)
    leg3, leg2, leg1 = make_legs(matrices, sink_counts, weights, workers)
    for place in range(IN_FLIGHT, len(order) - HELD_BACK):
        send(place)

    acc = None
    for group, units in enumerate(GROUPS):
        members = [arrived[u * per_unit + lane] for u in units for lane in range(per_unit)]
        acc = add_group(units, members, leg3, leg2, leg1, acc, group == len(GROUPS) - 1)
        if group == 0:
            for place in range(len(order) - HELD_BACK, len(order)):
                shift = order[place]
                pieces[shift], acc = lax.optimization_barrier((pieces[shift], acc))
                send(place)
    return acc.reshape(1, extent * extent, extent)


def solution(mesh):
    return jax.shard_map(
        per_device,
        mesh=mesh,
        in_specs=(P("cfg", "work", None), P("cfg", "work"), P(), P(), P(), P()),
        out_specs=P(("cfg", "work"), None, None),
        check_vma=False,
    )
```

```python
import functools

import jax
import jax.numpy as jnp
from jax import lax
from jax.experimental import pallas as pl
from jax.experimental.pallas import tpu as pltpu
from jax.sharding import PartitionSpec as P

MOST = 6
LEGS = 3
UNIT_ROWS = 16
B_BLOCK = 64
ACC = jnp.bfloat16
GROUPS = ((0, 2, 4), (3, 5), (1, 6), (7,))
IN_FLIGHT = 5
FAR_TURNS = (2, 4)
SMALL_VMEM = 16 * 1024 * 1024
ROOM = 13 * 1024 * 1024
FIRST_VMEM = 60 * 1024 * 1024


def pieces_kernel(shifts, ids_ref, source_ref, *refs):
    piece_refs, (held_ref, in_sems, out_sems) = refs[: len(shifts)], refs[len(shifts) :]
    own = lax.axis_index("work")
    reads, writes = [], []
    for i, shift in enumerate(shifts):
        reads.append(
            pltpu.make_async_copy(
                source_ref.at[ids_ref[own ^ shift]], held_ref.at[i], in_sems.at[i]
            )
        )
        writes.append(pltpu.make_async_copy(held_ref.at[i], piece_refs[i], out_sems.at[i]))
        reads[i].start()
    for read, write in zip(reads, writes):
        read.wait()
        write.start()
    for write in writes:
        write.wait()


def choose_pieces(sources, source_ids, shifts):
    return pl.pallas_call(
        functools.partial(pieces_kernel, shifts),
        in_specs=[pl.BlockSpec(memory_space=pltpu.SMEM), pl.BlockSpec(memory_space=pl.ANY)],
        out_specs=[pl.BlockSpec(memory_space=pl.ANY)] * len(shifts),
        out_shape=[jax.ShapeDtypeStruct(sources.shape[1:], sources.dtype)] * len(shifts),
        scratch_shapes=[
            pltpu.VMEM((len(shifts), *sources.shape[1:]), sources.dtype),
            pltpu.SemaphoreType.DMA((len(shifts),)),
            pltpu.SemaphoreType.DMA((len(shifts),)),
        ],
        compiler_params=pltpu.CompilerParams(vmem_limit_bytes=SMALL_VMEM),
    )(source_ids, sources)


def matrices_kernel(workers, counts_ref, matrix_ids_ref, peramb_ref, matrix_ref, choice_ref, spread_ref):
    rows = MOST * LEGS
    diagrams = matrix_ids_ref.shape[1]
    total = peramb_ref.shape[0]
    lanes = lax.broadcasted_iota(jnp.int32, (1, total), 1)

    def mark(sink, start):
        for slot in range(MOST):
            diagram = jnp.minimum(start + slot, diagrams - 1)
            for leg in range(LEGS):
                choice_ref[pl.ds(sink * rows + slot * LEGS + leg, 1), :] = jnp.where(
                    lanes == matrix_ids_ref[leg, diagram], 1.0, 0.0
                )
        return start + counts_ref[sink]

    lax.fori_loop(0, workers, mark, 0)
    chosen = jnp.dot(
        choice_ref[...].astype(jnp.bfloat16), peramb_ref[...], preferred_element_type=jnp.float32
    )
    extent = matrix_ref.shape[2]
    a_per = peramb_ref.shape[1] // extent
    for row in range(a_per):
        spread_ref[pl.ds(row, workers * rows, stride=a_per), :] = chosen[
            :, row * extent : (row + 1) * extent
        ]
    matrix_ref[...] = spread_ref[...].reshape(matrix_ref.shape).astype(jnp.bfloat16)


def choose_matrices(perambs, peramb_ids, sink_counts, workers, extent):
    rows = MOST * LEGS
    a_per = perambs.shape[1] // extent
    smem = pl.BlockSpec(memory_space=pltpu.SMEM)
    vmem = pl.BlockSpec(memory_space=pltpu.VMEM)
    return pl.pallas_call(
        functools.partial(matrices_kernel, workers),
        in_specs=[smem, smem, vmem],
        out_specs=vmem,
        out_shape=jax.ShapeDtypeStruct((workers, rows * a_per, extent), jnp.bfloat16),
        scratch_shapes=[
            pltpu.VMEM((workers * rows, perambs.shape[0]), jnp.float32),
            pltpu.VMEM((workers * rows * a_per, extent), jnp.float32),
        ],
        compiler_params=pltpu.CompilerParams(vmem_limit_bytes=SMALL_VMEM),
    )(sink_counts, peramb_ids.T, perambs)


def legs_kernel(
    workers, counts_ref, weights_ref, matrix_ref, leg3_ref, leg2_ref, leg1_ref, flat_ref, leg_ref
):
    extent = matrix_ref.shape[2]
    rows = MOST * LEGS
    a_per = matrix_ref.shape[1] // rows
    flat_ref[...] = matrix_ref[...].astype(jnp.float32).reshape(flat_ref.shape)
    own = lax.axis_index("work")
    start = lax.fori_loop(0, own, lambda i, total: total + counts_ref[i], 0)
    count = counts_ref[own]
    unit = UNIT_ROWS // a_per
    units = workers // unit
    for slot in range(MOST):
        for leg in range(LEGS):
            base = (slot * LEGS + leg) * a_per
            for row in range(a_per):
                leg_ref[pl.ds(row, workers, stride=a_per), :] = flat_ref[
                    pl.ds(base + row, workers, stride=rows * a_per), :
                ]
            if leg == 2:
                leg3_ref[:, slot * extent : (slot + 1) * extent] = leg_ref[...].T.astype(
                    jnp.bfloat16
                )
            elif leg == 1:
                leg2_ref[slot * extent : (slot + 1) * extent, :] = leg_ref[...].astype(
                    jnp.bfloat16
                )
            else:
                diagram = jnp.minimum(start + slot, weights_ref.shape[0] - 1)
                factor = jnp.where(slot < count, weights_ref[diagram], 0.0)
                leg_ref[...] = (factor * leg_ref[...]).T
                for block in range(units):
                    place = (own // unit) ^ block
                    leg1_ref[block, slot * UNIT_ROWS : (slot + 1) * UNIT_ROWS, :] = leg_ref[
                        pl.ds(pl.multiple_of(place * UNIT_ROWS, UNIT_ROWS), UNIT_ROWS), :
                    ].astype(jnp.bfloat16)


def make_legs(matrices, sink_counts, weights, workers):
    extent = matrices.shape[2]
    a_per = extent // workers
    smem = pl.BlockSpec(memory_space=pltpu.SMEM)
    vmem = pl.BlockSpec(memory_space=pltpu.VMEM)
    return pl.pallas_call(
        functools.partial(legs_kernel, workers),
        in_specs=[smem, smem, vmem],
        out_specs=[vmem] * 3,
        out_shape=[
            jax.ShapeDtypeStruct((extent, MOST * extent), jnp.bfloat16),
            jax.ShapeDtypeStruct((MOST * extent, extent), jnp.bfloat16),
            jax.ShapeDtypeStruct(
                (extent // UNIT_ROWS, MOST * UNIT_ROWS, extent), jnp.bfloat16
            ),
        ],
        scratch_shapes=[
            pltpu.VMEM((matrices.shape[0] * matrices.shape[1], extent), jnp.float32),
            pltpu.VMEM((extent, extent), jnp.float32),
        ],
        compiler_params=pltpu.CompilerParams(vmem_limit_bytes=SMALL_VMEM),
    )(sink_counts, weights, matrices)


def group_kernel(first, last, units, per_unit, extent, *refs):
    pieces = len(units) * per_unit
    piece_refs = refs[:pieces]
    leg3_ref, leg2_ref, leg1_ref = refs[pieces : pieces + 3]
    refs = refs[pieces + 3 :]
    if not first:
        acc_ref, refs = refs[0], refs[1:]
    out_ref, turned_ref, outer_ref, across_ref, held_ref, sems = refs[:6]
    a_per = piece_refs[0].shape[0] // extent
    unit_depth = MOST * UNIT_ROWS
    depth = unit_depth * len(units)
    pitch = depth + 8
    step = pl.program_id(0)

    def fetch(piece):
        return pltpu.make_async_copy(piece_refs[piece], held_ref.at[piece], sems.at[piece])

    @pl.when(step == 0)
    def fetch_all():
        for piece in range(pieces):
            if not first:
                fetch(piece).start()

    def inner_legs(piece):
        place, lane = piece // per_unit, piece % per_unit
        if not first:
            fetch(piece).wait()
        rows_ref = piece_refs[piece] if first else held_ref.at[piece]
        sender = (lax.axis_index("work") & (per_unit - 1)) ^ lane
        third = jnp.dot(
            rows_ref[...], leg3_ref[...], preferred_element_type=jnp.float32
        ).astype(jnp.bfloat16)
        for d in range(MOST):
            columns = third[:, d * extent : (d + 1) * extent]
            wide = jnp.concatenate(
                [columns[a * extent : (a + 1) * extent] for a in range(a_per)], axis=1
            )
            second = jnp.dot(
                leg2_ref[d * extent : (d + 1) * extent, :],
                wide,
                preferred_element_type=jnp.float32,
            )
            for a in range(a_per):
                row = place * unit_depth + d * UNIT_ROWS + sender * a_per + a
                turned_ref[pl.ds(row, extent, stride=pitch), :] = second[
                    :, a * extent : (a + 1) * extent
                ]

    @pl.when(step == 0)
    def turn_outer():
        for place, unit in enumerate(units):
            outer_ref[place * unit_depth : (place + 1) * unit_depth, :] = leg1_ref[
                unit
            ].astype(jnp.float32)
        across_ref[...] = outer_ref[...].T.astype(jnp.bfloat16)

    for piece in range(pieces):
        pl.when(step == piece)(functools.partial(inner_legs, piece))

    @pl.when(step >= pieces)
    def outer_leg():
        begin = (step - pieces) * B_BLOCK
        wide = jnp.concatenate(
            [
                turned_ref[pl.ds(pl.multiple_of((begin + b) * pitch, 8), depth), :].astype(
                    jnp.bfloat16
                )
                for b in range(B_BLOCK)
            ],
            axis=1,
        )
        whole = jnp.dot(across_ref[...], wide, preferred_element_type=jnp.float32)
        for b in range(B_BLOCK):
            part = whole[:, b * extent : (b + 1) * extent]
            if not first:
                part = part + acc_ref[b].astype(jnp.float32)
            if last:
                refs[6][pl.ds(b, extent, stride=B_BLOCK + 8), :] = part
            else:
                out_ref[b] = part.astype(out_ref.dtype)
        if last:
            for a in range(extent):
                out_ref[a] = refs[6][pl.ds(a * (B_BLOCK + 8), B_BLOCK), :].astype(jnp.bfloat16)


def add_group(units, pieces, leg3, leg2, leg1, acc, last):
    extent = leg3.shape[0]
    count = len(pieces)
    per_unit = count // len(units)
    depth = MOST * UNIT_ROWS * len(units)
    first = acc is None
    blocks = extent // B_BLOCK

    def whole_spec(x):
        return pl.BlockSpec(x.shape, lambda i: (0,) * x.ndim)

    def block_of(i):
        return jnp.maximum(i - count, 0)

    operands = [*pieces, leg3, leg2, leg1]
    in_specs = [whole_spec(x) for x in operands]
    if not first:
        in_specs[:count] = [pl.BlockSpec(memory_space=pl.ANY)] * count
    if not first:
        operands.append(acc)
        in_specs.append(pl.BlockSpec((B_BLOCK, extent, extent), lambda i: (block_of(i), 0, 0)))
    scratch = [
        pltpu.VMEM((extent * (depth + 8), extent), jnp.float32),
        pltpu.VMEM((depth, extent), jnp.float32),
        pltpu.VMEM((extent, depth), jnp.bfloat16),
        pltpu.VMEM((count, *pieces[0].shape), jnp.bfloat16),
        pltpu.SemaphoreType.DMA((count,)),
    ]
    if last:
        out_shape = jax.ShapeDtypeStruct((extent, extent, extent), jnp.bfloat16)
        out_spec = pl.BlockSpec((extent, B_BLOCK, extent), lambda i: (0, block_of(i), 0))
        scratch.append(pltpu.VMEM((extent * (B_BLOCK + 8), extent), jnp.float32))
    else:
        out_shape = jax.ShapeDtypeStruct((extent, extent, extent), ACC)
        out_spec = pl.BlockSpec((B_BLOCK, extent, extent), lambda i: (block_of(i), 0, 0))
    rows = count * pieces[0].shape[0]
    return pl.pallas_call(
        functools.partial(group_kernel, first, last, units, per_unit, extent),
        grid=(count + blocks,),
        in_specs=in_specs,
        out_specs=out_spec,
        out_shape=out_shape,
        scratch_shapes=scratch,
        compiler_params=pltpu.CompilerParams(
            dimension_semantics=("arbitrary",), vmem_limit_bytes=FIRST_VMEM if first else ROOM + 4 * extent * extent * (depth + 8)
        ),
        cost_estimate=pl.CostEstimate(
            flops=6 * MOST * rows * extent * extent,
            bytes_accessed=12 * extent**3,
            transcendentals=0,
        ),
    )(*operands)


def per_device(sources, perambs, source_ids, peramb_ids, sink_counts, weights):
    workers = lax.axis_size("work")
    extent = sources.shape[2]
    per_unit = UNIT_ROWS * workers // extent
    half = workers // 2
    far = list(range(half, workers))
    near = [s for pair in zip(range(half // 2), range(half // 2, half)) for s in pair][1:]
    near = [1, *(s for s in near if s != 1)]
    order = []
    while far or near:
        take_far = far and (not near or len(order) % IN_FLIGHT in FAR_TURNS)
        order.append(far.pop(0) if take_far else near.pop(0))
    early, late = tuple(order[:IN_FLIGHT]), (0, *order[IN_FLIGHT:])
    pieces = dict(zip(early, choose_pieces(sources, source_ids, early)))
    pieces.update(zip(late, choose_pieces(sources, source_ids, late)))
    arrived = {0: pieces[0]}

    def send(place):
        shift = order[place]
        piece = pieces[shift]
        if place >= IN_FLIGHT:
            before = order[place - IN_FLIGHT]
            piece, arrived[before] = lax.optimization_barrier((piece, arrived[before]))
        arrived[shift] = lax.ppermute(piece, "work", [(i, i ^ shift) for i in range(workers)])

    for place in range(IN_FLIGHT):
        send(place)
    matrices = choose_matrices(perambs, peramb_ids, sink_counts, workers, extent)
    matrices = lax.all_to_all(matrices, "work", split_axis=0, concat_axis=0, tiled=True)
    leg3, leg2, leg1 = make_legs(matrices, sink_counts, weights, workers)
    for place in range(IN_FLIGHT, len(order)):
        send(place)

    acc = None
    for group, units in enumerate(GROUPS):
        members = [arrived[u * per_unit + lane] for u in units for lane in range(per_unit)]
        acc = add_group(units, members, leg3, leg2, leg1, acc, group == len(GROUPS) - 1)
    return acc.reshape(1, extent * extent, extent)


def solution(mesh):
    return jax.shard_map(
        per_device,
        mesh=mesh,
        in_specs=(P("cfg", "work", None), P("cfg", "work"), P(), P(), P(), P()),
        out_specs=P(("cfg", "work"), None, None),
        check_vma=False,
    )
```

```python
import functools

import jax
import jax.numpy as jnp
from jax import lax
from jax.experimental import pallas as pl
from jax.experimental.pallas import tpu as pltpu
from jax.sharding import PartitionSpec as P

MOST = 6
LEGS = 3
UNIT_ROWS = 16
B_BLOCK = 64
ACC = jnp.bfloat16
GROUPS = ((0, 2, 4), (3, 5), (1, 6), (7,))
IN_FLIGHT = 5
FAR_TURNS = (2, 4)
SMALL_VMEM = 16 * 1024 * 1024
ROOM = 13 * 1024 * 1024


def pieces_kernel(shifts, ids_ref, source_ref, *refs):
    piece_refs, (held_ref, in_sems, out_sems) = refs[: len(shifts)], refs[len(shifts) :]
    own = lax.axis_index("work")
    reads, writes = [], []
    for i, shift in enumerate(shifts):
        reads.append(
            pltpu.make_async_copy(
                source_ref.at[ids_ref[own ^ shift]], held_ref.at[i], in_sems.at[i]
            )
        )
        writes.append(pltpu.make_async_copy(held_ref.at[i], piece_refs[i], out_sems.at[i]))
        reads[i].start()
    for read, write in zip(reads, writes):
        read.wait()
        write.start()
    for write in writes:
        write.wait()


def choose_pieces(sources, source_ids, shifts):
    return pl.pallas_call(
        functools.partial(pieces_kernel, shifts),
        in_specs=[pl.BlockSpec(memory_space=pltpu.SMEM), pl.BlockSpec(memory_space=pl.ANY)],
        out_specs=[pl.BlockSpec(memory_space=pl.ANY)] * len(shifts),
        out_shape=[jax.ShapeDtypeStruct(sources.shape[1:], sources.dtype)] * len(shifts),
        scratch_shapes=[
            pltpu.VMEM((len(shifts), *sources.shape[1:]), sources.dtype),
            pltpu.SemaphoreType.DMA((len(shifts),)),
            pltpu.SemaphoreType.DMA((len(shifts),)),
        ],
        compiler_params=pltpu.CompilerParams(vmem_limit_bytes=SMALL_VMEM),
    )(source_ids, sources)


def matrices_kernel(workers, counts_ref, matrix_ids_ref, peramb_ref, matrix_ref, choice_ref, spread_ref):
    rows = MOST * LEGS
    diagrams = matrix_ids_ref.shape[1]
    total = peramb_ref.shape[0]
    lanes = lax.broadcasted_iota(jnp.int32, (1, total), 1)

    def mark(sink, start):
        for slot in range(MOST):
            diagram = jnp.minimum(start + slot, diagrams - 1)
            for leg in range(LEGS):
                choice_ref[pl.ds(sink * rows + slot * LEGS + leg, 1), :] = jnp.where(
                    lanes == matrix_ids_ref[leg, diagram], 1.0, 0.0
                )
        return start + counts_ref[sink]

    lax.fori_loop(0, workers, mark, 0)
    chosen = jnp.dot(
        choice_ref[...].astype(jnp.bfloat16), peramb_ref[...], preferred_element_type=jnp.float32
    )
    extent = matrix_ref.shape[2]
    a_per = peramb_ref.shape[1] // extent
    for row in range(a_per):
        spread_ref[pl.ds(row, workers * rows, stride=a_per), :] = chosen[
            :, row * extent : (row + 1) * extent
        ]
    matrix_ref[...] = spread_ref[...].reshape(matrix_ref.shape).astype(jnp.bfloat16)


def choose_matrices(perambs, peramb_ids, sink_counts, workers, extent):
    rows = MOST * LEGS
    a_per = perambs.shape[1] // extent
    smem = pl.BlockSpec(memory_space=pltpu.SMEM)
    vmem = pl.BlockSpec(memory_space=pltpu.VMEM)
    return pl.pallas_call(
        functools.partial(matrices_kernel, workers),
        in_specs=[smem, smem, vmem],
        out_specs=vmem,
        out_shape=jax.ShapeDtypeStruct((workers, rows * a_per, extent), jnp.bfloat16),
        scratch_shapes=[
            pltpu.VMEM((workers * rows, perambs.shape[0]), jnp.float32),
            pltpu.VMEM((workers * rows * a_per, extent), jnp.float32),
        ],
        compiler_params=pltpu.CompilerParams(vmem_limit_bytes=SMALL_VMEM),
    )(sink_counts, peramb_ids.T, perambs)


def legs_kernel(
    workers, counts_ref, weights_ref, matrix_ref, leg3_ref, leg2_ref, leg1_ref, flat_ref, leg_ref
):
    extent = matrix_ref.shape[2]
    rows = MOST * LEGS
    a_per = matrix_ref.shape[1] // rows
    flat_ref[...] = matrix_ref[...].astype(jnp.float32).reshape(flat_ref.shape)
    own = lax.axis_index("work")
    start = lax.fori_loop(0, own, lambda i, total: total + counts_ref[i], 0)
    count = counts_ref[own]
    unit = UNIT_ROWS // a_per
    units = workers // unit
    for slot in range(MOST):
        for leg in range(LEGS):
            base = (slot * LEGS + leg) * a_per
            for row in range(a_per):
                leg_ref[pl.ds(row, workers, stride=a_per), :] = flat_ref[
                    pl.ds(base + row, workers, stride=rows * a_per), :
                ]
            if leg == 2:
                leg3_ref[:, slot * extent : (slot + 1) * extent] = leg_ref[...].T.astype(
                    jnp.bfloat16
                )
            elif leg == 1:
                leg2_ref[slot * extent : (slot + 1) * extent, :] = leg_ref[...].astype(
                    jnp.bfloat16
                )
            else:
                diagram = jnp.minimum(start + slot, weights_ref.shape[0] - 1)
                factor = jnp.where(slot < count, weights_ref[diagram], 0.0)
                leg_ref[...] = (factor * leg_ref[...]).T
                for block in range(units):
                    place = (own // unit) ^ block
                    leg1_ref[block, slot * UNIT_ROWS : (slot + 1) * UNIT_ROWS, :] = leg_ref[
                        pl.ds(pl.multiple_of(place * UNIT_ROWS, UNIT_ROWS), UNIT_ROWS), :
                    ].astype(jnp.bfloat16)


def make_legs(matrices, sink_counts, weights, workers):
    extent = matrices.shape[2]
    a_per = extent // workers
    smem = pl.BlockSpec(memory_space=pltpu.SMEM)
    vmem = pl.BlockSpec(memory_space=pltpu.VMEM)
    return pl.pallas_call(
        functools.partial(legs_kernel, workers),
        in_specs=[smem, smem, vmem],
        out_specs=[vmem] * 3,
        out_shape=[
            jax.ShapeDtypeStruct((extent, MOST * extent), jnp.bfloat16),
            jax.ShapeDtypeStruct((MOST * extent, extent), jnp.bfloat16),
            jax.ShapeDtypeStruct(
                (extent // UNIT_ROWS, MOST * UNIT_ROWS, extent), jnp.bfloat16
            ),
        ],
        scratch_shapes=[
            pltpu.VMEM((matrices.shape[0] * matrices.shape[1], extent), jnp.float32),
            pltpu.VMEM((extent, extent), jnp.float32),
        ],
        compiler_params=pltpu.CompilerParams(vmem_limit_bytes=SMALL_VMEM),
    )(sink_counts, weights, matrices)


def group_kernel(first, last, units, per_unit, extent, *refs):
    pieces = len(units) * per_unit
    piece_refs = refs[:pieces]
    leg3_ref, leg2_ref, leg1_ref = refs[pieces : pieces + 3]
    refs = refs[pieces + 3 :]
    if not first:
        acc_ref, refs = refs[0], refs[1:]
    out_ref, turned_ref, outer_ref, across_ref, held_ref, sems = refs[:6]
    a_per = piece_refs[0].shape[0] // extent
    unit_depth = MOST * UNIT_ROWS
    depth = unit_depth * len(units)
    pitch = depth + 8
    step = pl.program_id(0)

    def fetch(piece):
        return pltpu.make_async_copy(piece_refs[piece], held_ref.at[piece], sems.at[piece])

    @pl.when(step == 0)
    def fetch_all():
        for piece in range(pieces):
            if not first:
                fetch(piece).start()

    def inner_legs(piece):
        place, lane = piece // per_unit, piece % per_unit
        if not first:
            fetch(piece).wait()
        rows_ref = piece_refs[piece] if first else held_ref.at[piece]
        sender = (lax.axis_index("work") & (per_unit - 1)) ^ lane
        third = jnp.dot(
            rows_ref[...], leg3_ref[...], preferred_element_type=jnp.float32
        ).astype(jnp.bfloat16)
        for d in range(MOST):
            columns = third[:, d * extent : (d + 1) * extent]
            wide = jnp.concatenate(
                [columns[a * extent : (a + 1) * extent] for a in range(a_per)], axis=1
            )
            second = jnp.dot(
                leg2_ref[d * extent : (d + 1) * extent, :],
                wide,
                preferred_element_type=jnp.float32,
            )
            for a in range(a_per):
                row = place * unit_depth + d * UNIT_ROWS + sender * a_per + a
                turned_ref[pl.ds(row, extent, stride=pitch), :] = second[
                    :, a * extent : (a + 1) * extent
                ]

    @pl.when(step == 0)
    def turn_outer():
        for place, unit in enumerate(units):
            outer_ref[place * unit_depth : (place + 1) * unit_depth, :] = leg1_ref[
                unit
            ].astype(jnp.float32)
        across_ref[...] = outer_ref[...].T.astype(jnp.bfloat16)

    for piece in range(pieces):
        pl.when(step == piece)(functools.partial(inner_legs, piece))

    @pl.when(step >= pieces)
    def outer_leg():
        begin = (step - pieces) * B_BLOCK
        wide = jnp.concatenate(
            [
                turned_ref[pl.ds(pl.multiple_of((begin + b) * pitch, 8), depth), :].astype(
                    jnp.bfloat16
                )
                for b in range(B_BLOCK)
            ],
            axis=1,
        )
        whole = jnp.dot(across_ref[...], wide, preferred_element_type=jnp.float32)
        for b in range(B_BLOCK):
            part = whole[:, b * extent : (b + 1) * extent]
            if not first:
                part = part + acc_ref[b].astype(jnp.float32)
            if last:
                refs[6][pl.ds(b, extent, stride=B_BLOCK + 8), :] = part
            else:
                out_ref[b] = part.astype(out_ref.dtype)
        if last:
            for a in range(extent):
                out_ref[a] = refs[6][pl.ds(a * (B_BLOCK + 8), B_BLOCK), :].astype(jnp.bfloat16)


def add_group(units, pieces, leg3, leg2, leg1, acc, last):
    extent = leg3.shape[0]
    count = len(pieces)
    per_unit = count // len(units)
    depth = MOST * UNIT_ROWS * len(units)
    first = acc is None
    blocks = extent // B_BLOCK

    def whole_spec(x):
        return pl.BlockSpec(x.shape, lambda i: (0,) * x.ndim)

    def block_of(i):
        return jnp.maximum(i - count, 0)

    operands = [*pieces, leg3, leg2, leg1]
    in_specs = [whole_spec(x) for x in operands]
    if not first:
        in_specs[:count] = [pl.BlockSpec(memory_space=pl.ANY)] * count
    if not first:
        operands.append(acc)
        in_specs.append(pl.BlockSpec((B_BLOCK, extent, extent), lambda i: (block_of(i), 0, 0)))
    scratch = [
        pltpu.VMEM((extent * (depth + 8), extent), jnp.float32),
        pltpu.VMEM((depth, extent), jnp.float32),
        pltpu.VMEM((extent, depth), jnp.bfloat16),
        pltpu.VMEM((count, *pieces[0].shape), jnp.bfloat16),
        pltpu.SemaphoreType.DMA((count,)),
    ]
    if last:
        out_shape = jax.ShapeDtypeStruct((extent, extent, extent), jnp.bfloat16)
        out_spec = pl.BlockSpec((extent, B_BLOCK, extent), lambda i: (0, block_of(i), 0))
        scratch.append(pltpu.VMEM((extent * (B_BLOCK + 8), extent), jnp.float32))
    else:
        out_shape = jax.ShapeDtypeStruct((extent, extent, extent), ACC)
        out_spec = pl.BlockSpec((B_BLOCK, extent, extent), lambda i: (block_of(i), 0, 0))
    rows = count * pieces[0].shape[0]
    return pl.pallas_call(
        functools.partial(group_kernel, first, last, units, per_unit, extent),
        grid=(count + blocks,),
        in_specs=in_specs,
        out_specs=out_spec,
        out_shape=out_shape,
        scratch_shapes=scratch,
        compiler_params=pltpu.CompilerParams(
            dimension_semantics=("arbitrary",), vmem_limit_bytes=ROOM + 4 * extent * extent * (depth + 8)
        ),
        cost_estimate=pl.CostEstimate(
            flops=6 * MOST * rows * extent * extent,
            bytes_accessed=12 * extent**3,
            transcendentals=0,
        ),
    )(*operands)


def per_device(sources, perambs, source_ids, peramb_ids, sink_counts, weights):
    workers = lax.axis_size("work")
    extent = sources.shape[2]
    per_unit = UNIT_ROWS * workers // extent
    half = workers // 2
    far = list(range(half, workers))
    near = [s for pair in zip(range(half // 2), range(half // 2, half)) for s in pair][1:]
    near = [1, *(s for s in near if s != 1)]
    order = []
    while far or near:
        take_far = far and (not near or len(order) % IN_FLIGHT in FAR_TURNS)
        order.append(far.pop(0) if take_far else near.pop(0))
    early, late = tuple(order[:IN_FLIGHT]), (0, *order[IN_FLIGHT:])
    pieces = dict(zip(early, choose_pieces(sources, source_ids, early)))
    pieces.update(zip(late, choose_pieces(sources, source_ids, late)))
    arrived = {0: pieces[0]}

    def send(place):
        shift = order[place]
        piece = pieces[shift]
        if place >= IN_FLIGHT:
            before = order[place - IN_FLIGHT]
            piece, arrived[before] = lax.optimization_barrier((piece, arrived[before]))
        arrived[shift] = lax.ppermute(piece, "work", [(i, i ^ shift) for i in range(workers)])

    for place in range(IN_FLIGHT):
        send(place)
    matrices = choose_matrices(perambs, peramb_ids, sink_counts, workers, extent)
    matrices = lax.all_to_all(matrices, "work", split_axis=0, concat_axis=0, tiled=True)
    leg3, leg2, leg1 = make_legs(matrices, sink_counts, weights, workers)
    for place in range(IN_FLIGHT, len(order) - 1):
        send(place)

    acc = None
    for group, units in enumerate(GROUPS):
        members = [arrived[u * per_unit + lane] for u in units for lane in range(per_unit)]
        acc = add_group(units, members, leg3, leg2, leg1, acc, group == len(GROUPS) - 1)
        if group == 0:
            pieces[order[-1]], acc = lax.optimization_barrier((pieces[order[-1]], acc))
            send(len(order) - 1)
    return acc.reshape(1, extent * extent, extent)


def solution(mesh):
    return jax.shard_map(
        per_device,
        mesh=mesh,
        in_specs=(P("cfg", "work", None), P("cfg", "work"), P(), P(), P(), P()),
        out_specs=P(("cfg", "work"), None, None),
        check_vma=False,
    )
```

```python
import functools

import jax
import jax.numpy as jnp
from jax import lax
from jax.experimental import pallas as pl
from jax.experimental.pallas import tpu as pltpu
from jax.sharding import PartitionSpec as P

MOST = 6
LEGS = 3
UNIT_ROWS = 16
B_BLOCK = 64
ACC = jnp.bfloat16
GROUPS = ((0, 2, 4), (1, 3, 5), (6,), (7,))
IN_FLIGHT = 5
FAR_TURNS = (2, 4)
SMALL_VMEM = 16 * 1024 * 1024
ROOM = 13 * 1024 * 1024


def pieces_kernel(shifts, ids_ref, source_ref, *refs):
    piece_refs, (held_ref, in_sems, out_sems) = refs[: len(shifts)], refs[len(shifts) :]
    own = lax.axis_index("work")
    reads, writes = [], []
    for i, shift in enumerate(shifts):
        reads.append(
            pltpu.make_async_copy(
                source_ref.at[ids_ref[own ^ shift]], held_ref.at[i], in_sems.at[i]
            )
        )
        writes.append(pltpu.make_async_copy(held_ref.at[i], piece_refs[i], out_sems.at[i]))
        reads[i].start()
    for read, write in zip(reads, writes):
        read.wait()
        write.start()
    for write in writes:
        write.wait()


def choose_pieces(sources, source_ids, shifts):
    return pl.pallas_call(
        functools.partial(pieces_kernel, shifts),
        in_specs=[pl.BlockSpec(memory_space=pltpu.SMEM), pl.BlockSpec(memory_space=pl.ANY)],
        out_specs=[pl.BlockSpec(memory_space=pl.ANY)] * len(shifts),
        out_shape=[jax.ShapeDtypeStruct(sources.shape[1:], sources.dtype)] * len(shifts),
        scratch_shapes=[
            pltpu.VMEM((len(shifts), *sources.shape[1:]), sources.dtype),
            pltpu.SemaphoreType.DMA((len(shifts),)),
            pltpu.SemaphoreType.DMA((len(shifts),)),
        ],
        compiler_params=pltpu.CompilerParams(vmem_limit_bytes=SMALL_VMEM),
    )(source_ids, sources)


def matrices_kernel(workers, counts_ref, matrix_ids_ref, peramb_ref, matrix_ref, choice_ref, spread_ref):
    rows = MOST * LEGS
    diagrams = matrix_ids_ref.shape[1]
    total = peramb_ref.shape[0]
    lanes = lax.broadcasted_iota(jnp.int32, (1, total), 1)

    def mark(sink, start):
        for slot in range(MOST):
            diagram = jnp.minimum(start + slot, diagrams - 1)
            for leg in range(LEGS):
                choice_ref[pl.ds(sink * rows + slot * LEGS + leg, 1), :] = jnp.where(
                    lanes == matrix_ids_ref[leg, diagram], 1.0, 0.0
                )
        return start + counts_ref[sink]

    lax.fori_loop(0, workers, mark, 0)
    chosen = jnp.dot(
        choice_ref[...].astype(jnp.bfloat16), peramb_ref[...], preferred_element_type=jnp.float32
    )
    extent = matrix_ref.shape[2]
    a_per = peramb_ref.shape[1] // extent
    for row in range(a_per):
        spread_ref[pl.ds(row, workers * rows, stride=a_per), :] = chosen[
            :, row * extent : (row + 1) * extent
        ]
    matrix_ref[...] = spread_ref[...].reshape(matrix_ref.shape).astype(jnp.bfloat16)


def choose_matrices(perambs, peramb_ids, sink_counts, workers, extent):
    rows = MOST * LEGS
    a_per = perambs.shape[1] // extent
    smem = pl.BlockSpec(memory_space=pltpu.SMEM)
    vmem = pl.BlockSpec(memory_space=pltpu.VMEM)
    return pl.pallas_call(
        functools.partial(matrices_kernel, workers),
        in_specs=[smem, smem, vmem],
        out_specs=vmem,
        out_shape=jax.ShapeDtypeStruct((workers, rows * a_per, extent), jnp.bfloat16),
        scratch_shapes=[
            pltpu.VMEM((workers * rows, perambs.shape[0]), jnp.float32),
            pltpu.VMEM((workers * rows * a_per, extent), jnp.float32),
        ],
        compiler_params=pltpu.CompilerParams(vmem_limit_bytes=SMALL_VMEM),
    )(sink_counts, peramb_ids.T, perambs)


def legs_kernel(
    workers, counts_ref, weights_ref, matrix_ref, leg3_ref, leg2_ref, leg1_ref, flat_ref, leg_ref
):
    extent = matrix_ref.shape[2]
    rows = MOST * LEGS
    a_per = matrix_ref.shape[1] // rows
    flat_ref[...] = matrix_ref[...].astype(jnp.float32).reshape(flat_ref.shape)
    own = lax.axis_index("work")
    start = lax.fori_loop(0, own, lambda i, total: total + counts_ref[i], 0)
    count = counts_ref[own]
    unit = UNIT_ROWS // a_per
    units = workers // unit
    for slot in range(MOST):
        for leg in range(LEGS):
            base = (slot * LEGS + leg) * a_per
            for row in range(a_per):
                leg_ref[pl.ds(row, workers, stride=a_per), :] = flat_ref[
                    pl.ds(base + row, workers, stride=rows * a_per), :
                ]
            if leg == 2:
                leg3_ref[:, slot * extent : (slot + 1) * extent] = leg_ref[...].T.astype(
                    jnp.bfloat16
                )
            elif leg == 1:
                leg2_ref[slot * extent : (slot + 1) * extent, :] = leg_ref[...].astype(
                    jnp.bfloat16
                )
            else:
                diagram = jnp.minimum(start + slot, weights_ref.shape[0] - 1)
                factor = jnp.where(slot < count, weights_ref[diagram], 0.0)
                leg_ref[...] = (factor * leg_ref[...]).T
                for block in range(units):
                    place = (own // unit) ^ block
                    leg1_ref[block, slot * UNIT_ROWS : (slot + 1) * UNIT_ROWS, :] = leg_ref[
                        pl.ds(pl.multiple_of(place * UNIT_ROWS, UNIT_ROWS), UNIT_ROWS), :
                    ].astype(jnp.bfloat16)


def make_legs(matrices, sink_counts, weights, workers):
    extent = matrices.shape[2]
    a_per = extent // workers
    smem = pl.BlockSpec(memory_space=pltpu.SMEM)
    vmem = pl.BlockSpec(memory_space=pltpu.VMEM)
    return pl.pallas_call(
        functools.partial(legs_kernel, workers),
        in_specs=[smem, smem, vmem],
        out_specs=[vmem] * 3,
        out_shape=[
            jax.ShapeDtypeStruct((extent, MOST * extent), jnp.bfloat16),
            jax.ShapeDtypeStruct((MOST * extent, extent), jnp.bfloat16),
            jax.ShapeDtypeStruct(
                (extent // UNIT_ROWS, MOST * UNIT_ROWS, extent), jnp.bfloat16
            ),
        ],
        scratch_shapes=[
            pltpu.VMEM((matrices.shape[0] * matrices.shape[1], extent), jnp.float32),
            pltpu.VMEM((extent, extent), jnp.float32),
        ],
        compiler_params=pltpu.CompilerParams(vmem_limit_bytes=SMALL_VMEM),
    )(sink_counts, weights, matrices)


def group_kernel(first, last, units, per_unit, extent, *refs):
    pieces = len(units) * per_unit
    piece_refs = refs[:pieces]
    leg3_ref, leg2_ref, leg1_ref = refs[pieces : pieces + 3]
    refs = refs[pieces + 3 :]
    if not first:
        acc_ref, refs = refs[0], refs[1:]
    out_ref, turned_ref, outer_ref, across_ref, held_ref, sems = refs[:6]
    a_per = piece_refs[0].shape[0] // extent
    unit_depth = MOST * UNIT_ROWS
    depth = unit_depth * len(units)
    pitch = depth + 8
    step = pl.program_id(0)

    def fetch(piece):
        return pltpu.make_async_copy(piece_refs[piece], held_ref.at[piece], sems.at[piece])

    @pl.when(step == 0)
    def fetch_all():
        for piece in range(pieces):
            if not first:
                fetch(piece).start()

    def inner_legs(piece):
        place, lane = piece // per_unit, piece % per_unit
        if not first:
            fetch(piece).wait()
        rows_ref = piece_refs[piece] if first else held_ref.at[piece]
        sender = (lax.axis_index("work") & (per_unit - 1)) ^ lane
        third = jnp.dot(
            rows_ref[...], leg3_ref[...], preferred_element_type=jnp.float32
        ).astype(jnp.bfloat16)
        for d in range(MOST):
            columns = third[:, d * extent : (d + 1) * extent]
            wide = jnp.concatenate(
                [columns[a * extent : (a + 1) * extent] for a in range(a_per)], axis=1
            )
            second = jnp.dot(
                leg2_ref[d * extent : (d + 1) * extent, :],
                wide,
                preferred_element_type=jnp.float32,
            )
            for a in range(a_per):
                row = place * unit_depth + d * UNIT_ROWS + sender * a_per + a
                turned_ref[pl.ds(row, extent, stride=pitch), :] = second[
                    :, a * extent : (a + 1) * extent
                ]

    @pl.when(step == 0)
    def turn_outer():
        for place, unit in enumerate(units):
            outer_ref[place * unit_depth : (place + 1) * unit_depth, :] = leg1_ref[
                unit
            ].astype(jnp.float32)
        across_ref[...] = outer_ref[...].T.astype(jnp.bfloat16)

    for piece in range(pieces):
        pl.when(step == piece)(functools.partial(inner_legs, piece))

    @pl.when(step >= pieces)
    def outer_leg():
        begin = (step - pieces) * B_BLOCK
        wide = jnp.concatenate(
            [
                turned_ref[pl.ds(pl.multiple_of((begin + b) * pitch, 8), depth), :].astype(
                    jnp.bfloat16
                )
                for b in range(B_BLOCK)
            ],
            axis=1,
        )
        whole = jnp.dot(across_ref[...], wide, preferred_element_type=jnp.float32)
        for b in range(B_BLOCK):
            part = whole[:, b * extent : (b + 1) * extent]
            if not first:
                part = part + acc_ref[b].astype(jnp.float32)
            if last:
                refs[6][pl.ds(b, extent, stride=B_BLOCK + 8), :] = part
            else:
                out_ref[b] = part.astype(out_ref.dtype)
        if last:
            for a in range(extent):
                out_ref[a] = refs[6][pl.ds(a * (B_BLOCK + 8), B_BLOCK), :].astype(jnp.bfloat16)


def add_group(units, pieces, leg3, leg2, leg1, acc, last):
    extent = leg3.shape[0]
    count = len(pieces)
    per_unit = count // len(units)
    depth = MOST * UNIT_ROWS * len(units)
    first = acc is None
    blocks = extent // B_BLOCK

    def whole_spec(x):
        return pl.BlockSpec(x.shape, lambda i: (0,) * x.ndim)

    def block_of(i):
        return jnp.maximum(i - count, 0)

    operands = [*pieces, leg3, leg2, leg1]
    in_specs = [whole_spec(x) for x in operands]
    if not first:
        in_specs[:count] = [pl.BlockSpec(memory_space=pl.ANY)] * count
    if not first:
        operands.append(acc)
        in_specs.append(pl.BlockSpec((B_BLOCK, extent, extent), lambda i: (block_of(i), 0, 0)))
    scratch = [
        pltpu.VMEM((extent * (depth + 8), extent), jnp.float32),
        pltpu.VMEM((depth, extent), jnp.float32),
        pltpu.VMEM((extent, depth), jnp.bfloat16),
        pltpu.VMEM((count, *pieces[0].shape), jnp.bfloat16),
        pltpu.SemaphoreType.DMA((count,)),
    ]
    if last:
        out_shape = jax.ShapeDtypeStruct((extent, extent, extent), jnp.bfloat16)
        out_spec = pl.BlockSpec((extent, B_BLOCK, extent), lambda i: (0, block_of(i), 0))
        scratch.append(pltpu.VMEM((extent * (B_BLOCK + 8), extent), jnp.float32))
    else:
        out_shape = jax.ShapeDtypeStruct((extent, extent, extent), ACC)
        out_spec = pl.BlockSpec((B_BLOCK, extent, extent), lambda i: (block_of(i), 0, 0))
    rows = count * pieces[0].shape[0]
    return pl.pallas_call(
        functools.partial(group_kernel, first, last, units, per_unit, extent),
        grid=(count + blocks,),
        in_specs=in_specs,
        out_specs=out_spec,
        out_shape=out_shape,
        scratch_shapes=scratch,
        compiler_params=pltpu.CompilerParams(
            dimension_semantics=("arbitrary",), vmem_limit_bytes=ROOM + 4 * extent * extent * (depth + 8)
        ),
        cost_estimate=pl.CostEstimate(
            flops=6 * MOST * rows * extent * extent,
            bytes_accessed=12 * extent**3,
            transcendentals=0,
        ),
    )(*operands)


def per_device(sources, perambs, source_ids, peramb_ids, sink_counts, weights):
    workers = lax.axis_size("work")
    extent = sources.shape[2]
    per_unit = UNIT_ROWS * workers // extent
    half = workers // 2
    far = list(range(half, workers))
    near = [s for pair in zip(range(half // 2), range(half // 2, half)) for s in pair][1:]
    near = [1, *(s for s in near if s != 1)]
    order = []
    while far or near:
        take_far = far and (not near or len(order) % IN_FLIGHT in FAR_TURNS)
        order.append(far.pop(0) if take_far else near.pop(0))
    early, late = tuple(order[:IN_FLIGHT]), (0, *order[IN_FLIGHT:])
    pieces = dict(zip(early, choose_pieces(sources, source_ids, early)))
    pieces.update(zip(late, choose_pieces(sources, source_ids, late)))
    arrived = {0: pieces[0]}

    def send(place):
        shift = order[place]
        piece = pieces[shift]
        if place >= IN_FLIGHT:
            before = order[place - IN_FLIGHT]
            piece, arrived[before] = lax.optimization_barrier((piece, arrived[before]))
        arrived[shift] = lax.ppermute(piece, "work", [(i, i ^ shift) for i in range(workers)])

    for place in range(IN_FLIGHT):
        send(place)
    matrices = choose_matrices(perambs, peramb_ids, sink_counts, workers, extent)
    matrices = lax.all_to_all(matrices, "work", split_axis=0, concat_axis=0, tiled=True)
    leg3, leg2, leg1 = make_legs(matrices, sink_counts, weights, workers)
    for place in range(IN_FLIGHT, len(order) - 1):
        send(place)

    acc = None
    for group, units in enumerate(GROUPS):
        members = [arrived[u * per_unit + lane] for u in units for lane in range(per_unit)]
        acc = add_group(units, members, leg3, leg2, leg1, acc, group == len(GROUPS) - 1)
        if group == 0:
            pieces[order[-1]], acc = lax.optimization_barrier((pieces[order[-1]], acc))
            send(len(order) - 1)
    return acc.reshape(1, extent * extent, extent)


def solution(mesh):
    return jax.shard_map(
        per_device,
        mesh=mesh,
        in_specs=(P("cfg", "work", None), P("cfg", "work"), P(), P(), P(), P()),
        out_specs=P(("cfg", "work"), None, None),
        check_vma=False,
    )
```

```python
import functools

import jax
import jax.numpy as jnp
from jax import lax
from jax.experimental import pallas as pl
from jax.experimental.pallas import tpu as pltpu
from jax.sharding import PartitionSpec as P

MOST = 6
LEGS = 3
UNIT_ROWS = 16
B_BLOCK = 64
ACC = jnp.bfloat16
GROUPS = ((0, 2, 4), (1, 3, 5), (6,), (7,))
IN_FLIGHT = 5
FAR_TURNS = (2, 4)
SMALL_VMEM = 16 * 1024 * 1024
ROOM = 13 * 1024 * 1024


def pieces_kernel(shifts, ids_ref, source_ref, *refs):
    piece_refs, (held_ref, in_sems, out_sems) = refs[: len(shifts)], refs[len(shifts) :]
    own = lax.axis_index("work")
    reads, writes = [], []
    for i, shift in enumerate(shifts):
        reads.append(
            pltpu.make_async_copy(
                source_ref.at[ids_ref[own ^ shift]], held_ref.at[i], in_sems.at[i]
            )
        )
        writes.append(pltpu.make_async_copy(held_ref.at[i], piece_refs[i], out_sems.at[i]))
        reads[i].start()
    for read, write in zip(reads, writes):
        read.wait()
        write.start()
    for write in writes:
        write.wait()


def choose_pieces(sources, source_ids, shifts):
    return pl.pallas_call(
        functools.partial(pieces_kernel, shifts),
        in_specs=[pl.BlockSpec(memory_space=pltpu.SMEM), pl.BlockSpec(memory_space=pl.ANY)],
        out_specs=[pl.BlockSpec(memory_space=pl.ANY)] * len(shifts),
        out_shape=[jax.ShapeDtypeStruct(sources.shape[1:], sources.dtype)] * len(shifts),
        scratch_shapes=[
            pltpu.VMEM((len(shifts), *sources.shape[1:]), sources.dtype),
            pltpu.SemaphoreType.DMA((len(shifts),)),
            pltpu.SemaphoreType.DMA((len(shifts),)),
        ],
        compiler_params=pltpu.CompilerParams(vmem_limit_bytes=SMALL_VMEM),
    )(source_ids, sources)


def matrices_kernel(workers, counts_ref, matrix_ids_ref, peramb_ref, matrix_ref, choice_ref, spread_ref):
    rows = MOST * LEGS
    diagrams = matrix_ids_ref.shape[1]
    total = peramb_ref.shape[0]
    lanes = lax.broadcasted_iota(jnp.int32, (1, total), 1)

    def mark(sink, start):
        for slot in range(MOST):
            diagram = jnp.minimum(start + slot, diagrams - 1)
            for leg in range(LEGS):
                choice_ref[pl.ds(sink * rows + slot * LEGS + leg, 1), :] = jnp.where(
                    lanes == matrix_ids_ref[leg, diagram], 1.0, 0.0
                )
        return start + counts_ref[sink]

    lax.fori_loop(0, workers, mark, 0)
    chosen = jnp.dot(
        choice_ref[...].astype(jnp.bfloat16), peramb_ref[...], preferred_element_type=jnp.float32
    )
    extent = matrix_ref.shape[2]
    a_per = peramb_ref.shape[1] // extent
    for row in range(a_per):
        spread_ref[pl.ds(row, workers * rows, stride=a_per), :] = chosen[
            :, row * extent : (row + 1) * extent
        ]
    matrix_ref[...] = spread_ref[...].reshape(matrix_ref.shape).astype(jnp.bfloat16)


def choose_matrices(perambs, peramb_ids, sink_counts, workers, extent):
    rows = MOST * LEGS
    a_per = perambs.shape[1] // extent
    smem = pl.BlockSpec(memory_space=pltpu.SMEM)
    vmem = pl.BlockSpec(memory_space=pltpu.VMEM)
    return pl.pallas_call(
        functools.partial(matrices_kernel, workers),
        in_specs=[smem, smem, vmem],
        out_specs=vmem,
        out_shape=jax.ShapeDtypeStruct((workers, rows * a_per, extent), jnp.bfloat16),
        scratch_shapes=[
            pltpu.VMEM((workers * rows, perambs.shape[0]), jnp.float32),
            pltpu.VMEM((workers * rows * a_per, extent), jnp.float32),
        ],
        compiler_params=pltpu.CompilerParams(vmem_limit_bytes=SMALL_VMEM),
    )(sink_counts, peramb_ids.T, perambs)


def legs_kernel(
    workers, counts_ref, weights_ref, matrix_ref, leg3_ref, leg2_ref, leg1_ref, flat_ref, leg_ref
):
    extent = matrix_ref.shape[2]
    rows = MOST * LEGS
    a_per = matrix_ref.shape[1] // rows
    flat_ref[...] = matrix_ref[...].astype(jnp.float32).reshape(flat_ref.shape)
    own = lax.axis_index("work")
    start = lax.fori_loop(0, own, lambda i, total: total + counts_ref[i], 0)
    count = counts_ref[own]
    unit = UNIT_ROWS // a_per
    units = workers // unit
    for slot in range(MOST):
        for leg in range(LEGS):
            base = (slot * LEGS + leg) * a_per
            for row in range(a_per):
                leg_ref[pl.ds(row, workers, stride=a_per), :] = flat_ref[
                    pl.ds(base + row, workers, stride=rows * a_per), :
                ]
            if leg == 2:
                leg3_ref[:, slot * extent : (slot + 1) * extent] = leg_ref[...].T.astype(
                    jnp.bfloat16
                )
            elif leg == 1:
                leg2_ref[slot * extent : (slot + 1) * extent, :] = leg_ref[...].astype(
                    jnp.bfloat16
                )
            else:
                diagram = jnp.minimum(start + slot, weights_ref.shape[0] - 1)
                factor = jnp.where(slot < count, weights_ref[diagram], 0.0)
                leg_ref[...] = (factor * leg_ref[...]).T
                for block in range(units):
                    place = (own // unit) ^ block
                    leg1_ref[block, slot * UNIT_ROWS : (slot + 1) * UNIT_ROWS, :] = leg_ref[
                        pl.ds(pl.multiple_of(place * UNIT_ROWS, UNIT_ROWS), UNIT_ROWS), :
                    ].astype(jnp.bfloat16)


def make_legs(matrices, sink_counts, weights, workers):
    extent = matrices.shape[2]
    a_per = extent // workers
    smem = pl.BlockSpec(memory_space=pltpu.SMEM)
    vmem = pl.BlockSpec(memory_space=pltpu.VMEM)
    return pl.pallas_call(
        functools.partial(legs_kernel, workers),
        in_specs=[smem, smem, vmem],
        out_specs=[vmem] * 3,
        out_shape=[
            jax.ShapeDtypeStruct((extent, MOST * extent), jnp.bfloat16),
            jax.ShapeDtypeStruct((MOST * extent, extent), jnp.bfloat16),
            jax.ShapeDtypeStruct(
                (extent // UNIT_ROWS, MOST * UNIT_ROWS, extent), jnp.bfloat16
            ),
        ],
        scratch_shapes=[
            pltpu.VMEM((matrices.shape[0] * matrices.shape[1], extent), jnp.float32),
            pltpu.VMEM((extent, extent), jnp.float32),
        ],
        compiler_params=pltpu.CompilerParams(vmem_limit_bytes=SMALL_VMEM),
    )(sink_counts, weights, matrices)


def group_kernel(first, last, units, per_unit, extent, *refs):
    pieces = len(units) * per_unit
    piece_refs = refs[:pieces]
    leg3_ref, leg2_ref, leg1_ref = refs[pieces : pieces + 3]
    refs = refs[pieces + 3 :]
    if not first:
        acc_ref, refs = refs[0], refs[1:]
    out_ref, turned_ref, outer_ref, across_ref, held_ref, sems = refs[:6]
    a_per = piece_refs[0].shape[0] // extent
    unit_depth = MOST * UNIT_ROWS
    depth = unit_depth * len(units)
    pitch = depth + 8
    step = pl.program_id(0)

    def fetch(piece):
        return pltpu.make_async_copy(piece_refs[piece], held_ref.at[piece], sems.at[piece])

    @pl.when(step == 0)
    def fetch_all():
        for piece in range(pieces):
            if not first:
                fetch(piece).start()

    def inner_legs(piece):
        place, lane = piece // per_unit, piece % per_unit
        if not first:
            fetch(piece).wait()
        rows_ref = piece_refs[piece] if first else held_ref.at[piece]
        sender = (lax.axis_index("work") & (per_unit - 1)) ^ lane
        third = jnp.dot(
            rows_ref[...], leg3_ref[...], preferred_element_type=jnp.float32
        ).astype(jnp.bfloat16)
        for d in range(MOST):
            columns = third[:, d * extent : (d + 1) * extent]
            wide = jnp.concatenate(
                [columns[a * extent : (a + 1) * extent] for a in range(a_per)], axis=1
            )
            second = jnp.dot(
                leg2_ref[d * extent : (d + 1) * extent, :],
                wide,
                preferred_element_type=jnp.float32,
            )
            for a in range(a_per):
                row = place * unit_depth + d * UNIT_ROWS + sender * a_per + a
                turned_ref[pl.ds(row, extent, stride=pitch), :] = second[
                    :, a * extent : (a + 1) * extent
                ]

    @pl.when(step == 0)
    def turn_outer():
        for place, unit in enumerate(units):
            outer_ref[place * unit_depth : (place + 1) * unit_depth, :] = leg1_ref[
                unit
            ].astype(jnp.float32)
        across_ref[...] = outer_ref[...].T.astype(jnp.bfloat16)

    for piece in range(pieces):
        pl.when(step == piece)(functools.partial(inner_legs, piece))

    @pl.when(step >= pieces)
    def outer_leg():
        begin = (step - pieces) * B_BLOCK
        wide = jnp.concatenate(
            [
                turned_ref[pl.ds(pl.multiple_of((begin + b) * pitch, 8), depth), :].astype(
                    jnp.bfloat16
                )
                for b in range(B_BLOCK)
            ],
            axis=1,
        )
        whole = jnp.dot(across_ref[...], wide, preferred_element_type=jnp.float32)
        for b in range(B_BLOCK):
            part = whole[:, b * extent : (b + 1) * extent]
            if not first:
                part = part + acc_ref[b].astype(jnp.float32)
            if last:
                refs[6][pl.ds(b, extent, stride=B_BLOCK + 8), :] = part
            else:
                out_ref[b] = part.astype(out_ref.dtype)
        if last:
            for a in range(extent):
                out_ref[a] = refs[6][pl.ds(a * (B_BLOCK + 8), B_BLOCK), :].astype(jnp.bfloat16)


def add_group(units, pieces, leg3, leg2, leg1, acc, last):
    extent = leg3.shape[0]
    count = len(pieces)
    per_unit = count // len(units)
    depth = MOST * UNIT_ROWS * len(units)
    first = acc is None
    blocks = extent // B_BLOCK

    def whole_spec(x):
        return pl.BlockSpec(x.shape, lambda i: (0,) * x.ndim)

    def block_of(i):
        return jnp.maximum(i - count, 0)

    operands = [*pieces, leg3, leg2, leg1]
    in_specs = [whole_spec(x) for x in operands]
    if not first:
        in_specs[:count] = [pl.BlockSpec(memory_space=pl.ANY)] * count
    if not first:
        operands.append(acc)
        in_specs.append(pl.BlockSpec((B_BLOCK, extent, extent), lambda i: (block_of(i), 0, 0)))
    scratch = [
        pltpu.VMEM((extent * (depth + 8), extent), jnp.float32),
        pltpu.VMEM((depth, extent), jnp.float32),
        pltpu.VMEM((extent, depth), jnp.bfloat16),
        pltpu.VMEM((count, *pieces[0].shape), jnp.bfloat16),
        pltpu.SemaphoreType.DMA((count,)),
    ]
    if last:
        out_shape = jax.ShapeDtypeStruct((extent, extent, extent), jnp.bfloat16)
        out_spec = pl.BlockSpec((extent, B_BLOCK, extent), lambda i: (0, block_of(i), 0))
        scratch.append(pltpu.VMEM((extent * (B_BLOCK + 8), extent), jnp.float32))
    else:
        out_shape = jax.ShapeDtypeStruct((extent, extent, extent), ACC)
        out_spec = pl.BlockSpec((B_BLOCK, extent, extent), lambda i: (block_of(i), 0, 0))
    rows = count * pieces[0].shape[0]
    return pl.pallas_call(
        functools.partial(group_kernel, first, last, units, per_unit, extent),
        grid=(count + blocks,),
        in_specs=in_specs,
        out_specs=out_spec,
        out_shape=out_shape,
        scratch_shapes=scratch,
        compiler_params=pltpu.CompilerParams(
            dimension_semantics=("arbitrary",), vmem_limit_bytes=ROOM + 4 * extent * extent * (depth + 8)
        ),
        cost_estimate=pl.CostEstimate(
            flops=6 * MOST * rows * extent * extent,
            bytes_accessed=12 * extent**3,
            transcendentals=0,
        ),
    )(*operands)


def per_device(sources, perambs, source_ids, peramb_ids, sink_counts, weights):
    workers = lax.axis_size("work")
    extent = sources.shape[2]
    per_unit = UNIT_ROWS * workers // extent
    half = workers // 2
    far = list(range(half, workers))
    near = [s for pair in zip(range(half // 2), range(half // 2, half)) for s in pair][1:]
    near = [1, *(s for s in near if s != 1)]
    order = []
    while far or near:
        take_far = far and (not near or len(order) % IN_FLIGHT in FAR_TURNS)
        order.append(far.pop(0) if take_far else near.pop(0))
    early, late = tuple(order[:IN_FLIGHT]), (0, *order[IN_FLIGHT:])
    pieces = dict(zip(early, choose_pieces(sources, source_ids, early)))
    pieces.update(zip(late, choose_pieces(sources, source_ids, late)))
    arrived = {0: pieces[0]}

    def send(place):
        shift = order[place]
        piece = pieces[shift]
        if place >= IN_FLIGHT:
            before = order[place - IN_FLIGHT]
            piece, arrived[before] = lax.optimization_barrier((piece, arrived[before]))
        arrived[shift] = lax.ppermute(piece, "work", [(i, i ^ shift) for i in range(workers)])

    for place in range(IN_FLIGHT):
        send(place)
    matrices = choose_matrices(perambs, peramb_ids, sink_counts, workers, extent)
    matrices = lax.all_to_all(matrices, "work", split_axis=0, concat_axis=0, tiled=True)
    leg3, leg2, leg1 = make_legs(matrices, sink_counts, weights, workers)
    for place in range(IN_FLIGHT, len(order) - 1):
        if place == 2 * IN_FLIGHT:
            shift = order[place]
            pieces[shift], leg3 = lax.optimization_barrier((pieces[shift], leg3))
        send(place)

    acc = None
    for group, units in enumerate(GROUPS):
        members = [arrived[u * per_unit + lane] for u in units for lane in range(per_unit)]
        acc = add_group(units, members, leg3, leg2, leg1, acc, group == len(GROUPS) - 1)
        if group == 0:
            pieces[order[-1]], acc = lax.optimization_barrier((pieces[order[-1]], acc))
            send(len(order) - 1)
    return acc.reshape(1, extent * extent, extent)


def solution(mesh):
    return jax.shard_map(
        per_device,
        mesh=mesh,
        in_specs=(P("cfg", "work", None), P("cfg", "work"), P(), P(), P(), P()),
        out_specs=P(("cfg", "work"), None, None),
        check_vma=False,
    )
```

```python
import functools

import jax
import jax.numpy as jnp
from jax import lax
from jax.experimental import pallas as pl
from jax.experimental.pallas import tpu as pltpu
from jax.sharding import PartitionSpec as P

MOST = 6
LEGS = 3
UNIT_ROWS = 16
B_BLOCK = 64
ACC = jnp.bfloat16
GROUPS = ((0, 2), (1, 3, 4, 5), (6,), (7,))
IN_FLIGHT = 5
FAR_TURNS = (2, 4)
SMALL_VMEM = 16 * 1024 * 1024
ROOM = 13 * 1024 * 1024


def pieces_kernel(shifts, ids_ref, source_ref, *refs):
    piece_refs, (held_ref, in_sems, out_sems) = refs[: len(shifts)], refs[len(shifts) :]
    own = lax.axis_index("work")
    reads, writes = [], []
    for i, shift in enumerate(shifts):
        reads.append(
            pltpu.make_async_copy(
                source_ref.at[ids_ref[own ^ shift]], held_ref.at[i], in_sems.at[i]
            )
        )
        writes.append(pltpu.make_async_copy(held_ref.at[i], piece_refs[i], out_sems.at[i]))
        reads[i].start()
    for read, write in zip(reads, writes):
        read.wait()
        write.start()
    for write in writes:
        write.wait()


def choose_pieces(sources, source_ids, shifts):
    return pl.pallas_call(
        functools.partial(pieces_kernel, shifts),
        in_specs=[pl.BlockSpec(memory_space=pltpu.SMEM), pl.BlockSpec(memory_space=pl.ANY)],
        out_specs=[pl.BlockSpec(memory_space=pl.ANY)] * len(shifts),
        out_shape=[jax.ShapeDtypeStruct(sources.shape[1:], sources.dtype)] * len(shifts),
        scratch_shapes=[
            pltpu.VMEM((len(shifts), *sources.shape[1:]), sources.dtype),
            pltpu.SemaphoreType.DMA((len(shifts),)),
            pltpu.SemaphoreType.DMA((len(shifts),)),
        ],
        compiler_params=pltpu.CompilerParams(vmem_limit_bytes=SMALL_VMEM),
    )(source_ids, sources)


def matrices_kernel(workers, counts_ref, matrix_ids_ref, peramb_ref, matrix_ref, choice_ref, spread_ref):
    rows = MOST * LEGS
    diagrams = matrix_ids_ref.shape[1]
    total = peramb_ref.shape[0]
    lanes = lax.broadcasted_iota(jnp.int32, (1, total), 1)

    def mark(sink, start):
        for slot in range(MOST):
            diagram = jnp.minimum(start + slot, diagrams - 1)
            for leg in range(LEGS):
                choice_ref[pl.ds(sink * rows + slot * LEGS + leg, 1), :] = jnp.where(
                    lanes == matrix_ids_ref[leg, diagram], 1.0, 0.0
                )
        return start + counts_ref[sink]

    lax.fori_loop(0, workers, mark, 0)
    chosen = jnp.dot(
        choice_ref[...].astype(jnp.bfloat16), peramb_ref[...], preferred_element_type=jnp.float32
    )
    extent = matrix_ref.shape[2]
    a_per = peramb_ref.shape[1] // extent
    for row in range(a_per):
        spread_ref[pl.ds(row, workers * rows, stride=a_per), :] = chosen[
            :, row * extent : (row + 1) * extent
        ]
    matrix_ref[...] = spread_ref[...].reshape(matrix_ref.shape).astype(jnp.bfloat16)


def choose_matrices(perambs, peramb_ids, sink_counts, workers, extent):
    rows = MOST * LEGS
    a_per = perambs.shape[1] // extent
    smem = pl.BlockSpec(memory_space=pltpu.SMEM)
    vmem = pl.BlockSpec(memory_space=pltpu.VMEM)
    return pl.pallas_call(
        functools.partial(matrices_kernel, workers),
        in_specs=[smem, smem, vmem],
        out_specs=vmem,
        out_shape=jax.ShapeDtypeStruct((workers, rows * a_per, extent), jnp.bfloat16),
        scratch_shapes=[
            pltpu.VMEM((workers * rows, perambs.shape[0]), jnp.float32),
            pltpu.VMEM((workers * rows * a_per, extent), jnp.float32),
        ],
        compiler_params=pltpu.CompilerParams(vmem_limit_bytes=SMALL_VMEM),
    )(sink_counts, peramb_ids.T, perambs)


def legs_kernel(
    workers, counts_ref, weights_ref, matrix_ref, leg3_ref, leg2_ref, leg1_ref, flat_ref, leg_ref
):
    extent = matrix_ref.shape[2]
    rows = MOST * LEGS
    a_per = matrix_ref.shape[1] // rows
    flat_ref[...] = matrix_ref[...].astype(jnp.float32).reshape(flat_ref.shape)
    own = lax.axis_index("work")
    start = lax.fori_loop(0, own, lambda i, total: total + counts_ref[i], 0)
    count = counts_ref[own]
    unit = UNIT_ROWS // a_per
    units = workers // unit
    for slot in range(MOST):
        for leg in range(LEGS):
            base = (slot * LEGS + leg) * a_per
            for row in range(a_per):
                leg_ref[pl.ds(row, workers, stride=a_per), :] = flat_ref[
                    pl.ds(base + row, workers, stride=rows * a_per), :
                ]
            if leg == 2:
                leg3_ref[:, slot * extent : (slot + 1) * extent] = leg_ref[...].T.astype(
                    jnp.bfloat16
                )
            elif leg == 1:
                leg2_ref[slot * extent : (slot + 1) * extent, :] = leg_ref[...].astype(
                    jnp.bfloat16
                )
            else:
                diagram = jnp.minimum(start + slot, weights_ref.shape[0] - 1)
                factor = jnp.where(slot < count, weights_ref[diagram], 0.0)
                leg_ref[...] = (factor * leg_ref[...]).T
                for block in range(units):
                    place = (own // unit) ^ block
                    leg1_ref[block, slot * UNIT_ROWS : (slot + 1) * UNIT_ROWS, :] = leg_ref[
                        pl.ds(pl.multiple_of(place * UNIT_ROWS, UNIT_ROWS), UNIT_ROWS), :
                    ].astype(jnp.bfloat16)


def make_legs(matrices, sink_counts, weights, workers):
    extent = matrices.shape[2]
    a_per = extent // workers
    smem = pl.BlockSpec(memory_space=pltpu.SMEM)
    vmem = pl.BlockSpec(memory_space=pltpu.VMEM)
    return pl.pallas_call(
        functools.partial(legs_kernel, workers),
        in_specs=[smem, smem, vmem],
        out_specs=[vmem] * 3,
        out_shape=[
            jax.ShapeDtypeStruct((extent, MOST * extent), jnp.bfloat16),
            jax.ShapeDtypeStruct((MOST * extent, extent), jnp.bfloat16),
            jax.ShapeDtypeStruct(
                (extent // UNIT_ROWS, MOST * UNIT_ROWS, extent), jnp.bfloat16
            ),
        ],
        scratch_shapes=[
            pltpu.VMEM((matrices.shape[0] * matrices.shape[1], extent), jnp.float32),
            pltpu.VMEM((extent, extent), jnp.float32),
        ],
        compiler_params=pltpu.CompilerParams(vmem_limit_bytes=SMALL_VMEM),
    )(sink_counts, weights, matrices)


def group_kernel(first, last, units, per_unit, extent, *refs):
    pieces = len(units) * per_unit
    piece_refs = refs[:pieces]
    leg3_ref, leg2_ref, leg1_ref = refs[pieces : pieces + 3]
    refs = refs[pieces + 3 :]
    if not first:
        acc_ref, refs = refs[0], refs[1:]
    out_ref, turned_ref, outer_ref, across_ref, held_ref, sems = refs[:6]
    a_per = piece_refs[0].shape[0] // extent
    unit_depth = MOST * UNIT_ROWS
    depth = unit_depth * len(units)
    pitch = depth + 8
    step = pl.program_id(0)

    def fetch(piece):
        return pltpu.make_async_copy(piece_refs[piece], held_ref.at[piece], sems.at[piece])

    @pl.when(step == 0)
    def fetch_all():
        for piece in range(pieces):
            if not first:
                fetch(piece).start()

    def inner_legs(piece):
        place, lane = piece // per_unit, piece % per_unit
        if not first:
            fetch(piece).wait()
        rows_ref = piece_refs[piece] if first else held_ref.at[piece]
        sender = (lax.axis_index("work") & (per_unit - 1)) ^ lane
        third = jnp.dot(
            rows_ref[...], leg3_ref[...], preferred_element_type=jnp.float32
        ).astype(jnp.bfloat16)
        for d in range(MOST):
            columns = third[:, d * extent : (d + 1) * extent]
            wide = jnp.concatenate(
                [columns[a * extent : (a + 1) * extent] for a in range(a_per)], axis=1
            )
            second = jnp.dot(
                leg2_ref[d * extent : (d + 1) * extent, :],
                wide,
                preferred_element_type=jnp.float32,
            )
            for a in range(a_per):
                row = place * unit_depth + d * UNIT_ROWS + sender * a_per + a
                turned_ref[pl.ds(row, extent, stride=pitch), :] = second[
                    :, a * extent : (a + 1) * extent
                ]

    @pl.when(step == 0)
    def turn_outer():
        for place, unit in enumerate(units):
            outer_ref[place * unit_depth : (place + 1) * unit_depth, :] = leg1_ref[
                unit
            ].astype(jnp.float32)
        across_ref[...] = outer_ref[...].T.astype(jnp.bfloat16)

    for piece in range(pieces):
        pl.when(step == piece)(functools.partial(inner_legs, piece))

    @pl.when(step >= pieces)
    def outer_leg():
        begin = (step - pieces) * B_BLOCK
        wide = jnp.concatenate(
            [
                turned_ref[pl.ds(pl.multiple_of((begin + b) * pitch, 8), depth), :].astype(
                    jnp.bfloat16
                )
                for b in range(B_BLOCK)
            ],
            axis=1,
        )
        whole = jnp.dot(across_ref[...], wide, preferred_element_type=jnp.float32)
        for b in range(B_BLOCK):
            part = whole[:, b * extent : (b + 1) * extent]
            if not first:
                part = part + acc_ref[b].astype(jnp.float32)
            if last:
                refs[6][pl.ds(b, extent, stride=B_BLOCK + 8), :] = part
            else:
                out_ref[b] = part.astype(out_ref.dtype)
        if last:
            for a in range(extent):
                out_ref[a] = refs[6][pl.ds(a * (B_BLOCK + 8), B_BLOCK), :].astype(jnp.bfloat16)


def add_group(units, pieces, leg3, leg2, leg1, acc, last):
    extent = leg3.shape[0]
    count = len(pieces)
    per_unit = count // len(units)
    depth = MOST * UNIT_ROWS * len(units)
    first = acc is None
    blocks = extent // B_BLOCK

    def whole_spec(x):
        return pl.BlockSpec(x.shape, lambda i: (0,) * x.ndim)

    def block_of(i):
        return jnp.maximum(i - count, 0)

    operands = [*pieces, leg3, leg2, leg1]
    in_specs = [whole_spec(x) for x in operands]
    if not first:
        in_specs[:count] = [pl.BlockSpec(memory_space=pl.ANY)] * count
    if not first:
        operands.append(acc)
        in_specs.append(pl.BlockSpec((B_BLOCK, extent, extent), lambda i: (block_of(i), 0, 0)))
    scratch = [
        pltpu.VMEM((extent * (depth + 8), extent), jnp.float32),
        pltpu.VMEM((depth, extent), jnp.float32),
        pltpu.VMEM((extent, depth), jnp.bfloat16),
        pltpu.VMEM((count, *pieces[0].shape), jnp.bfloat16),
        pltpu.SemaphoreType.DMA((count,)),
    ]
    if last:
        out_shape = jax.ShapeDtypeStruct((extent, extent, extent), jnp.bfloat16)
        out_spec = pl.BlockSpec((extent, B_BLOCK, extent), lambda i: (0, block_of(i), 0))
        scratch.append(pltpu.VMEM((extent * (B_BLOCK + 8), extent), jnp.float32))
    else:
        out_shape = jax.ShapeDtypeStruct((extent, extent, extent), ACC)
        out_spec = pl.BlockSpec((B_BLOCK, extent, extent), lambda i: (block_of(i), 0, 0))
    rows = count * pieces[0].shape[0]
    return pl.pallas_call(
        functools.partial(group_kernel, first, last, units, per_unit, extent),
        grid=(count + blocks,),
        in_specs=in_specs,
        out_specs=out_spec,
        out_shape=out_shape,
        scratch_shapes=scratch,
        compiler_params=pltpu.CompilerParams(
            dimension_semantics=("arbitrary",), vmem_limit_bytes=ROOM + 4 * extent * extent * (depth + 8)
        ),
        cost_estimate=pl.CostEstimate(
            flops=6 * MOST * rows * extent * extent,
            bytes_accessed=12 * extent**3,
            transcendentals=0,
        ),
    )(*operands)


def per_device(sources, perambs, source_ids, peramb_ids, sink_counts, weights):
    workers = lax.axis_size("work")
    extent = sources.shape[2]
    per_unit = UNIT_ROWS * workers // extent
    half = workers // 2
    far = list(range(half, workers))
    near = [s for pair in zip(range(half // 2), range(half // 2, half)) for s in pair][1:]
    near = [1, *(s for s in near if s != 1)]
    order = []
    while far or near:
        take_far = far and (not near or len(order) % IN_FLIGHT in FAR_TURNS)
        order.append(far.pop(0) if take_far else near.pop(0))
    early, late = tuple(order[:IN_FLIGHT]), (0, *order[IN_FLIGHT:])
    pieces = dict(zip(early, choose_pieces(sources, source_ids, early)))
    pieces.update(zip(late, choose_pieces(sources, source_ids, late)))
    arrived = {0: pieces[0]}

    def send(place):
        shift = order[place]
        piece = pieces[shift]
        if place >= IN_FLIGHT:
            before = order[place - IN_FLIGHT]
            piece, arrived[before] = lax.optimization_barrier((piece, arrived[before]))
        arrived[shift] = lax.ppermute(piece, "work", [(i, i ^ shift) for i in range(workers)])

    for place in range(IN_FLIGHT):
        send(place)
    matrices = choose_matrices(perambs, peramb_ids, sink_counts, workers, extent)
    matrices = lax.all_to_all(matrices, "work", split_axis=0, concat_axis=0, tiled=True)
    leg3, leg2, leg1 = make_legs(matrices, sink_counts, weights, workers)
    for place in range(IN_FLIGHT, len(order) - 1):
        send(place)

    acc = None
    for group, units in enumerate(GROUPS):
        members = [arrived[u * per_unit + lane] for u in units for lane in range(per_unit)]
        acc = add_group(units, members, leg3, leg2, leg1, acc, group == len(GROUPS) - 1)
        if group == 0:
            pieces[order[-1]], acc = lax.optimization_barrier((pieces[order[-1]], acc))
            send(len(order) - 1)
    return acc.reshape(1, extent * extent, extent)


def solution(mesh):
    return jax.shard_map(
        per_device,
        mesh=mesh,
        in_specs=(P("cfg", "work", None), P("cfg", "work"), P(), P(), P(), P()),
        out_specs=P(("cfg", "work"), None, None),
        check_vma=False,
    )
```
